32 devices in a mesh: dp: 8 (over z, core), space: 4 (over y, x).
Axes of the slice: x: 2, y: 2, z: 4, core: 2. Of those that a mesh axis runs over, the one named last changes fastest.
Arguments:
- volume: bfloat16 [8, 16, 32, 32, 128], P('dp', 'space'), may hold values from -6 to 6
- kernel: bfloat16 [3, 3, 3, 128, 256], replicated, may hold values from -0.109375 to 0.109375
- cotangent: bfloat16 [8, 8, 16, 16, 256], P('dp', 'space'), may hold values from -6 to 6
Outputs:
- switched: bfloat16 [8, 256, 2048], P('dp', 'space')
- volume_grad: bfloat16 [8, 16, 32, 32, 128], P('dp', 'space')
- kernel_grad: float32 [3, 3, 3, 128, 256], P(None, None, None, 'dp')
The draws below stay inside these ranges and needn't reach their ends.
All inputs are finite; a program needn't handle non-finite values.
Results may differ from the reference program's by a relative error of at most 0.0049.
Values may be sent and summed in bfloat16 or wider, within the bound.
No kernel may reach another device: no remote copies, remote signals or barrier semaphores. Data moves between devices by JAX's collectives and lax.ppermute only.
A program may use at most 64 MiB of HBM per device.

```python
import math
import jax
import jax.numpy as jnp
from jax import lax

CIN = 128
COUT = 256
SIDE = 32
SAMPLES = 8
DEPTH = 16
D2 = 8
S2 = 16


def raised(drawn, rng, source, target, parts, factor):
    def block_of(position):
        return (jnp.arange(drawn.shape[position]) // (drawn.shape[position] // parts)).reshape((-1,) + (1,) * (drawn.ndim - 1 - position))

    near = jax.random.permutation(rng, parts)[block_of(target)]
    other_side = (block_of(target) + parts // 2) % parts
    return jnp.where((block_of(source) == near) | (block_of(source) == other_side), factor * drawn, drawn)


def steps_of(stream_key, shape, pieces, low, largest):
    def one(position, parts):
        steps = jax.random.uniform(jax.random.fold_in(jax.random.fold_in(stream_key, 6), position), (parts,), jnp.float32, low / len(pieces), largest / len(pieces))
        return jnp.repeat(jnp.exp(steps), shape[position] // parts).reshape((-1,) + (1,) * (len(shape) - position - 1))

    level = one(*pieces[0])
    for cut in pieces[1:]:
        level = level * one(*cut)
    return level


def noise(stream_key, dims, spread, reach, pieces=(), kind=jnp.bfloat16):
    gain = steps_of(stream_key, dims, pieces, -0.22, 0.18) if pieces else 1.0
    array = jax.random.normal(stream_key, dims, jnp.float32) * spread * gain
    return jnp.minimum(jnp.maximum(array, -reach), reach).astype(kind)


def bell_draw_with(key, extent, spread, bound, cuts, heavy, dtype=jnp.bfloat16):
    drawn = spread * jax.random.normal(key, extent, jnp.float32)
    if cuts:
        drawn = drawn * steps_of(key, extent, cuts, -0.22, 0.18)
    return jnp.clip(raised(drawn, jax.random.fold_in(key, 3), *heavy), -bound, bound).astype(dtype)


def setup_inputs(seed: int = 0) -> dict:
    key_list = jax.random.split(jax.random.key(seed), 4)
    return {
        "volume": bell_draw_with(key_list[0], (SAMPLES, DEPTH, SIDE, SIDE, CIN), 1.0, 6.0, ((0, 8), (1, 4)), (0, 4, 8, 2.0)),
        "kernel": noise(key_list[1], (3, 3, 3, CIN, COUT), (27 * CIN) ** -0.5, 0.109375),
        "cotangent": noise(key_list[2], (SAMPLES, D2, S2, S2, COUT), 1.0, 6.0, ((0, 8), (1, 4))),
    }


def forward_conv(volume_one, kernel):
    return lax.conv_general_dilated(volume_one, kernel, (2, 2, 2), ((1, 1), (1, 1), (1, 1)), dimension_numbers=('NDHWC', 'DHWIO', 'NDHWC'), preferred_element_type=jnp.float32)

def one_sample(volume_one, kernel, cotangent_one):
    preact = forward_conv(volume_one, kernel)
    sigmoid_z = jax.nn.sigmoid(preact)
    activated = (preact * sigmoid_z).astype(jnp.bfloat16)
    slope = sigmoid_z * (1.0 + preact * (1.0 - sigmoid_z))
    grad_pre = (cotangent_one.astype(jnp.float32) * slope).astype(jnp.bfloat16)
    flipped = kernel[::-1, ::-1, ::-1]
    data_grad = lax.conv_general_dilated(grad_pre, flipped, (1, 1, 1), ((1, 2), (1, 2), (1, 2)), lhs_dilation=(2, 2, 2), dimension_numbers=('NDHWC', 'DHWOI', 'NDHWC'), preferred_element_type=jnp.float32).astype(jnp.bfloat16)
    kernel_part = lax.conv_general_dilated(volume_one, grad_pre, (1, 1, 1), ((1, 0), (1, 0), (1, 0)), rhs_dilation=(2, 2, 2), dimension_numbers=('CDHWN', 'IDHWO', 'DHWNC'), preferred_element_type=jnp.float32)
    return (activated, data_grad, kernel_part)

def reference(volume, kernel, cotangent):

    def step(total, pair):
        activated, data_grad, kernel_part = one_sample(pair[0][None], kernel, pair[1][None])
        return (total + kernel_part, (activated[0], data_grad[0]))
    start = jnp.zeros((3, 3, 3, volume.shape[4], kernel.shape[4]), jnp.float32)
    total, outs = lax.scan(step, start, (volume, cotangent))
    activated, volume_grad = outs
    samples, planes, rows, cols, chans = activated.shape
    switched = jnp.transpose(activated, (0, 4, 1, 2, 3)).reshape(samples, chans, planes * rows * cols)
    scale = 1.0 / math.sqrt(samples * planes * rows * cols)
    return (switched, volume_grad, total * scale)
```

```python
import math

import jax
import jax.numpy as jnp
from jax import lax
from jax.sharding import PartitionSpec as P

BF16 = jnp.bfloat16
F32 = jnp.float32


def from_behind(value, axis, steps):
    count = lax.axis_size(axis)
    first, last = (max(0, -steps), min(count, count - steps))
    return lax.ppermute(value, axis, [(source, source + steps) for source in range(first, last)])


def reduce_kernel_grad(part):
    taps, chans_in, chans_out = part.shape
    dp, space = lax.axis_size("dp"), lax.axis_size("space")
    cores = 2 if dp % 2 == 0 else 1
    chips = dp // cores
    padded = -(-taps // space) * space
    block = chans_in // dp
    share = padded // space
    part = jnp.pad(part, ((0, padded - taps), (0, 0), (0, 0)))
    pieces = part.reshape(space, share, chips, cores, block, chans_out)
    pieces = pieces.transpose(3, 0, 2, 1, 4, 5)
    if cores == 2:
        core = lax.axis_index("dp") % 2
        mine = lax.dynamic_index_in_dim(pieces, core, 0, keepdims=False)
        other = lax.dynamic_index_in_dim(pieces, 1 - core, 0, keepdims=False).astype(BF16)
        got = lax.ppermute(other, "dp", [(i, i ^ 1) for i in range(dp)])
        total = mine + got.astype(F32)
    else:
        total = pieces[0]
    rows = share * block
    total = total.reshape(space, chips * rows, chans_out).astype(BF16)
    got = lax.all_to_all(total, "space", 0, 0, tiled=True)
    total = jnp.sum(got.astype(F32), axis=0).astype(BF16)
    if chips > 1:
        groups = [[chip * cores + core for chip in range(chips)] for core in range(cores)]
        got = lax.all_to_all(
            total.reshape(chips, rows, chans_out), "dp", 0, 0, axis_index_groups=groups, tiled=True
        )
        total = jnp.sum(got.astype(F32), axis=0).astype(BF16)
    spread = jnp.broadcast_to(total.reshape(1, rows, chans_out), (space, rows, chans_out))
    full = lax.all_to_all(spread, "space", 0, 0, tiled=True)
    return full.reshape(padded, block, chans_out)[:taps].astype(F32)


def body(volume, kernel, cotangent):
    below = from_behind(volume[:, -1:], "space", 1)
    extended = jnp.concatenate([below, volume], axis=1)
    preact = lax.conv_general_dilated(
        extended,
        kernel,
        (2, 2, 2),
        ((0, 0), (1, 1), (1, 1)),
        dimension_numbers=("NDHWC", "DHWIO", "NDHWC"),
        preferred_element_type=jnp.float32,
    )
    sigmoid_z = jax.nn.sigmoid(preact)
    activated = (preact * sigmoid_z).astype(jnp.bfloat16)
    slope = sigmoid_z * (1.0 + preact * (1.0 - sigmoid_z))
    grad_pre = (cotangent.astype(jnp.float32) * slope).astype(jnp.bfloat16)
    samples, planes, rows, cols, chans = activated.shape
    channel_major = jnp.transpose(activated, (0, 4, 1, 2, 3)).reshape(
        samples, chans, planes * rows * cols
    )
    switched = lax.all_to_all(channel_major, "space", split_axis=1, concat_axis=2, tiled=True)
    flipped = kernel[::-1, ::-1, ::-1]
    above = from_behind(grad_pre[:, :1], "space", -1)
    grad_ext = jnp.concatenate([grad_pre, above], axis=1)
    data_grad = lax.conv_general_dilated(
        grad_ext,
        flipped,
        (1, 1, 1),
        ((1, 0), (1, 2), (1, 2)),
        lhs_dilation=(2, 2, 2),
        dimension_numbers=("NDHWC", "DHWOI", "NDHWC"),
        preferred_element_type=jnp.float32,
    )
    volume_grad = data_grad.astype(jnp.bfloat16)
    kernel_part = lax.conv_general_dilated(
        extended,
        grad_pre,
        (1, 1, 1),
        ((0, 0), (1, 0), (1, 0)),
        rhs_dilation=(2, 2, 2),
        dimension_numbers=("CDHWN", "IDHWO", "DHWNC"),
        preferred_element_type=jnp.float32,
    )
    count = lax.axis_size("dp") * lax.axis_size("space") * planes * rows * cols
    kernel_part = kernel_part * (1.0 / math.sqrt(count))
    kd, kh, kw, ci, co = kernel_part.shape
    kernel_grad = reduce_kernel_grad(kernel_part.reshape(kd * kh * kw, ci, co))
    return (switched, volume_grad, kernel_grad.reshape(kd, kh, kw, -1, co))


def solution(mesh):
    in_specs = (P("dp", "space", None, None, None), P(), P("dp", "space", None, None, None))
    out_specs = (
        P("dp", "space", None),
        P("dp", "space", None, None, None),
        P(None, None, None, "dp", None),
    )
    return jax.shard_map(body, mesh=mesh, in_specs=in_specs, out_specs=out_specs, check_vma=False)
```

```python
import math

import jax
import jax.numpy as jnp
from jax import lax
from jax.sharding import PartitionSpec as P

BF16 = jnp.bfloat16
F32 = jnp.float32


def from_behind(value, axis, steps):
    count = lax.axis_size(axis)
    first, last = (max(0, -steps), min(count, count - steps))
    return lax.ppermute(value, axis, [(source, source + steps) for source in range(first, last)])


def chip_groups():
    dp = lax.axis_size("dp")
    cores = 2 if dp % 2 == 0 else 1
    return cores, dp // cores, [list(range(core, dp, cores)) for core in range(cores)]


def add_cores(part):
    units, chans_in, lanes = part.shape
    cores, chips, _ = chip_groups()
    pieces = part.reshape(units, chips, cores, chans_in // (chips * cores), lanes)
    if cores == 1:
        return pieces[:, :, 0]
    core = lax.axis_index("dp") % 2
    mine = lax.dynamic_index_in_dim(pieces, core, 2, keepdims=False)
    other = lax.dynamic_index_in_dim(pieces, 1 - core, 2, keepdims=False).astype(BF16)
    got = lax.ppermute(other, "dp", [(i, i ^ 1) for i in range(cores * chips)])
    return mine + got.astype(F32)


def scatter_space(total):
    space = lax.axis_size("space")
    units, rows, lanes = total.shape
    share = -(-units // space)
    total = jnp.pad(total.astype(BF16), ((0, share * space - units), (0, 0), (0, 0)))
    got = lax.all_to_all(total.reshape(space, share * rows, lanes), "space", 0, 0, tiled=True)
    return jnp.sum(got.astype(F32), axis=0).reshape(share, rows, lanes)


def scatter_chips(total):
    units, chips, block, lanes = total.shape
    if chips == 1:
        return total[:, 0]
    _, _, groups = chip_groups()
    moved = jnp.swapaxes(total, 0, 1).astype(BF16).reshape(chips, units * block, lanes)
    got = lax.all_to_all(moved, "dp", 0, 0, axis_index_groups=groups, tiled=True)
    return jnp.sum(got.astype(F32), axis=0).reshape(units, block, lanes)


def reduce_kernel_grad(part, late):
    space = lax.axis_size("space")
    early = part.shape[0] - late
    first = add_cores(part[:early])
    second = add_cores(part[early:])
    units, chips, block, lanes = first.shape
    first = scatter_space(first.reshape(units, chips * block, lanes))
    second = scatter_chips(second)
    first = scatter_chips(first.reshape(-1, chips, block, lanes))
    second = scatter_space(second)
    both = jnp.concatenate([first, second], axis=0).astype(BF16)
    share = both.shape[0]
    spread = jnp.broadcast_to(both.reshape(1, share * block, lanes), (space, share * block, lanes))
    full = lax.all_to_all(spread, "space", 0, 0, tiled=True).reshape(space, share, block, lanes)
    cut = first.shape[0]
    early_full = full[:, :cut].reshape(-1, block, lanes)[:early]
    late_full = full[:, cut:].reshape(-1, block, lanes)[:late]
    return jnp.concatenate([early_full, late_full], axis=0).astype(F32)


def body(volume, kernel, cotangent):
    below = from_behind(volume[:, -1:], "space", 1)
    extended = jnp.concatenate([below, volume], axis=1)
    preact = lax.conv_general_dilated(
        extended,
        kernel,
        (2, 2, 2),
        ((0, 0), (1, 1), (1, 1)),
        dimension_numbers=("NDHWC", "DHWIO", "NDHWC"),
        preferred_element_type=jnp.float32,
    )
    sigmoid_z = jax.nn.sigmoid(preact)
    activated = (preact * sigmoid_z).astype(jnp.bfloat16)
    slope = sigmoid_z * (1.0 + preact * (1.0 - sigmoid_z))
    grad_pre = (cotangent.astype(jnp.float32) * slope).astype(jnp.bfloat16)
    samples, planes, rows, cols, chans = activated.shape
    channel_major = jnp.transpose(activated, (0, 4, 1, 2, 3)).reshape(
        samples, chans, planes * rows * cols
    )
    switched = lax.all_to_all(channel_major, "space", split_axis=1, concat_axis=2, tiled=True)
    flipped = kernel[::-1, ::-1, ::-1]
    above = from_behind(grad_pre[:, :1], "space", -1)
    grad_ext = jnp.concatenate([grad_pre, above], axis=1)
    data_grad = lax.conv_general_dilated(
        grad_ext,
        flipped,
        (1, 1, 1),
        ((1, 0), (1, 2), (1, 2)),
        lhs_dilation=(2, 2, 2),
        dimension_numbers=("NDHWC", "DHWOI", "NDHWC"),
        preferred_element_type=jnp.float32,
    )
    volume_grad = data_grad.astype(jnp.bfloat16)
    kernel_part = lax.conv_general_dilated(
        extended,
        grad_pre,
        (1, 1, 1),
        ((0, 0), (1, 0), (1, 0)),
        rhs_dilation=(2, 2, 2),
        dimension_numbers=("CDHWN", "IDHWO", "DHWNC"),
        preferred_element_type=jnp.float32,
    )
    count = lax.axis_size("dp") * lax.axis_size("space") * planes * rows * cols
    kernel_part = kernel_part * (1.0 / math.sqrt(count))
    kd, kh, kw, ci, co = kernel_part.shape
    lanes = 128 if co % 128 == 0 else co
    halves = co // lanes
    units = kernel_part.reshape(kd * kh * kw, ci, halves, lanes).swapaxes(1, 2)
    units = units.reshape(-1, ci, lanes)
    total = reduce_kernel_grad(units, kh * kw * halves)
    kernel_grad = total.reshape(kd * kh * kw, halves, -1, lanes).swapaxes(1, 2)
    return (switched, volume_grad, kernel_grad.reshape(kd, kh, kw, -1, co))


def solution(mesh):
    in_specs = (P("dp", "space", None, None, None), P(), P("dp", "space", None, None, None))
    out_specs = (
        P("dp", "space", None),
        P("dp", "space", None, None, None),
        P(None, None, None, "dp", None),
    )
    return jax.shard_map(body, mesh=mesh, in_specs=in_specs, out_specs=out_specs, check_vma=False)
```

```python
import functools
import math

import jax
import jax.numpy as jnp
from jax import lax
from jax.experimental import pallas as pl
from jax.experimental.pallas import tpu as pltpu
from jax.sharding import PartitionSpec as P

BF16 = jnp.bfloat16
F32 = jnp.float32
VMEM_LIMIT = 40 * 1024 * 1024


def params():
    return pltpu.CompilerParams(vmem_limit_bytes=VMEM_LIMIT)


def call(kernel, out_shape, scratch=(), flops=0, moved=0):
    return pl.pallas_call(
        kernel,
        out_shape=out_shape,
        scratch_shapes=list(scratch),
        compiler_params=params(),
        cost_estimate=pl.CostEstimate(flops=flops, bytes_accessed=moved, transcendentals=0),
    )


def spread_plane(plane, wide):
    height, width, chans = plane.shape
    cells = height * width
    half = width // 2
    wide[pl.ds(8, cells), :] = plane.reshape(cells, chans).astype(F32)
    left = wide[pl.ds(7, cells // 2, stride=2), :]
    even = wide[pl.ds(8, cells // 2, stride=2), :]
    odd = wide[pl.ds(9, cells // 2, stride=2), :]
    column = lax.broadcasted_iota(jnp.int32, left.shape, 0) % half
    left = jnp.where(column == 0, 0.0, left)
    joined = jnp.concatenate([left.astype(BF16), even.astype(BF16), odd.astype(BF16)], axis=1)
    joined = joined.reshape(height // 2, 2, half, 3 * chans)
    return joined[:, 0], joined[:, 1]


def tap_rows(even, odd, plane, kh):
    height = even.shape[1]
    picked = even[plane] if kh == 1 else odd[plane, pl.ds(0 if kh == 0 else 1, height)]
    return picked.reshape(height * even.shape[2], even.shape[3])


def halo_kernel(plane_ref, kernel_ref, share_ref, wide):
    _, _, height, width, chans = plane_ref.shape
    even, odd = spread_plane(plane_ref[0, 0], wide)
    above = jnp.concatenate([jnp.zeros_like(odd[:1]), odd[:-1]], axis=0)
    total = None
    for kh, rows in enumerate((above, even, odd)):
        lhs = rows.reshape(height * width // 4, 3 * chans)
        rhs = kernel_ref[0, kh].reshape(3 * chans, kernel_ref.shape[-1])
        term = jnp.dot(lhs, rhs, preferred_element_type=F32)
        total = term if total is None else total + term
    share_ref[...] = total.astype(BF16)


def halo_share(volume, kernel):
    _, planes, height, width, chans = volume.shape
    co = kernel.shape[-1]
    cells = height * width // 4
    return pl.pallas_call(
        halo_kernel,
        grid=(1,),
        out_shape=jax.ShapeDtypeStruct((cells, co), BF16),
        in_specs=[
            pl.BlockSpec((1, 1, height, width, chans), lambda i: (0, planes - 1, 0, 0, 0)),
            pl.BlockSpec((1, 3, 3, chans, co), lambda i: (0, 0, 0, 0, 0)),
        ],
        out_specs=pl.BlockSpec((cells, co), lambda i: (0, 0)),
        scratch_shapes=[pltpu.VMEM((height * width + 16, chans), F32)],
        compiler_params=params(),
        cost_estimate=pl.CostEstimate(
            flops=2 * cells * 9 * chans * co, bytes_accessed=2**20, transcendentals=0
        ),
    )(volume, kernel)


def preact_kernel(volume_ref, kernel_ref, preact_ref, even_ref, odd_ref, wide):
    _, planes, height, width, chans = volume_ref.shape
    cells = height * width // 4
    outs = planes // 2
    for plane in range(planes):
        even, odd = spread_plane(volume_ref[0, plane], wide)
        even_ref[plane] = even
        odd_ref[plane, pl.ds(0, 1)] = jnp.zeros_like(odd[:1])
        odd_ref[plane, pl.ds(1, height // 2)] = odd
    co = kernel_ref.shape[-1]
    total = None
    for kd in (1, 2):
        for kh in range(3):
            lhs = [tap_rows(even_ref, odd_ref, 2 * d - 1 + kd, kh) for d in range(outs)]
            rhs = kernel_ref[kd, kh].reshape(3 * chans, co)
            term = jnp.dot(jnp.concatenate(lhs, axis=0), rhs, preferred_element_type=F32)
            total = term if total is None else total + term
    preact_ref[...] = total
    if outs > 1:
        total = preact_ref[pl.ds(cells, (outs - 1) * cells), :]
        for kh in range(3):
            lhs = [tap_rows(even_ref, odd_ref, 2 * d - 1, kh) for d in range(1, outs)]
            rhs = kernel_ref[0, kh].reshape(3 * chans, co)
            total += jnp.dot(jnp.concatenate(lhs, axis=0), rhs, preferred_element_type=F32)
        preact_ref[pl.ds(cells, (outs - 1) * cells), :] = total


def partial_preact(volume, kernel):
    _, planes, height, width, chans = volume.shape
    co = kernel.shape[-1]
    cells = height * width // 4
    h2, w2 = height // 2, width // 2
    return call(
        preact_kernel,
        (
            jax.ShapeDtypeStruct((planes // 2 * cells, co), F32),
            jax.ShapeDtypeStruct((planes, h2, w2, 3 * chans), BF16),
            jax.ShapeDtypeStruct((planes, h2 + 1, w2, 3 * chans), BF16),
        ),
        [pltpu.VMEM((height * width + 16, chans), F32)],
        flops=2 * planes // 2 * cells * 27 * chans * co,
        moved=6 * 2**20,
    )(volume, kernel)


def activation_kernel(preact_ref, share_ref, cotangent_ref, grad_ref, flipped_ref):
    cells = share_ref.shape[0]
    count = preact_ref.shape[0] // cells
    for d in range(count):
        rows = pl.ds(d * cells, cells)
        value = preact_ref[rows, :]
        if d == 0:
            value = value + share_ref[...].astype(F32)
        sig = jax.nn.sigmoid(value)
        slope = sig * (1.0 + value * (1.0 - sig))
        grad_ref[rows, :] = (cotangent_ref[rows, :].astype(F32) * slope).astype(BF16)
        flipped_ref[:, rows] = (value * sig).T.astype(BF16)


def activation(preact, share, cotangent):
    cells, co = preact.shape
    return call(
        activation_kernel,
        (
            jax.ShapeDtypeStruct((cells, co), BF16),
            jax.ShapeDtypeStruct((co, cells), BF16),
        ),
        flops=20 * cells * co,
        moved=2 * 2**20,
    )(preact, share, cotangent)


def store_units(product, scale, core, cores, chips, put):
    chans = product.shape[0] // 3
    co = product.shape[1]
    block = chans // (cores * chips)
    halves = co // 128
    product = product * scale
    for kw in range(3):
        for half in range(halves):
            unit = product[kw * chans : (kw + 1) * chans, half * 128 : (half + 1) * 128]
            unit = unit.reshape(chips, cores, block, 128)
            for chip in range(chips):
                first = unit[chip, 0]
                last = unit[chip, cores - 1]
                keep = jnp.where(core == 0, first, last)
                send = jnp.where(core == 0, last, first)
                put(kw * halves + half, chip, keep, send)


def kernel_grad_kernel(kds, chip_major, cores, chips, scale, *refs):
    even_ref, odd_ref, grads_ref = refs[:3]
    above_ref = refs[3] if 0 in kds else None
    keep_ref, send_ref = refs[-2:]
    outs = even_ref.shape[0] // 2
    cells = even_ref.shape[1] * even_ref.shape[2]
    core = lax.axis_index("dp") % cores
    per_row = 3 * (grads_ref.shape[1] // 128)
    for place, kd in enumerate(kds):
        if kd == 0:
            planes = [2 * d - 1 for d in range(1, outs + 1)]
            rhs = [grads_ref[pl.ds(d * cells, cells), :] for d in range(1, outs)] + [above_ref[...]]
            rhs = jnp.concatenate(rhs, axis=0)
        else:
            planes = [2 * d - 1 + kd for d in range(outs)]
            rhs = grads_ref[...]
        for kh in range(3):
            lhs = [tap_rows(even_ref, odd_ref, plane, kh) for plane in planes]
            product = lax.dot_general(
                jnp.concatenate(lhs, axis=0), rhs, (((0,), (0,)), ((), ())), preferred_element_type=F32
            )

            def put(unit, chip, keep, send, base=(place * 3 + kh) * per_row):
                where = (chip, base + unit) if chip_major else (base + unit, chip)
                keep_ref[where] = keep
                send_ref[where] = send.astype(BF16)

            store_units(product, scale, core, cores, chips, put)


def kernel_grad_part(even, odd, grads, above, kds, chip_major, cores, chips, scale):
    chans = even.shape[-1] // 3
    co = grads.shape[-1]
    units = len(kds) * 9 * (co // 128)
    block = chans // (cores * chips)
    shape = (chips, units, block, 128) if chip_major else (units, chips, block, 128)
    operands = (even, odd, grads) + ((above,) if 0 in kds else ())
    return call(
        functools.partial(kernel_grad_kernel, kds, chip_major, cores, chips, scale),
        (jax.ShapeDtypeStruct(shape, F32), jax.ShapeDtypeStruct(shape, BF16)),
        flops=2 * grads.shape[0] * len(kds) * 9 * chans * co,
        moved=6 * 2**20,
    )(*operands)


def volume_grad_kernel(grads_ref, above_ref, kernel_ref, out_ref, shifted, wide):
    planes, h2, _, width, chans = out_ref.shape
    w2 = width // 2
    cells = h2 * w2
    outs = planes // 2
    co = grads_ref.shape[1]
    here, right = [], []
    for d in range(outs + 1):
        plane = grads_ref[pl.ds(d * cells, cells), :] if d < outs else above_ref[...]
        shifted[pl.ds(0, cells), :] = plane.astype(F32)
        moved = shifted[pl.ds(1, cells), :]
        column = lax.broadcasted_iota(jnp.int32, moved.shape, 0) % w2
        moved = jnp.where(column == w2 - 1, 0.0, moved).astype(BF16)
        here.append(plane)
        right.append(moved)

    def down(rows):
        return jnp.concatenate([rows[w2:], jnp.zeros((w2, co), BF16)], axis=0)

    contract = (((1,), (1,)), ((), ()))
    for plane in range(planes):
        d = plane // 2
        depth = [(1, d)] if plane % 2 == 0 else [(2, d), (0, d + 1)]
        for odd_row in range(2):
            taps = [(1, False)] if odd_row == 0 else [(2, False), (0, True)]
            both, right_only = None, None
            for kd, source in depth:
                for kh, lower in taps:
                    lhs = down(here[source]) if lower else here[source]
                    rhs = kernel_ref[kd, kh, pl.ds(1, 2)].reshape(2 * chans, co)
                    term = lax.dot_general(lhs, rhs, contract, preferred_element_type=F32)
                    both = term if both is None else both + term
                    lhs = down(right[source]) if lower else right[source]
                    term = lax.dot_general(lhs, kernel_ref[kd, kh, 0], contract, preferred_element_type=F32)
                    right_only = term if right_only is None else right_only + term
            wide[pl.ds(0, cells, stride=2), :] = both[:, :chans]
            wide[pl.ds(1, cells, stride=2), :] = both[:, chans:] + right_only
            out_ref[plane, :, odd_row] = wide[...].reshape(h2, width, chans).astype(BF16)


def volume_grad_of(grads, above, kernel, height, width):
    cells, co = grads.shape
    chans = kernel.shape[3]
    planes = 2 * cells * 4 // (height * width)
    shape = (planes, height // 2, 2, width, chans)
    return call(
        volume_grad_kernel,
        jax.ShapeDtypeStruct(shape, BF16),
        [
            pltpu.VMEM((height * width // 4 + 8, co), F32),
            pltpu.VMEM((height * width // 2, chans), F32),
        ],
        flops=2 * cells * 27 * chans * co,
        moved=4 * 2**20,
    )(grads, above, kernel)


def bits_of(count):
    bits = count.bit_length() - 1
    assert 1 << bits == count
    return bits


def exchange(value, partner):
    dp, space = lax.axis_size("dp"), lax.axis_size("space")
    pairs = []
    for i in range(dp):
        for j in range(space):
            to_dp, to_space = partner(i, j)
            pairs.append((i * space + j, to_dp * space + to_space))
    return lax.ppermute(value, ("dp", "space"), pairs)


def space_bit(stage, odd_core):
    bits = bits_of(lax.axis_size("space"))
    return bits - 1 - stage if odd_core else stage


def space_partner(stage, cores):
    return lambda i, j: (i, j ^ (1 << space_bit(stage, cores == 2 and i % 2 == 1)))


def my_space_bit(stage, cores):
    index = lax.axis_index("space")
    even = (index >> space_bit(stage, False)) & 1
    odd = (index >> space_bit(stage, True)) & 1
    return jnp.where(lax.axis_index("dp") % cores == 1, odd, even) if cores == 2 else even


def halve(value, bit):
    value = value.reshape((2, value.shape[0] // 2) + value.shape[1:])
    keep = lax.dynamic_index_in_dim(value, bit, 0, keepdims=False)
    send = lax.dynamic_index_in_dim(value, 1 - bit, 0, keepdims=False)
    return keep, send.astype(BF16)


def scatter_space(value, cores):
    for stage in range(bits_of(lax.axis_size("space"))):
        keep, send = halve(value, my_space_bit(stage, cores))
        value = keep + exchange(send, space_partner(stage, cores)).astype(F32)
    return value


def scatter_chips(value, cores, chips):
    order = list(range(bits_of(chips)))
    if order:
        rest = value.shape[1:]
        value = value.reshape((2,) * len(order) + rest)
        value = jnp.transpose(
            value, tuple(reversed(order)) + tuple(range(len(order), len(order) + len(rest)))
        )
        value = value.reshape((chips,) + rest)
    chip = lax.axis_index("dp") // cores
    for bit in order:
        keep, send = halve(value, (chip >> bit) & 1)
        got = exchange(send, lambda i, j, bit=bit: (i ^ (cores << bit), j))
        value = keep + got.astype(F32)
    return value[0]


def gather_space(value, cores):
    value = value[None]
    for stage in reversed(range(bits_of(lax.axis_size("space")))):
        got = exchange(value, space_partner(stage, cores))
        bit = my_space_bit(stage, cores)
        value = jnp.where(
            bit == 0, jnp.concatenate([value, got], 0), jnp.concatenate([got, value], 0)
        )
    return value


def neighbour(value, steps):
    count = lax.axis_size("space")
    first, last = (max(0, -steps), min(count, count - steps))
    return lax.ppermute(value, "space", [(source, source + steps) for source in range(first, last)])


def add_cores(keep, send, cores):
    if cores == 1:
        return keep
    return keep + exchange(send, lambda i, j: (i ^ 1, j)).astype(F32)


def reduce_parts(early, late, cores, chips):
    space = lax.axis_size("space")
    units, _, block, lanes = early.shape
    extra = -units % space
    early = jnp.pad(early, ((0, extra), (0, 0), (0, 0), (0, 0)))
    early = scatter_space(early, cores)
    early = scatter_chips(jnp.swapaxes(early, 0, 1), cores, chips)
    late_units = late.shape[1]
    late = scatter_chips(late, cores, chips)
    late = jnp.pad(late, ((0, -late_units % space), (0, 0), (0, 0)))
    late = scatter_space(late, cores)
    full = gather_space(jnp.concatenate([early, late], axis=0).astype(BF16), cores)
    cut = early.shape[0]
    early = full[:, :cut].reshape(-1, block, lanes)[:units]
    late = full[:, cut:].reshape(-1, block, lanes)[:late_units]
    return early, late


def body(volume, kernel, cotangent):
    samples, planes, height, width, ci = volume.shape
    co = kernel.shape[-1]
    assert samples == 1
    dp, space = lax.axis_size("dp"), lax.axis_size("space")
    cores = 2 if dp % 2 == 0 else 1
    chips = dp // cores
    outs = planes // 2
    cells = height * width // 4
    scale = 1.0 / math.sqrt(dp * space * samples * outs * cells)

    share = neighbour(halo_share(volume, kernel), 1)
    preact, even, odd = partial_preact(volume, kernel)
    grads, flipped = activation(preact, share, cotangent.reshape(outs * cells, co))
    above = neighbour(grads[:cells], -1)

    early = kernel_grad_part(even, odd, grads, None, (1, 2), False, cores, chips, scale)
    early = add_cores(*early, cores)
    late = kernel_grad_part(even, odd, grads, above, (0,), True, cores, chips, scale)
    late = add_cores(*late, cores)
    early, late = reduce_parts(early, late, cores, chips)

    switched = lax.all_to_all(
        flipped.reshape(space, co // space, outs * cells), "space", 0, 0, tiled=True
    )
    switched = jnp.swapaxes(switched, 0, 1).reshape(1, co // space, space * outs * cells)

    volume_grad = volume_grad_of(grads, above, kernel, height, width).reshape(volume.shape)

    lanes = late.shape[-1]
    taps = jnp.concatenate([late, early], axis=0).reshape(3, 3, 3, co // lanes, ci // dp, lanes)
    kernel_grad = jnp.swapaxes(taps, 3, 4).reshape(3, 3, 3, ci // dp, co).astype(F32)
    return (switched, volume_grad, kernel_grad)


def solution(mesh):
    in_specs = (P("dp", "space", None, None, None), P(), P("dp", "space", None, None, None))
    out_specs = (
        P("dp", "space", None),
        P("dp", "space", None, None, None),
        P(None, None, None, "dp", None),
    )
    return jax.shard_map(body, mesh=mesh, in_specs=in_specs, out_specs=out_specs, check_vma=False)
```

```python
import functools
import math

import jax
import jax.numpy as jnp
from jax import lax
from jax.experimental import pallas as pl
from jax.experimental.pallas import tpu as pltpu
from jax.sharding import PartitionSpec as P

BF16 = jnp.bfloat16
F32 = jnp.float32
VMEM_LIMIT = 20 * 1024 * 1024
VMEM_WHOLE = 60 * 1024 * 1024


def call(kernel, out_shape, scratch=(), in_specs=None, limit=VMEM_LIMIT):
    extra = {} if in_specs is None else {"in_specs": in_specs}
    return pl.pallas_call(
        kernel,
        out_shape=out_shape,
        scratch_shapes=list(scratch),
        compiler_params=pltpu.CompilerParams(vmem_limit_bytes=limit),
        cost_estimate=pl.CostEstimate(flops=1000, bytes_accessed=1000, transcendentals=0),
        **extra,
    )


def after(value, *others):
    return lax.optimization_barrier((value,) + others)[0]


def spread_plane(plane, wide):
    height, width, chans = plane.shape
    cells = height * width
    half = width // 2
    wide[pl.ds(8, cells), :] = plane.reshape(cells, chans).astype(F32)
    left = wide[pl.ds(7, cells // 2, stride=2), :]
    even = wide[pl.ds(8, cells // 2, stride=2), :]
    odd = wide[pl.ds(9, cells // 2, stride=2), :]
    column = lax.broadcasted_iota(jnp.int32, left.shape, 0) % half
    left = jnp.where(column == 0, 0.0, left)
    joined = jnp.concatenate([left.astype(BF16), even.astype(BF16), odd.astype(BF16)], axis=1)
    joined = joined.reshape(height // 2, 2, half, 3 * chans)
    return joined[:, 0], joined[:, 1]


def tap_rows(even, odd, plane, kh):
    height = even.shape[1]
    picked = even[plane] if kh == 1 else odd[plane, pl.ds(0 if kh == 0 else 1, height)]
    return picked.reshape(height * even.shape[2], even.shape[3])


def bits_of(count):
    bits = count.bit_length() - 1
    assert 1 << bits == count
    return bits


def odd_core(cores):
    return lax.axis_index("dp") % cores == 1 if cores == 2 else False


def reverse_bits(value, bits):
    return sum(((value >> bit) & 1) << (bits - 1 - bit) for bit in range(bits))


def staged_place(target, space, cores):
    return jnp.where(odd_core(cores), target, reverse_bits(target, bits_of(space)))


def relative_place(source, space, cores):
    bits = bits_of(space)
    off = source ^ lax.axis_index("space")
    return jnp.where(odd_core(cores), reverse_bits(off, bits), off)


def relative_group(group, space, cores):
    bits = bits_of(space)
    index = lax.axis_index("space")
    mine = jnp.where(odd_core(cores), index, reverse_bits(index, bits))
    return group ^ mine


def halo_kernel(volume_ref, kernel_ref, share_ref, plane, weights, wide, sems):
    planes, height, width, chans = volume_ref.shape[1:]
    first = pltpu.make_async_copy(volume_ref.at[0, planes - 1], plane, sems.at[0])
    second = pltpu.make_async_copy(kernel_ref.at[0], weights, sems.at[1])
    first.start()
    second.start()
    first.wait()
    even, odd = spread_plane(plane[...], wide)
    above = jnp.concatenate([jnp.zeros_like(odd[:1]), odd[:-1]], axis=0)
    second.wait()
    total = None
    for kh, rows in enumerate((above, even, odd)):
        lhs = rows.reshape(height * width // 4, 3 * chans)
        rhs = weights[kh].reshape(3 * chans, weights.shape[-1])
        term = jnp.dot(lhs, rhs, preferred_element_type=F32)
        total = term if total is None else total + term
    share_ref[...] = total.astype(BF16)


def halo_share(volume, kernel):
    _, planes, height, width, chans = volume.shape
    co = kernel.shape[-1]
    return call(
        halo_kernel,
        jax.ShapeDtypeStruct((height * width // 4, co), BF16),
        [
            pltpu.VMEM((height, width, chans), BF16),
            pltpu.VMEM((3, 3, chans, co), BF16),
            pltpu.VMEM((height * width + 16, chans), F32),
            pltpu.SemaphoreType.DMA((2,)),
        ],
        [pl.BlockSpec(memory_space=pltpu.HBM)] * 2,
        VMEM_WHOLE,
    )(volume, kernel)


def preact_kernel(volume_ref, kernel_ref, preact_ref, even_ref, odd_ref, slab, weights, wide, sems):
    planes, height, width, chans = volume_ref.shape[1:]
    cells = height * width // 4
    outs = planes // 2
    copies = [
        pltpu.make_async_copy(volume_ref.at[0, plane], slab.at[plane], sems.at[plane])
        for plane in range(planes)
    ]
    loads = {
        kd: pltpu.make_async_copy(kernel_ref.at[kd], weights.at[kd], sems.at[planes + kd])
        for kd in range(3)
    }
    for copy in copies:
        copy.start()
    for kd in (1, 2, 0):
        loads[kd].start()
    for plane in range(planes):
        copies[plane].wait()
        even, odd = spread_plane(slab[plane], wide)
        even_ref[plane] = even
        odd_ref[plane, pl.ds(0, 1)] = jnp.zeros_like(odd[:1])
        odd_ref[plane, pl.ds(1, height // 2)] = odd
    co = kernel_ref.shape[-1]
    total = None
    for kd in (1, 2):
        loads[kd].wait()
        for kh in range(3):
            lhs = [tap_rows(even_ref, odd_ref, 2 * d - 1 + kd, kh) for d in range(outs)]
            rhs = weights[kd, kh].reshape(3 * chans, co)
            term = jnp.dot(jnp.concatenate(lhs, axis=0), rhs, preferred_element_type=F32)
            total = term if total is None else total + term
    preact_ref[...] = total
    loads[0].wait()
    if outs > 1:
        total = preact_ref[pl.ds(cells, (outs - 1) * cells), :]
        for kh in range(3):
            lhs = [tap_rows(even_ref, odd_ref, 2 * d - 1, kh) for d in range(1, outs)]
            rhs = weights[0, kh].reshape(3 * chans, co)
            total += jnp.dot(jnp.concatenate(lhs, axis=0), rhs, preferred_element_type=F32)
        preact_ref[pl.ds(cells, (outs - 1) * cells), :] = total


def partial_preact(volume, kernel):
    _, planes, height, width, chans = volume.shape
    co = kernel.shape[-1]
    cells = height * width // 4
    h2, w2 = height // 2, width // 2
    return call(
        preact_kernel,
        (
            jax.ShapeDtypeStruct((planes // 2 * cells, co), F32),
            jax.ShapeDtypeStruct((planes, h2, w2, 3 * chans), BF16),
            jax.ShapeDtypeStruct((planes, h2 + 1, w2, 3 * chans), BF16),
        ),
        [
            pltpu.VMEM(volume.shape[1:], BF16),
            pltpu.VMEM(kernel.shape, BF16),
            pltpu.VMEM((height * width + 16, chans), F32),
            pltpu.SemaphoreType.DMA((planes + 3,)),
        ],
        [pl.BlockSpec(memory_space=pltpu.HBM)] * 2,
    )(volume, kernel)


def activation_kernel(space, cores, preact_ref, share_ref, cotangent_ref, grad_ref, flipped_ref):
    cells, co = share_ref.shape
    count = preact_ref.shape[0] // cells
    group = co // space
    strips = cells // 128
    for d in range(count):
        rows = pl.ds(d * cells, cells)
        value = preact_ref[rows, :]
        if d == 0:
            value = value + share_ref[...].astype(F32)
        sig = jax.nn.sigmoid(value)
        slope = sig * (1.0 + value * (1.0 - sig))
        grad_ref[rows, :] = (cotangent_ref[rows, :].astype(F32) * slope).astype(BF16)
        flipped = (value * sig).T.astype(BF16)
        for target in range(space):
            place = staged_place(target, space, cores)
            for strip in range(strips):
                flipped_ref[place, d * strips + strip] = flipped[
                    target * group : (target + 1) * group, strip * 128 : (strip + 1) * 128
                ]


def activation(preact, share, cotangent, space, cores):
    cells, co = preact.shape
    return call(
        functools.partial(activation_kernel, space, cores),
        (
            jax.ShapeDtypeStruct((cells, co), BF16),
            jax.ShapeDtypeStruct((space, cells // 128, co // space, 128), BF16),
        ),
    )(preact, share, cotangent)


def switched_kernel(space, cores, kept_ref, got_ref, out_ref):
    half = space // 2
    strips = kept_ref.shape[0] // half
    for source in range(space):
        place = relative_place(source, space, cores)
        for strip in range(strips):
            column = (source * strips + strip) * 128
            far = place // half
            row = (place % half) * strips + strip
            out_ref[:, column : column + 128] = jnp.where(far == 1, got_ref[row], kept_ref[row])


def switched_of(kept, got, space, cores):
    half = space // 2
    group = kept.shape[-2]
    kept = kept.reshape(-1, group, 128)
    got = got.reshape(-1, group, 128)
    return call(
        functools.partial(switched_kernel, space, cores),
        jax.ShapeDtypeStruct((group, 2 * kept.shape[0] * 128), BF16),
    )(kept, got)


def kernel_grad_out_kernel(space, cores, early_units, late_units, pieces_ref, out_ref):
    block = pieces_ref.shape[2]
    halves = out_ref.shape[-1] // 128
    early_share = -(-early_units // space)
    late_share = -(-late_units // space)
    for group in range(space):
        place = relative_group(group, space, cores)
        for unit in range(early_share + late_share):
            late = unit >= early_share
            index = group * late_share + unit - early_share if late else group * early_share + unit
            if index >= (late_units if late else early_units):
                continue
            index = index if late else index + late_units
            tap, half = divmod(index, halves)
            out_ref[tap, :, half * 128 : (half + 1) * 128] = pieces_ref[place, unit].astype(F32)


def kernel_grad_out(pieces, early_units, late_units, space, cores, co):
    taps = (early_units + late_units) * 128 // co
    return call(
        functools.partial(kernel_grad_out_kernel, space, cores, early_units, late_units),
        jax.ShapeDtypeStruct((taps, pieces.shape[2], co), F32),
    )(pieces)


def store_units(product, scale, core, cores, chips, put):
    chans = product.shape[0] // 3
    co = product.shape[1]
    block = chans // (cores * chips)
    halves = co // 128
    product = product * scale
    for kw in range(3):
        for half in range(halves):
            unit = product[kw * chans : (kw + 1) * chans, half * 128 : (half + 1) * 128]
            unit = unit.reshape(chips, cores, block, 128)
            for chip in range(chips):
                first = unit[chip, 0]
                last = unit[chip, cores - 1]
                keep = jnp.where(core == 0, first, last)
                send = jnp.where(core == 0, last, first)
                put(kw * halves + half, chip, keep, send)


def kernel_grad_kernel(kds, chip_major, cores, chips, scale, *refs):
    even_ref, odd_ref, grads_ref = refs[:3]
    above_ref = refs[3] if 0 in kds else None
    keep_ref, send_ref = refs[-2:]
    outs = even_ref.shape[0] // 2
    cells = even_ref.shape[1] * even_ref.shape[2]
    core = lax.axis_index("dp") % cores
    per_row = 3 * (grads_ref.shape[1] // 128)
    for place, kd in enumerate(kds):
        if kd == 0:
            planes = [2 * d - 1 for d in range(1, outs + 1)]
            rhs = [grads_ref[pl.ds(d * cells, cells), :] for d in range(1, outs)] + [above_ref[...]]
            rhs = jnp.concatenate(rhs, axis=0)
        else:
            planes = [2 * d - 1 + kd for d in range(outs)]
            rhs = grads_ref[...]
        for kh in range(3):
            lhs = [tap_rows(even_ref, odd_ref, plane, kh) for plane in planes]
            product = lax.dot_general(
                jnp.concatenate(lhs, axis=0), rhs, (((0,), (0,)), ((), ())), preferred_element_type=F32
            )

            def put(unit, chip, keep, send, base=(place * 3 + kh) * per_row):
                where = (chip, base + unit) if chip_major else (base + unit, chip)
                keep_ref[where] = keep
                send_ref[where] = send.astype(BF16)

            store_units(product, scale, core, cores, chips, put)


def kernel_grad_part(even, odd, grads, above, kds, chip_major, cores, chips, scale):
    chans = even.shape[-1] // 3
    co = grads.shape[-1]
    units = len(kds) * 9 * (co // 128)
    block = chans // (cores * chips)
    shape = (chips, units, block, 128) if chip_major else (units, chips, block, 128)
    operands = (even, odd, grads) + ((above,) if 0 in kds else ())
    return call(
        functools.partial(kernel_grad_kernel, kds, chip_major, cores, chips, scale),
        (jax.ShapeDtypeStruct(shape, F32), jax.ShapeDtypeStruct(shape, BF16)),
    )(*operands)


def volume_grad_kernel(grads_ref, above_ref, kernel_ref, out_ref, shifted, wide):
    planes, h2, _, width, chans = out_ref.shape
    w2 = width // 2
    cells = h2 * w2
    outs = planes // 2
    co = grads_ref.shape[1]
    here, right = [], []
    for d in range(outs + 1):
        plane = grads_ref[pl.ds(d * cells, cells), :] if d < outs else above_ref[...]
        shifted[pl.ds(0, cells), :] = plane.astype(F32)
        moved = shifted[pl.ds(1, cells), :]
        column = lax.broadcasted_iota(jnp.int32, moved.shape, 0) % w2
        moved = jnp.where(column == w2 - 1, 0.0, moved).astype(BF16)
        here.append(plane)
        right.append(moved)

    def down(rows):
        return jnp.concatenate([rows[w2:], jnp.zeros((w2, co), BF16)], axis=0)

    contract = (((1,), (1,)), ((), ()))
    for plane in range(planes):
        d = plane // 2
        depth = [(1, d)] if plane % 2 == 0 else [(2, d), (0, d + 1)]
        for odd_row in range(2):
            taps = [(1, False)] if odd_row == 0 else [(2, False), (0, True)]
            both, right_only = None, None
            for kd, source in depth:
                for kh, lower in taps:
                    lhs = down(here[source]) if lower else here[source]
                    rhs = kernel_ref[kd, kh, pl.ds(1, 2)].reshape(2 * chans, co)
                    term = lax.dot_general(lhs, rhs, contract, preferred_element_type=F32)
                    both = term if both is None else both + term
                    lhs = down(right[source]) if lower else right[source]
                    term = lax.dot_general(lhs, kernel_ref[kd, kh, 0], contract, preferred_element_type=F32)
                    right_only = term if right_only is None else right_only + term
            wide[pl.ds(0, cells, stride=2), :] = both[:, :chans]
            wide[pl.ds(1, cells, stride=2), :] = both[:, chans:] + right_only
            out_ref[plane, :, odd_row] = wide[...].reshape(h2, width, chans).astype(BF16)


def volume_grad_of(grads, above, kernel, height, width):
    cells, co = grads.shape
    chans = kernel.shape[3]
    planes = 2 * cells * 4 // (height * width)
    shape = (planes, height // 2, 2, width, chans)
    return call(
        volume_grad_kernel,
        jax.ShapeDtypeStruct(shape, BF16),
        [
            pltpu.VMEM((height * width // 4 + 8, co), F32),
            pltpu.VMEM((height * width // 2, chans), F32),
        ],
    )(grads, above, kernel)


def exchange(value, partner):
    dp, space = lax.axis_size("dp"), lax.axis_size("space")
    pairs = []
    for i in range(dp):
        for j in range(space):
            to_dp, to_space = partner(i, j)
            pairs.append((i * space + j, to_dp * space + to_space))
    return lax.ppermute(value, ("dp", "space"), pairs)


def exchange_space(value, stage, cores):
    bits = bits_of(lax.axis_size("space"))

    def partner(i, j):
        bit = bits - 1 - stage if cores == 2 and i % 2 == 1 else stage
        return i, j ^ (1 << bit)

    return exchange(value, partner)


def exchange_chips(value, bit, cores):
    return exchange(value, lambda i, j: (i ^ (cores << bit), j))


def space_bit(stage, cores):
    bits = bits_of(lax.axis_size("space"))
    index = lax.axis_index("space")
    even, odd = (index >> stage) & 1, (index >> (bits - 1 - stage)) & 1
    return jnp.where(odd_core(cores), odd, even)


def chip_bit(bit, cores):
    return ((lax.axis_index("dp") // cores) >> bit) & 1


def pick(value, bit):
    value = value.reshape((2, value.shape[0] // 2) + value.shape[1:])
    return lax.dynamic_index_in_dim(value, bit, 0, keepdims=False)


def by_nearest(value, chips):
    count = bits_of(chips)
    if count < 2:
        return value
    rest = value.shape[1:]
    value = value.reshape((2,) * count + rest)
    order = tuple(reversed(range(count))) + tuple(range(count, count + len(rest)))
    return jnp.transpose(value, order).reshape((chips,) + rest)


def neighbour(value, steps):
    count = lax.axis_size("space")
    first, last = (max(0, -steps), min(count, count - steps))
    return lax.ppermute(value, "space", [(source, source + steps) for source in range(first, last)])


def add_cores(keep, send, cores):
    if cores == 1:
        return keep
    return keep + exchange(send, lambda i, j: (i ^ 1, j)).astype(F32)


def pad_units(value, space):
    extra = -value.shape[0] % space
    return jnp.pad(value, ((0, extra),) + ((0, 0),) * (value.ndim - 1)) if extra else value


def rows_of(value):
    return value.reshape(-1, value.shape[-1])


def early_chain(value, cores, chips):
    for stage in range(bits_of(lax.axis_size("space"))):
        bit = space_bit(stage, cores)
        sent = pick(value, 1 - bit).astype(BF16)
        got = exchange_space(sent, stage, cores)
        got = after(got, *(yield sent))
        value = pick(value, bit) + got.astype(F32)
    value = by_nearest(jnp.swapaxes(value, 0, 1), chips)
    for stage in range(bits_of(chips)):
        bit = chip_bit(stage, cores)
        sent = pick(value, 1 - bit).astype(BF16)
        got = exchange_chips(sent, stage, cores)
        got = after(got, *(yield sent))
        value = pick(value, bit) + got.astype(F32)
    return value[0]


def late_chain(value, switch, cores, chips):
    value = by_nearest(value, chips)
    for stage in range(bits_of(chips)):
        bit = chip_bit(stage, cores)
        sent = pick(value, 1 - bit).astype(BF16)
        got = exchange_chips(sent, stage, cores)
        got = after(got, *(yield sent))
        value = pick(value, bit) + got.astype(F32)
    value = pad_units(value[0], lax.axis_size("space"))
    stay, moved = switch[None], None
    for stage in range(bits_of(lax.axis_size("space"))):
        bit = space_bit(stage, cores)
        if moved is not None:
            stay = jnp.concatenate([stay, moved], axis=0)
        halves = stay.reshape((stay.shape[0], 2, stay.shape[1] // 2) + stay.shape[2:])
        out = lax.dynamic_index_in_dim(halves, 1 - bit, 1, keepdims=False)
        stay = lax.dynamic_index_in_dim(halves, bit, 1, keepdims=False)
        sent = pick(value, 1 - bit).astype(BF16)
        got = exchange_space(jnp.concatenate([rows_of(sent), rows_of(out)], axis=0), stage, cores)
        got = after(got, *(yield sent))
        cut = sent.size // sent.shape[-1]
        moved = got[cut:].reshape(out.shape)
        value = pick(value, bit) + got[:cut].reshape(sent.shape).astype(F32)
    return value, stay, moved


def body(volume, kernel, cotangent):
    samples, planes, height, width, ci = volume.shape
    co = kernel.shape[-1]
    assert samples == 1
    dp, space = lax.axis_size("dp"), lax.axis_size("space")
    cores = 2 if dp % 2 == 0 else 1
    chips = dp // cores
    outs = planes // 2
    cells = height * width // 4
    scale = 1.0 / math.sqrt(dp * space * samples * outs * cells)

    share = neighbour(halo_share(volume, kernel), 1)
    preact, even, odd = partial_preact(volume, kernel)
    grads, flipped = activation(preact, share, cotangent.reshape(outs * cells, co), space, cores)
    first = grads[:cells]
    grads, first = lax.optimization_barrier((grads, first))
    above = neighbour(first, -1)

    early = kernel_grad_part(even, odd, grads, None, (1, 2), False, cores, chips, scale)
    early_units = early[0].shape[0]
    ahead = early_chain(pad_units(add_cores(*early, cores), space), cores, chips)
    token = next(ahead)

    above = after(above, token)
    late = kernel_grad_part(even, odd, grads, above, (0,), True, cores, chips, scale)
    late_units = late[0].shape[1]
    behind = late_chain(add_cores(*late, cores), flipped, cores, chips)
    late_token = next(behind)

    volume_grad = volume_grad_of(grads, after(above, late_token), kernel, height, width)
    tokens = (late_token, volume_grad)
    early_total = late_total = None
    while early_total is None or late_total is None:
        if early_total is None:
            try:
                tokens = (ahead.send(tokens),)
            except StopIteration as end:
                early_total = end.value
                tokens = (early_total,)
        if late_total is None:
            try:
                tokens = (behind.send(tokens),)
            except StopIteration as end:
                late_total, kept, arrived = end.value
                tokens = (late_total,)

    pieces = jnp.concatenate([early_total, late_total], axis=0).astype(BF16)[None]
    switched = None
    for stage in reversed(range(bits_of(space))):
        got = exchange_space(pieces, stage, cores)
        if switched is None:
            switched = switched_of(after(kept, pieces), arrived, space, cores)
            got = after(got, switched)
        pieces = jnp.concatenate([pieces, got], axis=0)
    kernel_grad = kernel_grad_out(pieces, early_units, late_units, space, cores, co)

    return (
        switched[None],
        volume_grad.reshape(volume.shape),
        kernel_grad.reshape(3, 3, 3, ci // dp, co),
    )


def solution(mesh):
    in_specs = (P("dp", "space", None, None, None), P(), P("dp", "space", None, None, None))
    out_specs = (
        P("dp", "space", None),
        P("dp", "space", None, None, None),
        P(None, None, None, "dp", None),
    )
    return jax.shard_map(body, mesh=mesh, in_specs=in_specs, out_specs=out_specs, check_vma=False)
```

```python
import functools
import math

import jax
import jax.numpy as jnp
from jax import lax
from jax.experimental import pallas as pl
from jax.experimental.pallas import tpu as pltpu
from jax.sharding import PartitionSpec as P

BF16 = jnp.bfloat16
F32 = jnp.float32
VMEM_LIMIT = 20 * 1024 * 1024
DONE = (8, 128)
VMEM_WHOLE = 63 * 1024 * 1024


def call(kernel, out_shape, scratch=(), in_specs=None, limit=VMEM_LIMIT, order=(), inputs=0):
    extra = {} if in_specs is None else {"in_specs": in_specs}
    if order:
        whole = pl.BlockSpec(memory_space=pltpu.VMEM)
        extra["in_specs"] = [whole] * inputs + [pl.BlockSpec(memory_space=pl.ANY)] * len(order)
        inner, count = kernel, len(order)

        def kernel(*refs):
            inner(*refs[:inputs], *refs[inputs + count :])

    return pl.pallas_call(
        kernel,
        out_shape=out_shape,
        scratch_shapes=list(scratch),
        compiler_params=pltpu.CompilerParams(vmem_limit_bytes=limit),
        cost_estimate=pl.CostEstimate(flops=1000, bytes_accessed=1000, transcendentals=0),
        **extra,
    )


def spread_plane(plane, wide):
    height, width, chans = plane.shape
    cells = height * width
    half = width // 2
    wide[pl.ds(8, cells), :] = plane.reshape(cells, chans).astype(F32)
    left = wide[pl.ds(7, cells // 2, stride=2), :]
    even = wide[pl.ds(8, cells // 2, stride=2), :]
    odd = wide[pl.ds(9, cells // 2, stride=2), :]
    column = lax.broadcasted_iota(jnp.int32, left.shape, 0) % half
    left = jnp.where(column == 0, 0.0, left)
    joined = jnp.concatenate([left.astype(BF16), even.astype(BF16), odd.astype(BF16)], axis=1)
    joined = joined.reshape(height // 2, 2, half, 3 * chans)
    return joined[:, 0], joined[:, 1]


def tap_rows(even, odd, plane, kh):
    height = even.shape[1]
    picked = even[plane] if kh == 1 else odd[plane, pl.ds(0 if kh == 0 else 1, height)]
    return picked.reshape(height * even.shape[2], even.shape[3])


def bits_of(count):
    bits = count.bit_length() - 1
    assert 1 << bits == count
    return bits


def odd_core(cores):
    return lax.axis_index("dp") % cores == 1 if cores == 2 else False


def reverse_bits(value, bits):
    return sum(((value >> bit) & 1) << (bits - 1 - bit) for bit in range(bits))


def staged_place(target, space, cores):
    return jnp.where(odd_core(cores), target, reverse_bits(target, bits_of(space)))


def relative_place(source, space, cores):
    bits = bits_of(space)
    off = source ^ lax.axis_index("space")
    return jnp.where(odd_core(cores), reverse_bits(off, bits), off)


def relative_group(group, space, cores):
    bits = bits_of(space)
    index = lax.axis_index("space")
    mine = jnp.where(odd_core(cores), index, reverse_bits(index, bits))
    return group ^ mine


def halo_kernel(volume_ref, kernel_ref, share_ref, plane, weights, wide, sems):
    planes, height, width, chans = volume_ref.shape[1:]
    first = pltpu.make_async_copy(volume_ref.at[0, planes - 1], plane, sems.at[0])
    second = pltpu.make_async_copy(kernel_ref.at[0], weights, sems.at[1])
    first.start()
    second.start()
    first.wait()
    even, odd = spread_plane(plane[...], wide)
    above = jnp.concatenate([jnp.zeros_like(odd[:1]), odd[:-1]], axis=0)
    second.wait()
    total = None
    for kh, rows in enumerate((above, even, odd)):
        lhs = rows.reshape(height * width // 4, 3 * chans)
        rhs = weights[kh].reshape(3 * chans, weights.shape[-1])
        term = jnp.dot(lhs, rhs, preferred_element_type=F32)
        total = term if total is None else total + term
    share_ref[...] = total.astype(BF16)


def halo_share(volume, kernel):
    _, planes, height, width, chans = volume.shape
    co = kernel.shape[-1]
    return call(
        halo_kernel,
        jax.ShapeDtypeStruct((height * width // 4, co), BF16),
        [
            pltpu.VMEM((height, width, chans), BF16),
            pltpu.VMEM((3, 3, chans, co), BF16),
            pltpu.VMEM((height * width + 16, chans), F32),
            pltpu.SemaphoreType.DMA((2,)),
        ],
        [pl.BlockSpec(memory_space=pltpu.HBM)] * 2,
        VMEM_WHOLE,
    )(volume, kernel)


def preact_kernel(volume_ref, kernel_ref, preact_ref, even_ref, odd_ref, wide):
    planes, height, width, chans = volume_ref.shape[1:]
    cells = height * width // 4
    outs = planes // 2
    for plane in range(planes):
        even, odd = spread_plane(volume_ref[0, plane], wide)
        even_ref[plane] = even
        odd_ref[plane, pl.ds(0, 1)] = jnp.zeros_like(odd[:1])
        odd_ref[plane, pl.ds(1, height // 2)] = odd
    co = kernel_ref.shape[-1]
    total = None
    for kd in (1, 2):
        for kh in range(3):
            lhs = [tap_rows(even_ref, odd_ref, 2 * d - 1 + kd, kh) for d in range(outs)]
            rhs = kernel_ref[kd, kh].reshape(3 * chans, co)
            term = jnp.dot(jnp.concatenate(lhs, axis=0), rhs, preferred_element_type=F32)
            total = term if total is None else total + term
    preact_ref[...] = total
    if outs > 1:
        total = preact_ref[pl.ds(cells, (outs - 1) * cells), :]
        for kh in range(3):
            lhs = [tap_rows(even_ref, odd_ref, 2 * d - 1, kh) for d in range(1, outs)]
            rhs = kernel_ref[0, kh].reshape(3 * chans, co)
            total += jnp.dot(jnp.concatenate(lhs, axis=0), rhs, preferred_element_type=F32)
        preact_ref[pl.ds(cells, (outs - 1) * cells), :] = total


def partial_preact(volume, kernel):
    _, planes, height, width, chans = volume.shape
    co = kernel.shape[-1]
    cells = height * width // 4
    h2, w2 = height // 2, width // 2
    return call(
        preact_kernel,
        (
            jax.ShapeDtypeStruct((planes // 2 * cells, co), F32),
            jax.ShapeDtypeStruct((planes, h2, w2, 3 * chans), BF16),
            jax.ShapeDtypeStruct((planes, h2 + 1, w2, 3 * chans), BF16),
        ),
        [pltpu.VMEM((height * width + 16, chans), F32)],
    )(volume, kernel)


def activation_kernel(space, cores, preact_ref, share_ref, cotangent_ref, grad_ref, flipped_ref):
    cells, co = share_ref.shape
    count = preact_ref.shape[0] // cells
    group = co // space
    strips = cells // 128
    for d in range(count):
        rows = pl.ds(d * cells, cells)
        value = preact_ref[rows, :]
        if d == 0:
            value = value + share_ref[...].astype(F32)
        sig = jax.nn.sigmoid(value)
        slope = sig * (1.0 + value * (1.0 - sig))
        grad_ref[rows, :] = (cotangent_ref[rows, :].astype(F32) * slope).astype(BF16)
        flipped = (value * sig).T.astype(BF16)
        for target in range(space):
            place = staged_place(target, space, cores)
            for strip in range(strips):
                flipped_ref[place, d * strips + strip] = flipped[
                    target * group : (target + 1) * group, strip * 128 : (strip + 1) * 128
                ]


def activation(preact, share, cotangent, space, cores):
    cells, co = preact.shape
    return call(
        functools.partial(activation_kernel, space, cores),
        (
            jax.ShapeDtypeStruct((cells, co), BF16),
            jax.ShapeDtypeStruct((space, cells // 128, co // space, 128), BF16),
        ),
    )(preact, share, cotangent)


def switched_kernel(space, cores, kept_ref, got_ref, out_ref, done_ref):
    done_ref[...] = jnp.zeros_like(done_ref)
    half = space // 2
    strips = kept_ref.shape[0] // half
    for source in range(space):
        place = relative_place(source, space, cores)
        for strip in range(strips):
            column = (source * strips + strip) * 128
            far = place // half
            row = (place % half) * strips + strip
            out_ref[:, column : column + 128] = jnp.where(far == 1, got_ref[row], kept_ref[row])


def switched_of(kept, got, space, cores, order):
    group = kept.shape[-2]
    kept = kept.reshape(-1, group, 128)
    got = got.reshape(-1, group, 128)
    return call(
        functools.partial(switched_kernel, space, cores),
        (
            jax.ShapeDtypeStruct((group, 2 * kept.shape[0] * 128), BF16),
            jax.ShapeDtypeStruct(DONE, F32),
        ),
        order=order,
        inputs=2,
    )(kept, got, *order)


def side(axis, stage, cores):
    if axis == "chips":
        return (lax.axis_index("dp") // cores >> stage) & 1
    bits = bits_of(lax.axis_size("space"))
    index = lax.axis_index("space")
    return jnp.where(odd_core(cores), (index >> (bits - 1 - stage)) & 1, (index >> stage) & 1)


def halves_of(shape, axis):
    units, chips = shape[:2]
    lead = (1, 2, units // 2 * chips) if axis == "space" else (units * chips // 2, 2, 1)
    return lead + tuple(shape[2:])


def half_shape(shape, axis):
    units, chips = shape[:2]
    return ((units // 2, chips) if axis == "space" else (units, chips // 2)) + tuple(shape[2:])


def add_kernel(now, then, cores, value_ref, got_ref, *outs):
    if now is None:
        total = value_ref[...]
    else:
        total = value_ref[:, side(*now, cores)]
    total = total.reshape(got_ref.shape) + got_ref[...].astype(F32)
    if then is None:
        outs[0][...] = total.astype(BF16)
        return
    keep_ref, sent_ref = outs
    keep_ref[...] = total.reshape(keep_ref.shape)
    sent_ref[...] = keep_ref[:, 1 - side(*then, cores)].reshape(sent_ref.shape).astype(BF16)


def add_stage(value, got, now, then, cores, order=()):
    shape = got.shape
    if then is None:
        outs = jax.ShapeDtypeStruct(shape, BF16)
    else:
        outs = (
            jax.ShapeDtypeStruct(halves_of(shape, then[0]), F32),
            jax.ShapeDtypeStruct(half_shape(shape, then[0]), BF16),
        )
    return call(
        functools.partial(add_kernel, now, then, cores), outs, order=order, inputs=2
    )(value, got, *order)


def switch_kernel(stage, cores, first_ref, *refs):
    got_ref = refs[0] if len(refs) == 3 else None
    stay_ref, out_ref = refs[-2:]
    bit = side("space", stage, cores)
    sources = first_ref.shape[0]
    for part, ref in enumerate((first_ref, got_ref)):
        if ref is not None:
            for source in range(sources):
                stay_ref[part * sources + source] = ref[source, bit]
                out_ref[part * sources + source] = ref[source, 1 - bit]


def switch_stage(first, got, stage, cores, order):
    sources, targets = first.shape[:2]
    split = (sources, 2, targets // 2) + first.shape[2:]
    operands = (first.reshape(split),) + ((got.reshape(split),) if got is not None else ())
    shape = jax.ShapeDtypeStruct((sources * len(operands), targets // 2) + first.shape[2:], BF16)
    return call(
        functools.partial(switch_kernel, stage, cores),
        (shape, shape),
        order=order,
        inputs=len(operands),
    )(*operands, *order)


def gather_kernel(early_count, mine_ref, got_ref, out_ref):
    out_ref[pl.ds(0, early_count)] = mine_ref[pl.ds(0, early_count)]
    out_ref[pl.ds(early_count, early_count)] = got_ref[pl.ds(0, early_count)]
    late = mine_ref.shape[0] - early_count
    rows = pl.ds(early_count, late)
    total = mine_ref[rows].astype(F32) + got_ref[rows].astype(F32)
    out_ref[pl.ds(2 * early_count, late)] = total.astype(BF16)


def gather_stage(mine, got, early_count, order):
    shape = (mine.shape[0] + early_count,) + mine.shape[1:]
    return call(
        functools.partial(gather_kernel, early_count),
        jax.ShapeDtypeStruct(shape, BF16),
        order=order,
        inputs=2,
    )(mine, got, *order)


def join_kernel(now, cores, value_ref, got_ref, late_ref, out_ref):
    total = value_ref[:, side(*now, cores)].reshape(got_ref.shape) + got_ref[...].astype(F32)
    early = total.shape[0]
    out_ref[pl.ds(0, early)] = total.reshape((early,) + out_ref.shape[1:]).astype(BF16)
    out_ref[pl.ds(early, late_ref.shape[0])] = late_ref[...].reshape((-1,) + out_ref.shape[1:])


def join(value, got, late, now, cores, order):
    shape = (got.shape[0] + late.shape[0],) + got.shape[2:]
    return call(
        functools.partial(join_kernel, now, cores),
        jax.ShapeDtypeStruct(shape, BF16),
        order=order,
        inputs=3,
    )(value, got, late, *order)


def kernel_grad_out_kernel(space, cores, early_units, share, mine_ref, got_ref, out_ref):
    halves = out_ref.shape[-1] // 128
    count = mine_ref.shape[0]
    late_units = out_ref.shape[0] * halves - early_units
    near = share * (space // 2)

    def put(index, value):
        tap, half = divmod(index, halves)
        out_ref[tap, :, half * 128 : (half + 1) * 128] = value

    for index in range(late_units):
        row = near + index
        put(index, mine_ref[row].astype(F32) + got_ref[row].astype(F32))
    for group in range(space):
        place = relative_group(group, space, cores)
        far = place // (space // 2)
        row = (place % (space // 2)) * share
        for unit in range(share):
            index = group * share + unit
            if index < early_units:
                value = jnp.where(far == 1, got_ref[row + unit], mine_ref[row + unit])
                put(late_units + index, value.astype(F32))


def kernel_grad_out(mine, got, early_units, late_units, space, cores, co):
    taps = (early_units + late_units) * 128 // co
    share = -(-early_units // space)
    return call(
        functools.partial(kernel_grad_out_kernel, space, cores, early_units, share),
        jax.ShapeDtypeStruct((taps, mine.shape[1], co), F32),
    )(mine, got)


def store_units(product, scale, core, cores, chips, put):
    chans = product.shape[0] // 3
    co = product.shape[1]
    block = chans // (cores * chips)
    halves = co // 128
    product = product * scale
    for kw in range(3):
        for half in range(halves):
            unit = product[kw * chans : (kw + 1) * chans, half * 128 : (half + 1) * 128]
            unit = unit.reshape(chips, cores, block, 128)
            for chip in range(chips):
                first = unit[chip, 0]
                last = unit[chip, cores - 1]
                keep = jnp.where(core == 0, first, last)
                send = jnp.where(core == 0, last, first)
                put(kw * halves + half, chip, keep, send)


def kernel_grad_kernel(kds, cores, chips, scale, even_ref, odd_ref, grads_ref, *refs):
    above_ref = refs[0] if 0 in kds else None
    keep_ref, send_ref = refs[-2:]
    outs = even_ref.shape[0] // 2
    cells = even_ref.shape[1] * even_ref.shape[2]
    core = lax.axis_index("dp") % cores
    per_row = 3 * (grads_ref.shape[1] // 128)
    for place, kd in enumerate(kds):
        if kd == 0:
            planes = [2 * d - 1 for d in range(1, outs + 1)]
            rhs = [grads_ref[pl.ds(d * cells, cells), :] for d in range(1, outs)] + [above_ref[...]]
            rhs = jnp.concatenate(rhs, axis=0)
        else:
            planes = [2 * d - 1 + kd for d in range(outs)]
            rhs = grads_ref[...]
        for kh in range(3):
            lhs = [tap_rows(even_ref, odd_ref, plane, kh) for plane in planes]
            product = lax.dot_general(
                jnp.concatenate(lhs, axis=0), rhs, (((0,), (0,)), ((), ())), preferred_element_type=F32
            )

            def put(unit, chip, keep, send, base=(place * 3 + kh) * per_row):
                keep_ref[base + unit, chip] = keep
                send_ref[base + unit, chip] = send.astype(BF16)

            store_units(product, scale, core, cores, chips, put)


def kernel_grad_part(even, odd, grads, above, kds, cores, chips, scale, order=()):
    chans = even.shape[-1] // 3
    co = grads.shape[-1]
    units = len(kds) * 9 * (co // 128)
    shape = (units, chips, chans // (cores * chips), 128)
    operands = (even, odd, grads) + ((above,) if 0 in kds else ())
    return call(
        functools.partial(kernel_grad_kernel, kds, cores, chips, scale),
        (jax.ShapeDtypeStruct(shape, F32), jax.ShapeDtypeStruct(shape, BF16)),
        order=order,
        inputs=len(operands),
    )(*operands, *order)


def volume_grad_kernel(grads_ref, above_ref, kernel_ref, out_ref, done_ref, shifted, wide):
    done_ref[...] = jnp.zeros_like(done_ref)
    planes, h2, _, width, chans = out_ref.shape
    w2 = width // 2
    cells = h2 * w2
    outs = planes // 2
    co = grads_ref.shape[1]
    here, right = [], []
    for d in range(outs + 1):
        plane = grads_ref[pl.ds(d * cells, cells), :] if d < outs else above_ref[...]
        shifted[pl.ds(0, cells), :] = plane.astype(F32)
        moved = shifted[pl.ds(1, cells), :]
        column = lax.broadcasted_iota(jnp.int32, moved.shape, 0) % w2
        moved = jnp.where(column == w2 - 1, 0.0, moved).astype(BF16)
        here.append(plane)
        right.append(moved)

    def down(rows):
        return jnp.concatenate([rows[w2:], jnp.zeros((w2, co), BF16)], axis=0)

    contract = (((1,), (1,)), ((), ()))
    for plane in range(planes):
        d = plane // 2
        depth = [(1, d)] if plane % 2 == 0 else [(2, d), (0, d + 1)]
        for odd_row in range(2):
            taps = [(1, False)] if odd_row == 0 else [(2, False), (0, True)]
            both, right_only = None, None
            for kd, source in depth:
                for kh, lower in taps:
                    lhs = down(here[source]) if lower else here[source]
                    rhs = kernel_ref[kd, kh, pl.ds(1, 2)].reshape(2 * chans, co)
                    term = lax.dot_general(lhs, rhs, contract, preferred_element_type=F32)
                    both = term if both is None else both + term
                    lhs = down(right[source]) if lower else right[source]
                    term = lax.dot_general(lhs, kernel_ref[kd, kh, 0], contract, preferred_element_type=F32)
                    right_only = term if right_only is None else right_only + term
            wide[pl.ds(0, cells, stride=2), :] = both[:, :chans]
            wide[pl.ds(1, cells, stride=2), :] = both[:, chans:] + right_only
            out_ref[plane, :, odd_row] = wide[...].reshape(h2, width, chans).astype(BF16)


def volume_grad_of(grads, above, kernel, height, width, order=()):
    cells, co = grads.shape
    chans = kernel.shape[3]
    planes = 2 * cells * 4 // (height * width)
    shape = (planes, height // 2, 2, width, chans)
    return call(
        volume_grad_kernel,
        (jax.ShapeDtypeStruct(shape, BF16), jax.ShapeDtypeStruct(DONE, F32)),
        [
            pltpu.VMEM((height * width // 4 + 8, co), F32),
            pltpu.VMEM((height * width // 2, chans), F32),
        ],
        order=order,
        inputs=3,
    )(grads, above, kernel, *order)


def exchange(value, partner):
    dp, space = lax.axis_size("dp"), lax.axis_size("space")
    pairs = []
    for i in range(dp):
        for j in range(space):
            to_dp, to_space = partner(i, j)
            pairs.append((i * space + j, to_dp * space + to_space))
    return lax.ppermute(value, ("dp", "space"), pairs)


def exchange_space(value, stage, cores):
    bits = bits_of(lax.axis_size("space"))

    def partner(i, j):
        bit = bits - 1 - stage if cores == 2 and i % 2 == 1 else stage
        return i, j ^ (1 << bit)

    return exchange(value, partner)


def exchange_chips(value, bit, cores):
    return exchange(value, lambda i, j: (i ^ (cores << bit), j))


def neighbour(value, steps):
    count = lax.axis_size("space")
    first, last = (max(0, -steps), min(count, count - steps))
    return lax.ppermute(value, "space", [(source, source + steps) for source in range(first, last)])


def exchange_stage(value, axis, stage, cores):
    return exchange_space(value, stage, cores) if axis == "space" else exchange_chips(value, stage, cores)


def add_cores(keep, send, then, cores, order=()):
    if cores == 1:
        got = jnp.zeros_like(send)
    else:
        got = exchange(send, lambda i, j: (i ^ 1, j))
    return add_stage(keep, got, None, then, cores, order)


def pad_units(value, space):
    extra = -value.shape[0] % space
    return jnp.pad(value, ((0, extra),) + ((0, 0),) * (value.ndim - 1)) if extra else value


def body(volume, kernel, cotangent):
    samples, planes, height, width, ci = volume.shape
    co = kernel.shape[-1]
    assert samples == 1
    dp, space = lax.axis_size("dp"), lax.axis_size("space")
    cores = 2 if dp % 2 == 0 else 1
    chips = dp // cores
    outs = planes // 2
    cells = height * width // 4
    scale = 1.0 / math.sqrt(dp * space * samples * outs * cells)
    over_space = [("space", stage) for stage in range(bits_of(space))]
    over_chips = [("chips", stage) for stage in range(bits_of(chips))]

    share = neighbour(halo_share(volume, kernel), 1)
    preact, even, odd = partial_preact(volume, kernel)
    grads, flipped = activation(preact, share, cotangent.reshape(outs * cells, co), space, cores)
    above = neighbour(grads[:cells], -1)

    early = kernel_grad_part(even, odd, grads, None, (1, 2), cores, chips, scale)
    early_units = early[0].shape[0]
    early = [pad_units(half, space) for half in early]
    plan = over_space + over_chips
    late_plan = list(over_chips)
    switch_plan = list(over_space)
    value, sent = add_cores(*early, plan[0], cores)
    late_state = stay = moved = None
    late_units = volume_grad = None
    late_ready = None
    for place, now in enumerate(plan):
        got = exchange_stage(sent, *now, cores)
        tokens = []
        if place == 0:
            volume_grad, done = volume_grad_of(grads, above, kernel, height, width, (sent,))
            late = kernel_grad_part(even, odd, grads, above, (0,), cores, chips, scale, (done,))
            late_units = late[0].shape[0]
            tokens.append(late[0])
        elif late_ready is None:
            if late_state is None:
                then = late_plan[0] if late_plan else None
                result = add_cores(*late, then, cores, (sent,))
            else:
                then = late_plan[0] if late_plan else None
                result = add_stage(*late_state, late_now, then, cores, (sent,))
            if then is None:
                late_ready = result
                tokens.append(late_ready)
            else:
                late_now = late_plan.pop(0)
                late_state = (result[0], exchange_stage(result[1], *late_now, cores))
                tokens.append(result[1])
        if place >= len(over_space) and switch_plan:
            _, stage = switch_plan.pop(0)
            if stay is None:
                stay = flipped[None]
            stay, out = switch_stage(stay, moved, stage, cores, (sent,))
            moved = exchange_space(out, stage, cores)
            tokens.append(out)
        if place + 1 < len(plan):
            value, sent = add_stage(value, got, now, plan[place + 1], cores, tuple(tokens))
    while late_ready is None:
        then = late_plan[0] if late_plan else None
        result = add_stage(*late_state, late_now, then, cores)
        if then is None:
            late_ready = result
        else:
            late_now = late_plan.pop(0)
            late_state = (result[0], exchange_stage(result[1], *late_now, cores))

    mine = join(value, got, late_ready, plan[-1], cores, tuple(tokens))
    share_units = mine.shape[0] - late_units
    switched = None
    for step, (_, stage) in enumerate(reversed(over_space)):
        got = exchange_space(mine, stage, cores)
        order = ()
        if switched is None:
            switched, done = switched_of(stay, moved, space, cores, (mine,))
            order = (done,)
        if step + 1 < len(over_space):
            mine = gather_stage(mine, got, share_units << step, order)
    kernel_grad = kernel_grad_out(mine, got, early_units, late_units, space, cores, co)

    return (
        switched[None],
        volume_grad.reshape(volume.shape),
        kernel_grad.reshape(3, 3, 3, ci // dp, co),
    )


def solution(mesh):
    in_specs = (P("dp", "space", None, None, None), P(), P("dp", "space", None, None, None))
    out_specs = (
        P("dp", "space", None),
        P("dp", "space", None, None, None),
        P(None, None, None, "dp", None),
    )
    return jax.shard_map(body, mesh=mesh, in_specs=in_specs, out_specs=out_specs, check_vma=False)
```

```python
import functools
import math

import jax
import jax.numpy as jnp
from jax import lax
from jax.experimental import pallas as pl
from jax.experimental.pallas import tpu as pltpu
from jax.sharding import PartitionSpec as P

BF16 = jnp.bfloat16
F32 = jnp.float32
VMEM_LIMIT = 20 * 1024 * 1024
DONE = (8, 128)
PLANE_PARTS = 4
SPACER = 6 * 10**9
VMEM_WHOLE = 63 * 1024 * 1024


def call(kernel, out_shape, scratch=(), in_specs=None, limit=VMEM_LIMIT, order=(), inputs=0, flops=1000):
    extra = {} if in_specs is None else {"in_specs": in_specs}
    if order:
        whole = pl.BlockSpec(memory_space=pltpu.VMEM)
        extra["in_specs"] = [whole] * inputs + [pl.BlockSpec(memory_space=pl.ANY)] * len(order)
        inner, count = kernel, len(order)

        def kernel(*refs):
            inner(*refs[:inputs], *refs[inputs + count :])

    return pl.pallas_call(
        kernel,
        out_shape=out_shape,
        scratch_shapes=list(scratch),
        compiler_params=pltpu.CompilerParams(vmem_limit_bytes=limit),
        cost_estimate=pl.CostEstimate(flops=flops, bytes_accessed=1000, transcendentals=0),
        **extra,
    )


def spread_plane(plane, wide):
    height, width, chans = plane.shape
    cells = height * width
    half = width // 2
    wide[pl.ds(8, cells), :] = plane.reshape(cells, chans).astype(F32)
    left = wide[pl.ds(7, cells // 2, stride=2), :]
    even = wide[pl.ds(8, cells // 2, stride=2), :]
    odd = wide[pl.ds(9, cells // 2, stride=2), :]
    column = lax.broadcasted_iota(jnp.int32, left.shape, 0) % half
    left = jnp.where(column == 0, 0.0, left)
    joined = jnp.concatenate([left.astype(BF16), even.astype(BF16), odd.astype(BF16)], axis=1)
    joined = joined.reshape(height // 2, 2, half, 3 * chans)
    return joined[:, 0], joined[:, 1]


def tap_rows(even, odd, plane, kh):
    height = even.shape[1]
    picked = even[plane] if kh == 1 else odd[plane, pl.ds(0 if kh == 0 else 1, height)]
    return picked.reshape(height * even.shape[2], even.shape[3])


def bits_of(count):
    bits = count.bit_length() - 1
    assert 1 << bits == count
    return bits


def odd_core(cores):
    return lax.axis_index("dp") % cores == 1 if cores == 2 else False


def reverse_bits(value, bits):
    return sum(((value >> bit) & 1) << (bits - 1 - bit) for bit in range(bits))


def staged_place(target, space, cores):
    return jnp.where(odd_core(cores), target, reverse_bits(target, bits_of(space)))


def relative_place(source, space, cores):
    bits = bits_of(space)
    off = source ^ lax.axis_index("space")
    return jnp.where(odd_core(cores), reverse_bits(off, bits), off)


def relative_group(group, space, cores):
    bits = bits_of(space)
    index = lax.axis_index("space")
    mine = jnp.where(odd_core(cores), index, reverse_bits(index, bits))
    return group ^ mine


def halo_kernel(volume_ref, kernel_ref, share_ref, plane, weights, wide, sems):
    planes, height, width, chans = volume_ref.shape[1:]
    part = height // PLANE_PARTS
    rows = [pl.ds(index * part, part) for index in range(PLANE_PARTS)]
    copies = [
        pltpu.make_async_copy(volume_ref.at[0, planes - 1, row], plane.at[row], sems.at[index])
        for index, row in enumerate(rows)
    ]
    loads = [
        pltpu.make_async_copy(kernel_ref.at[0, kh], weights.at[kh], sems.at[PLANE_PARTS + kh])
        for kh in range(3)
    ]
    for copy in copies + loads:
        copy.start()
    for copy in copies:
        copy.wait()
    even, odd = spread_plane(plane[...], wide)
    above = jnp.concatenate([jnp.zeros_like(odd[:1]), odd[:-1]], axis=0)
    total = None
    for kh, rows in enumerate((above, even, odd)):
        loads[kh].wait()
        lhs = rows.reshape(height * width // 4, 3 * chans)
        rhs = weights[kh].reshape(3 * chans, weights.shape[-1])
        term = jnp.dot(lhs, rhs, preferred_element_type=F32)
        total = term if total is None else total + term
    share_ref[...] = total.astype(BF16)


def halo_share(volume, kernel):
    _, planes, height, width, chans = volume.shape
    co = kernel.shape[-1]
    return call(
        halo_kernel,
        jax.ShapeDtypeStruct((height * width // 4, co), BF16),
        [
            pltpu.VMEM((height, width, chans), BF16),
            pltpu.VMEM((3, 3, chans, co), BF16),
            pltpu.VMEM((height * width + 16, chans), F32),
            pltpu.SemaphoreType.DMA((PLANE_PARTS + 3,)),
        ],
        [pl.BlockSpec(memory_space=pltpu.HBM)] * 2,
        VMEM_WHOLE,
    )(volume, kernel)


def preact_kernel(volume_ref, kernel_ref, preact_ref, even_ref, odd_ref, wide):
    planes, height, width, chans = volume_ref.shape[1:]
    cells = height * width // 4
    outs = planes // 2
    for plane in range(planes):
        even, odd = spread_plane(volume_ref[0, plane], wide)
        even_ref[plane] = even
        odd_ref[plane, pl.ds(0, 1)] = jnp.zeros_like(odd[:1])
        odd_ref[plane, pl.ds(1, height // 2)] = odd
    co = kernel_ref.shape[-1]
    total = None
    for kd in (1, 2):
        for kh in range(3):
            lhs = [tap_rows(even_ref, odd_ref, 2 * d - 1 + kd, kh) for d in range(outs)]
            rhs = kernel_ref[kd, kh].reshape(3 * chans, co)
            term = jnp.dot(jnp.concatenate(lhs, axis=0), rhs, preferred_element_type=F32)
            total = term if total is None else total + term
    preact_ref[...] = total
    if outs > 1:
        total = preact_ref[pl.ds(cells, (outs - 1) * cells), :]
        for kh in range(3):
            lhs = [tap_rows(even_ref, odd_ref, 2 * d - 1, kh) for d in range(1, outs)]
            rhs = kernel_ref[0, kh].reshape(3 * chans, co)
            total += jnp.dot(jnp.concatenate(lhs, axis=0), rhs, preferred_element_type=F32)
        preact_ref[pl.ds(cells, (outs - 1) * cells), :] = total


def partial_preact(volume, kernel):
    _, planes, height, width, chans = volume.shape
    co = kernel.shape[-1]
    cells = height * width // 4
    h2, w2 = height // 2, width // 2
    return call(
        preact_kernel,
        (
            jax.ShapeDtypeStruct((planes // 2 * cells, co), F32),
            jax.ShapeDtypeStruct((planes, h2, w2, 3 * chans), BF16),
            jax.ShapeDtypeStruct((planes, h2 + 1, w2, 3 * chans), BF16),
        ),
        [pltpu.VMEM((height * width + 16, chans), F32)],
    )(volume, kernel)


def activation_kernel(space, cores, preact_ref, share_ref, cotangent_ref, grad_ref, flipped_ref):
    cells, co = share_ref.shape
    count = preact_ref.shape[0] // cells
    group = co // space
    strips = cells // 128
    for d in range(count):
        rows = pl.ds(d * cells, cells)
        value = preact_ref[rows, :]
        if d == 0:
            value = value + share_ref[...].astype(F32)
        sig = jax.nn.sigmoid(value)
        slope = sig * (1.0 + value * (1.0 - sig))
        grad_ref[rows, :] = (cotangent_ref[rows, :].astype(F32) * slope).astype(BF16)
        flipped = (value * sig).T.astype(BF16)
        for target in range(space):
            place = staged_place(target, space, cores)
            for strip in range(strips):
                flipped_ref[place, d * strips + strip] = flipped[
                    target * group : (target + 1) * group, strip * 128 : (strip + 1) * 128
                ]


def activation(preact, share, cotangent, space, cores):
    cells, co = preact.shape
    return call(
        functools.partial(activation_kernel, space, cores),
        (
            jax.ShapeDtypeStruct((cells, co), BF16),
            jax.ShapeDtypeStruct((space, cells // 128, co // space, 128), BF16),
        ),
    )(preact, share, cotangent)


def switched_kernel(space, cores, came, kept_ref, got_ref, out_ref, done_ref):
    done_ref[...] = jnp.zeros_like(done_ref)
    half = space // 2
    rows = kept_ref.shape[1]
    strips = kept_ref.shape[0] // half
    for source in range(space):
        place = relative_place(source, space, cores)
        far = place // half
        for strip in range(strips):
            column = (source * strips + strip) * 128
            row = (place % half) * strips + strip
            there = got_ref[pl.ds(pl.multiple_of(came + row * rows, rows), rows), :]
            out_ref[:, column : column + 128] = jnp.where(far == 1, there, kept_ref[row])


def switched_of(kept, got, came, space, cores, order):
    group = kept.shape[-2]
    kept = kept.reshape(-1, group, 128)
    return call(
        functools.partial(switched_kernel, space, cores, came),
        (
            jax.ShapeDtypeStruct((group, 2 * kept.shape[0] * 128), BF16),
            jax.ShapeDtypeStruct(DONE, F32),
        ),
        order=order,
        inputs=2,
    )(kept, got, *order)


def side(axis, stage, cores):
    if axis == "chips":
        return (lax.axis_index("dp") // cores >> stage) & 1
    bits = bits_of(lax.axis_size("space"))
    index = lax.axis_index("space")
    return jnp.where(odd_core(cores), (index >> (bits - 1 - stage)) & 1, (index >> stage) & 1)


def halves_of(shape, axis):
    units, chips = shape[:2]
    lead = (1, 2, units // 2 * chips) if axis == "space" else (units * chips // 2, 2, 1)
    return lead + tuple(shape[2:])


def half_shape(shape, axis):
    units, chips = shape[:2]
    return ((units // 2, chips) if axis == "space" else (units, chips // 2)) + tuple(shape[2:])


def add_kernel(now, then, cores, value_ref, *refs):
    keep_ref, sent_ref = refs[-2:]
    got = jnp.concatenate([ref[...] for ref in refs[:-2]], axis=0).astype(F32)
    total = value_ref[...] if now is None else value_ref[:, side(*now, cores)]
    total = total.reshape(got.shape) + got
    if then is None:
        keep_ref[...] = total
        sent_ref[...] = total.astype(BF16)
        return
    keep_ref[...] = total.reshape(keep_ref.shape)
    sent_ref[...] = keep_ref[:, 1 - side(*then, cores)].reshape(sent_ref.shape).astype(BF16)


def add_stage(value, got, now, then, cores, order=(), flops=1000):
    shape = (sum(piece.shape[0] for piece in got),) + got[0].shape[1:]
    if then is None:
        outs = (jax.ShapeDtypeStruct(shape, F32), jax.ShapeDtypeStruct(shape, BF16))
    else:
        outs = (
            jax.ShapeDtypeStruct(halves_of(shape, then[0]), F32),
            jax.ShapeDtypeStruct(half_shape(shape, then[0]), BF16),
        )
    return call(
        functools.partial(add_kernel, now, then, cores),
        outs,
        order=order,
        inputs=1 + len(got),
        flops=flops,
    )(value, *got, *order)


def switch_kernel(stage, cores, came, first_ref, *refs):
    stay_ref, out_ref = refs[-2:]
    refs = list(refs[:-2])
    bit = side("space", stage, cores)
    sources, _, targets, strips, rows, lanes = first_ref.shape
    half = targets * strips * rows
    if came is None:
        ahead = out_ref.shape[0] - sources * half
    else:
        ahead = out_ref.shape[0] - 2 * sources * half
    rider = refs.pop() if ahead else None
    if rider is not None:
        out_ref[pl.ds(0, ahead), :] = rider[...]
    place = ahead
    for source in range(sources):
        stay_ref[source] = first_ref[source, bit]
        out_ref[pl.ds(place, half), :] = first_ref[source, 1 - bit].reshape(half, lanes)
        place += half
    if came is not None:
        got_ref = refs[0]
        for source in range(sources):
            base = came + source * 2 * half
            mine = got_ref[pl.ds(pl.multiple_of(base + bit * half, rows), half), :]
            stay_ref[sources + source] = mine.reshape(targets, strips, rows, lanes)
            out_ref[pl.ds(place, half), :] = got_ref[
                pl.ds(pl.multiple_of(base + (1 - bit) * half, rows), half), :
            ]
            place += half


def switch_stage(first, got, came, rider, stage, cores, order):
    sources, targets, strips, rows, lanes = first.shape
    operands = (first.reshape(sources, 2, targets // 2, strips, rows, lanes),)
    total = sources * (1 if got is None else 2)
    count = total * targets // 2 * strips * rows
    if got is not None:
        operands += (got,)
    if rider is not None:
        operands += (rider.reshape(-1, lanes),)
        count += operands[-1].shape[0]
    return call(
        functools.partial(switch_kernel, stage, cores, None if got is None else came),
        (
            jax.ShapeDtypeStruct((total, targets // 2, strips, rows, lanes), BF16),
            jax.ShapeDtypeStruct((count, lanes), BF16),
        ),
        order=order,
        inputs=len(operands),
    )(*operands, *order)


def gather_kernel(early, add_late, mine_ref, got_ref, out_ref):
    late = mine_ref.shape[0] - early
    rows = pl.ds(early, late)
    out_ref[pl.ds(0, early)] = mine_ref[pl.ds(0, early)]
    out_ref[pl.ds(early, early)] = got_ref[pl.ds(0, early)]
    if add_late:
        total = mine_ref[rows].astype(F32) + got_ref[rows].astype(F32)
        out_ref[pl.ds(2 * early, late)] = total.astype(BF16)
    else:
        out_ref[pl.ds(2 * early, late)] = mine_ref[rows]
        out_ref[pl.ds(2 * early + late, late)] = got_ref[rows]


def gather_stage(mine, got, early, add_late, order=()):
    late = mine.shape[0] - early
    shape = (2 * early + (late if add_late else 2 * late),) + mine.shape[1:]
    return call(
        functools.partial(gather_kernel, early, add_late),
        jax.ShapeDtypeStruct(shape, BF16),
        order=order,
        inputs=2,
    )(mine, got, *order)


def join_kernel(now, cores, value_ref, got_ref, late_ref, out_ref):
    total = value_ref[:, side(*now, cores)].reshape(got_ref.shape) + got_ref[...].astype(F32)
    early = total.shape[0]
    out_ref[pl.ds(0, early)] = total.reshape((early,) + out_ref.shape[1:]).astype(BF16)
    out_ref[pl.ds(early, late_ref.shape[0])] = late_ref[...].reshape((-1,) + out_ref.shape[1:])


def join(value, got, late, now, cores, order):
    shape = (got.shape[0] + late.shape[0],) + got.shape[2:]
    return call(
        functools.partial(join_kernel, now, cores),
        jax.ShapeDtypeStruct(shape, BF16),
        order=order,
        inputs=3,
        flops=SPACER,
    )(value, got, late, *order)


def kernel_grad_out_kernel(space, cores, early_units, late_units, mine_ref, got_ref, out_ref):
    halves = out_ref.shape[-1] // 128
    half = space // 2
    share = -(-early_units // space)
    late_share = late_units if space == 2 else -(-late_units // half)

    def put(index, value):
        tap, part = divmod(index, halves)
        out_ref[tap, :, part * 128 : (part + 1) * 128] = value

    for group in range(space):
        place = relative_group(group, space, cores)
        far, row = place // half, (place % half) * share
        for unit in range(share):
            index = group * share + unit
            if index < early_units:
                value = jnp.where(far == 1, got_ref[row + unit], mine_ref[row + unit])
                put(late_units + index, value.astype(F32))
    base = half * share
    if space == 2:
        for unit in range(late_units):
            put(unit, mine_ref[base + unit].astype(F32) + got_ref[base + unit].astype(F32))
        return
    inner = half // 2
    for group in range(half):
        place = relative_group(2 * group, space, cores) // 2
        far, row = place // inner, base + (place % inner) * late_share
        for unit in range(late_share):
            index = group * late_share + unit
            if index < late_units:
                value = jnp.where(far == 1, got_ref[row + unit], mine_ref[row + unit])
                put(index, value.astype(F32))


def kernel_grad_out(mine, got, early_units, late_units, space, cores, co):
    taps = (early_units + late_units) * 128 // co
    return call(
        functools.partial(kernel_grad_out_kernel, space, cores, early_units, late_units),
        jax.ShapeDtypeStruct((taps, mine.shape[1], co), F32),
    )(mine, got)


def store_units(product, scale, core, cores, chips, put):
    chans = product.shape[0] // 3
    co = product.shape[1]
    block = chans // (cores * chips)
    halves = co // 128
    product = product * scale
    for kw in range(3):
        for half in range(halves):
            unit = product[kw * chans : (kw + 1) * chans, half * 128 : (half + 1) * 128]
            unit = unit.reshape(chips, cores, block, 128)
            for chip in range(chips):
                first = unit[chip, 0]
                last = unit[chip, cores - 1]
                keep = jnp.where(core == 0, first, last)
                send = jnp.where(core == 0, last, first)
                put(kw * halves + half, chip, keep, send)


def kernel_grad_kernel(kds, cores, chips, scale, parts, even_ref, odd_ref, grads_ref, *refs):
    above_ref = refs[0] if 0 in kds else None
    keep_ref, send_refs = refs[-1 - parts], refs[-parts:]
    size = send_refs[0].shape[0]
    outs = even_ref.shape[0] // 2
    cells = even_ref.shape[1] * even_ref.shape[2]
    core = lax.axis_index("dp") % cores
    per_row = 3 * (grads_ref.shape[1] // 128)
    for unit in range(len(kds) * 3 * per_row, keep_ref.shape[0]):
        keep_ref[unit] = jnp.zeros(keep_ref.shape[1:], F32)
        send_refs[unit // size][unit % size] = jnp.zeros(keep_ref.shape[1:], BF16)
    for place, kd in enumerate(kds):
        if kd == 0:
            planes = [2 * d - 1 for d in range(1, outs + 1)]
            rhs = [grads_ref[pl.ds(d * cells, cells), :] for d in range(1, outs)] + [above_ref[...]]
            rhs = jnp.concatenate(rhs, axis=0)
        else:
            planes = [2 * d - 1 + kd for d in range(outs)]
            rhs = grads_ref[...]
        for kh in range(3):
            lhs = [tap_rows(even_ref, odd_ref, plane, kh) for plane in planes]
            product = lax.dot_general(
                jnp.concatenate(lhs, axis=0), rhs, (((0,), (0,)), ((), ())), preferred_element_type=F32
            )

            def put(unit, chip, keep, send, base=(place * 3 + kh) * per_row):
                keep_ref[base + unit, chip] = keep
                send_refs[(base + unit) // size][(base + unit) % size, chip] = send.astype(BF16)

            store_units(product, scale, core, cores, chips, put)


def kernel_grad_part(even, odd, grads, above, kds, cores, chips, scale, multiple, parts=1, order=()):
    chans = even.shape[-1] // 3
    co = grads.shape[-1]
    units = len(kds) * 9 * (co // 128)
    units += -units % math.lcm(multiple, parts)
    shape = (units, chips, chans // (cores * chips), 128)
    operands = (even, odd, grads) + ((above,) if 0 in kds else ())
    return call(
        functools.partial(kernel_grad_kernel, kds, cores, chips, scale, parts),
        (jax.ShapeDtypeStruct(shape, F32),)
        + (jax.ShapeDtypeStruct((units // parts,) + shape[1:], BF16),) * parts,
        order=order,
        inputs=len(operands),
    )(*operands, *order)


def volume_grad_kernel(grads_ref, above_ref, kernel_ref, out_ref, done_ref, shifted, wide):
    done_ref[...] = jnp.zeros_like(done_ref)
    planes, h2, _, width, chans = out_ref.shape
    w2 = width // 2
    cells = h2 * w2
    outs = planes // 2
    co = grads_ref.shape[1]
    here, right = [], []
    for d in range(outs + 1):
        plane = grads_ref[pl.ds(d * cells, cells), :] if d < outs else above_ref[...]
        shifted[pl.ds(0, cells), :] = plane.astype(F32)
        moved = shifted[pl.ds(1, cells), :]
        column = lax.broadcasted_iota(jnp.int32, moved.shape, 0) % w2
        moved = jnp.where(column == w2 - 1, 0.0, moved).astype(BF16)
        here.append(plane)
        right.append(moved)

    def down(rows):
        return jnp.concatenate([rows[w2:], jnp.zeros((w2, co), BF16)], axis=0)

    contract = (((1,), (1,)), ((), ()))
    for plane in range(planes):
        d = plane // 2
        depth = [(1, d)] if plane % 2 == 0 else [(2, d), (0, d + 1)]
        for odd_row in range(2):
            taps = [(1, False)] if odd_row == 0 else [(2, False), (0, True)]
            both, right_only = None, None
            for kd, source in depth:
                for kh, lower in taps:
                    lhs = down(here[source]) if lower else here[source]
                    rhs = kernel_ref[kd, kh, pl.ds(1, 2)].reshape(2 * chans, co)
                    term = lax.dot_general(lhs, rhs, contract, preferred_element_type=F32)
                    both = term if both is None else both + term
                    lhs = down(right[source]) if lower else right[source]
                    term = lax.dot_general(lhs, kernel_ref[kd, kh, 0], contract, preferred_element_type=F32)
                    right_only = term if right_only is None else right_only + term
            wide[pl.ds(0, cells, stride=2), :] = both[:, :chans]
            wide[pl.ds(1, cells, stride=2), :] = both[:, chans:] + right_only
            out_ref[plane, :, odd_row] = wide[...].reshape(h2, width, chans).astype(BF16)


def volume_grad_of(grads, above, kernel, height, width, order=()):
    cells, co = grads.shape
    chans = kernel.shape[3]
    planes = 2 * cells * 4 // (height * width)
    shape = (planes, height // 2, 2, width, chans)
    return call(
        volume_grad_kernel,
        (jax.ShapeDtypeStruct(shape, BF16), jax.ShapeDtypeStruct(DONE, F32)),
        [
            pltpu.VMEM((height * width // 4 + 8, co), F32),
            pltpu.VMEM((height * width // 2, chans), F32),
        ],
        order=order,
        inputs=3,
    )(grads, above, kernel, *order)


def exchange(value, partner):
    dp, space = lax.axis_size("dp"), lax.axis_size("space")
    pairs = []
    for i in range(dp):
        for j in range(space):
            to_dp, to_space = partner(i, j)
            pairs.append((i * space + j, to_dp * space + to_space))
    return lax.ppermute(value, ("dp", "space"), pairs)


def exchange_space(value, stage, cores):
    bits = bits_of(lax.axis_size("space"))

    def partner(i, j):
        bit = bits - 1 - stage if cores == 2 and i % 2 == 1 else stage
        return i, j ^ (1 << bit)

    return exchange(value, partner)


def exchange_chips(value, bit, cores):
    return exchange(value, lambda i, j: (i ^ (cores << bit), j))


def neighbour(value, steps):
    count = lax.axis_size("space")
    first, last = (max(0, -steps), min(count, count - steps))
    return lax.ppermute(value, "space", [(source, source + steps) for source in range(first, last)])


def exchange_stage(value, axis, stage, cores):
    return exchange_space(value, stage, cores) if axis == "space" else exchange_chips(value, stage, cores)


def add_cores(keep, sends, then, cores, order=()):
    got = tuple(exchange(send, lambda i, j: (i ^ 1, j)) if cores == 2 else 0 * send for send in sends)
    return add_stage(keep, got, None, then, cores, order)


def body(volume, kernel, cotangent):
    samples, planes, height, width, ci = volume.shape
    co = kernel.shape[-1]
    assert samples == 1
    dp, space = lax.axis_size("dp"), lax.axis_size("space")
    cores = 2 if dp % 2 == 0 else 1
    chips = dp // cores
    outs = planes // 2
    cells = height * width // 4
    scale = 1.0 / math.sqrt(dp * space * samples * outs * cells)
    over_space = [("space", stage) for stage in range(bits_of(space))]
    over_chips = [("chips", stage) for stage in range(bits_of(chips))]

    share = neighbour(halo_share(volume, kernel), 1)
    preact, even, odd = partial_preact(volume, kernel)
    grads, flipped = activation(preact, share, cotangent.reshape(outs * cells, co), space, cores)
    above = neighbour(grads[:cells], -1)

    early = kernel_grad_part(even, odd, grads, None, (1, 2), cores, chips, scale, space)
    early_units, late_units = 18 * (co // 128), 9 * (co // 128)
    plan = over_space + over_chips
    late_plan = over_chips + over_space[:-1]
    switch_plan = list(over_space)
    value, sent = add_cores(early[0], early[1:], plan[0], cores)
    stay, moved, came = flipped[None], None, 0
    late_now = late_value = late_got = late_half = None
    for place, now in enumerate(plan):
        got = exchange_stage(sent, *now, cores)
        tokens = []
        if place == 0:
            late = kernel_grad_part(even, odd, grads, above, (0,), cores, chips, scale, space // 2, 2, (sent,))
            volume_grad, done = volume_grad_of(grads, above, kernel, height, width, (late[1],))
            late_value, late_sent = add_cores(late[0], late[1:], late_plan[0], cores, (done,))
        elif late_now is not None:
            then = late_plan[0] if late_plan else None
            late_value, late_sent = add_stage(late_value, late_got, late_now, then, cores, (sent,))
        if late_plan and late_plan[0][0] == "chips":
            late_now = late_plan.pop(0)
            late_got = (exchange_stage(late_sent, *late_now, cores),)
            tokens.append(late_sent)
        elif late_plan or switch_plan:
            rider = None
            if late_plan:
                late_now = late_plan.pop(0)
                rider = late_sent
            elif late_now is not None:
                late_now, late_half = None, late_sent
            _, stage = switch_plan.pop(0)
            stay, out = switch_stage(stay, moved, came, rider, stage, cores, (sent,))
            moved = exchange_space(out, stage, cores)
            came = 0
            if rider is not None:
                came = rider.size // rider.shape[-1]
                late_got = (moved[:came].reshape(rider.shape),)
            tokens.append(out)
        if place + 1 < len(plan):
            weight = SPACER if place >= len(over_space) else 1000
            value, sent = add_stage(value, (got,), now, plan[place + 1], cores, tuple(tokens), weight)
    if late_half is None:
        late_half = add_stage(late_value, late_got, late_now, None, cores)[1]

    mine = join(value, got, late_half, plan[-1], cores, tuple(tokens))
    early_rows = mine.shape[0] - late_half.shape[0]
    switched = None
    for step, (_, stage) in enumerate(reversed(over_space)):
        got = exchange_space(mine, stage, cores)
        order = ()
        if switched is None:
            switched, done = switched_of(stay, moved, came, space, cores, (mine,))
            order = (done,)
        if step + 1 < len(over_space):
            mine = gather_stage(mine, got, early_rows << step, step == 0, order)
    kernel_grad = kernel_grad_out(mine, got, early_units, late_units, space, cores, co)

    return (
        switched[None],
        volume_grad.reshape(volume.shape),
        kernel_grad.reshape(3, 3, 3, ci // dp, co),
    )


def solution(mesh):
    in_specs = (P("dp", "space", None, None, None), P(), P("dp", "space", None, None, None))
    out_specs = (
        P("dp", "space", None),
        P("dp", "space", None, None, None),
        P(None, None, None, "dp", None),
    )
    return jax.shard_map(body, mesh=mesh, in_specs=in_specs, out_specs=out_specs, check_vma=False)
```

```python
import functools
import math

import jax
import jax.numpy as jnp
from jax import lax
from jax.experimental import pallas as pl
from jax.experimental.pallas import tpu as pltpu
from jax.sharding import PartitionSpec as P

BF16 = jnp.bfloat16
F32 = jnp.float32
VMEM_LIMIT = 20 * 1024 * 1024
DONE = (8, 128)
PLANE_PARTS = 1
SPACER = 6 * 10**9
VMEM_WHOLE = 60 * 1024 * 1024


def call(kernel, out_shape, scratch=(), in_specs=None, limit=VMEM_LIMIT, order=(), inputs=0, flops=1000):
    extra = {} if in_specs is None else {"in_specs": in_specs}
    if order:
        whole = pl.BlockSpec(memory_space=pltpu.VMEM)
        extra["in_specs"] = [whole] * inputs + [pl.BlockSpec(memory_space=pl.ANY)] * len(order)
        inner, count = kernel, len(order)

        def kernel(*refs):
            inner(*refs[:inputs], *refs[inputs + count :])

    return pl.pallas_call(
        kernel,
        out_shape=out_shape,
        scratch_shapes=list(scratch),
        compiler_params=pltpu.CompilerParams(vmem_limit_bytes=limit),
        cost_estimate=pl.CostEstimate(flops=flops, bytes_accessed=1000, transcendentals=0),
        **extra,
    )


def spread_plane(plane, wide):
    height, width, chans = plane.shape
    cells = height * width
    half = width // 2
    wide[pl.ds(8, cells), :] = plane.reshape(cells, chans).astype(F32)
    left = wide[pl.ds(7, cells // 2, stride=2), :]
    even = wide[pl.ds(8, cells // 2, stride=2), :]
    odd = wide[pl.ds(9, cells // 2, stride=2), :]
    column = lax.broadcasted_iota(jnp.int32, left.shape, 0) % half
    left = jnp.where(column == 0, 0.0, left)
    joined = jnp.concatenate([left.astype(BF16), even.astype(BF16), odd.astype(BF16)], axis=1)
    joined = joined.reshape(height // 2, 2, half, 3 * chans)
    return joined[:, 0], joined[:, 1]


def tap_rows(even, odd, plane, kh):
    height = even.shape[1]
    picked = even[plane] if kh == 1 else odd[plane, pl.ds(0 if kh == 0 else 1, height)]
    return picked.reshape(height * even.shape[2], even.shape[3])


def bits_of(count):
    bits = count.bit_length() - 1
    assert 1 << bits == count
    return bits


def odd_core(cores):
    return lax.axis_index("dp") % cores == 1 if cores == 2 else False


def reverse_bits(value, bits):
    return sum(((value >> bit) & 1) << (bits - 1 - bit) for bit in range(bits))


def staged_place(target, space, cores):
    return jnp.where(odd_core(cores), target, reverse_bits(target, bits_of(space)))


def relative_place(source, space, cores):
    bits = bits_of(space)
    off = source ^ lax.axis_index("space")
    return jnp.where(odd_core(cores), reverse_bits(off, bits), off)


def relative_group(group, space, cores):
    bits = bits_of(space)
    index = lax.axis_index("space")
    mine = jnp.where(odd_core(cores), index, reverse_bits(index, bits))
    return group ^ mine


def halo_kernel(volume_ref, kernel_ref, share_ref, plane, weights, wide, sems):
    planes, height, width, chans = volume_ref.shape[1:]
    part = height // PLANE_PARTS
    rows = [pl.ds(index * part, part) for index in range(PLANE_PARTS)]
    copies = [
        pltpu.make_async_copy(volume_ref.at[0, planes - 1, row], plane.at[row], sems.at[index])
        for index, row in enumerate(rows)
    ]
    loads = [
        pltpu.make_async_copy(kernel_ref.at[0, kh], weights.at[kh], sems.at[PLANE_PARTS + kh])
        for kh in range(3)
    ]
    for copy in copies + loads:
        copy.start()
    for copy in copies:
        copy.wait()
    even, odd = spread_plane(plane[...], wide)
    above = jnp.concatenate([jnp.zeros_like(odd[:1]), odd[:-1]], axis=0)
    total = None
    for kh, rows in enumerate((above, even, odd)):
        loads[kh].wait()
        lhs = rows.reshape(height * width // 4, 3 * chans)
        rhs = weights[kh].reshape(3 * chans, weights.shape[-1])
        term = jnp.dot(lhs, rhs, preferred_element_type=F32)
        total = term if total is None else total + term
    share_ref[...] = total.astype(BF16)


def halo_share(volume, kernel):
    _, planes, height, width, chans = volume.shape
    co = kernel.shape[-1]
    return call(
        halo_kernel,
        jax.ShapeDtypeStruct((height * width // 4, co), BF16),
        [
            pltpu.VMEM((height, width, chans), BF16),
            pltpu.VMEM((3, 3, chans, co), BF16),
            pltpu.VMEM((height * width + 16, chans), F32),
            pltpu.SemaphoreType.DMA((PLANE_PARTS + 3,)),
        ],
        [pl.BlockSpec(memory_space=pltpu.HBM)] * 2,
        VMEM_WHOLE,
    )(volume, kernel)


def preact_kernel(volume_ref, kernel_ref, preact_ref, even_ref, odd_ref, wide):
    planes, height, width, chans = volume_ref.shape[1:]
    cells = height * width // 4
    outs = planes // 2
    for plane in range(planes):
        even, odd = spread_plane(volume_ref[0, plane], wide)
        even_ref[plane] = even
        odd_ref[plane, pl.ds(0, 1)] = jnp.zeros_like(odd[:1])
        odd_ref[plane, pl.ds(1, height // 2)] = odd
    co = kernel_ref.shape[-1]
    total = None
    for kd in (1, 2):
        for kh in range(3):
            lhs = [tap_rows(even_ref, odd_ref, 2 * d - 1 + kd, kh) for d in range(outs)]
            rhs = kernel_ref[kd, kh].reshape(3 * chans, co)
            term = jnp.dot(jnp.concatenate(lhs, axis=0), rhs, preferred_element_type=F32)
            total = term if total is None else total + term
    preact_ref[...] = total
    if outs > 1:
        total = preact_ref[pl.ds(cells, (outs - 1) * cells), :]
        for kh in range(3):
            lhs = [tap_rows(even_ref, odd_ref, 2 * d - 1, kh) for d in range(1, outs)]
            rhs = kernel_ref[0, kh].reshape(3 * chans, co)
            total += jnp.dot(jnp.concatenate(lhs, axis=0), rhs, preferred_element_type=F32)
        preact_ref[pl.ds(cells, (outs - 1) * cells), :] = total


def partial_preact(volume, kernel):
    _, planes, height, width, chans = volume.shape
    co = kernel.shape[-1]
    cells = height * width // 4
    h2, w2 = height // 2, width // 2
    return call(
        preact_kernel,
        (
            jax.ShapeDtypeStruct((planes // 2 * cells, co), F32),
            jax.ShapeDtypeStruct((planes, h2, w2, 3 * chans), BF16),
            jax.ShapeDtypeStruct((planes, h2 + 1, w2, 3 * chans), BF16),
        ),
        [pltpu.VMEM((height * width + 16, chans), F32)],
    )(volume, kernel)


def activation_kernel(space, cores, preact_ref, share_ref, cotangent_ref, grad_ref, flipped_ref):
    cells, co = share_ref.shape
    count = preact_ref.shape[0] // cells
    group = co // space
    strips = cells // 128
    for d in range(count):
        rows = pl.ds(d * cells, cells)
        value = preact_ref[rows, :]
        if d == 0:
            value = value + share_ref[...].astype(F32)
        sig = jax.nn.sigmoid(value)
        slope = sig * (1.0 + value * (1.0 - sig))
        grad_ref[rows, :] = (cotangent_ref[rows, :].astype(F32) * slope).astype(BF16)
        flipped = (value * sig).T.astype(BF16)
        for target in range(space):
            place = staged_place(target, space, cores)
            for strip in range(strips):
                flipped_ref[place, d * strips + strip] = flipped[
                    target * group : (target + 1) * group, strip * 128 : (strip + 1) * 128
                ]


def activation(preact, share, cotangent, space, cores):
    cells, co = preact.shape
    return call(
        functools.partial(activation_kernel, space, cores),
        (
            jax.ShapeDtypeStruct((cells, co), BF16),
            jax.ShapeDtypeStruct((space, cells // 128, co // space, 128), BF16),
        ),
    )(preact, share, cotangent)


def switched_kernel(space, cores, came, kept_ref, got_ref, out_ref, done_ref):
    done_ref[...] = jnp.zeros_like(done_ref)
    half = space // 2
    rows = kept_ref.shape[1]
    strips = kept_ref.shape[0] // half
    for source in range(space):
        place = relative_place(source, space, cores)
        far = place // half
        for strip in range(strips):
            column = (source * strips + strip) * 128
            row = (place % half) * strips + strip
            there = got_ref[pl.ds(pl.multiple_of(came + row * rows, rows), rows), :]
            out_ref[:, column : column + 128] = jnp.where(far == 1, there, kept_ref[row])


def switched_of(kept, got, came, space, cores, order):
    group = kept.shape[-2]
    kept = kept.reshape(-1, group, 128)
    return call(
        functools.partial(switched_kernel, space, cores, came),
        (
            jax.ShapeDtypeStruct((group, 2 * kept.shape[0] * 128), BF16),
            jax.ShapeDtypeStruct(DONE, F32),
        ),
        order=order,
        inputs=2,
    )(kept, got, *order)


def side(axis, stage, cores):
    if axis == "chips":
        return (lax.axis_index("dp") // cores >> stage) & 1
    bits = bits_of(lax.axis_size("space"))
    index = lax.axis_index("space")
    return jnp.where(odd_core(cores), (index >> (bits - 1 - stage)) & 1, (index >> stage) & 1)


def halves_of(shape, axis):
    units, chips = shape[:2]
    lead = (1, 2, units // 2 * chips) if axis == "space" else (units * chips // 2, 2, 1)
    return lead + tuple(shape[2:])


def half_shape(shape, axis):
    units, chips = shape[:2]
    return ((units // 2, chips) if axis == "space" else (units, chips // 2)) + tuple(shape[2:])


def add_kernel(now, then, cores, value_ref, *refs):
    outs = 1 if then is None else 2
    got = jnp.concatenate([ref[...] for ref in refs[:-outs]], axis=0).astype(F32)
    total = value_ref[...] if now is None else value_ref[:, side(*now, cores)]
    total = total.reshape(got.shape) + got
    if then is None:
        refs[-1][...] = total.astype(BF16)
        return
    keep_ref, sent_ref = refs[-2:]
    keep_ref[...] = total.reshape(keep_ref.shape)
    sent_ref[...] = keep_ref[:, 1 - side(*then, cores)].reshape(sent_ref.shape).astype(BF16)


def add_stage(value, got, now, then, cores, order=()):
    shape = (sum(piece.shape[0] for piece in got),) + got[0].shape[1:]
    if then is None:
        outs = jax.ShapeDtypeStruct(shape, BF16)
    else:
        outs = (
            jax.ShapeDtypeStruct(halves_of(shape, then[0]), F32),
            jax.ShapeDtypeStruct(half_shape(shape, then[0]), BF16),
        )
    return call(
        functools.partial(add_kernel, now, then, cores),
        outs,
        order=order,
        inputs=1 + len(got),
    )(value, *got, *order)


def switch_kernel(stage, cores, came, first_ref, *refs):
    stay_ref, out_ref = refs[-2:]
    refs = list(refs[:-2])
    bit = side("space", stage, cores)
    sources, _, targets, strips, rows, lanes = first_ref.shape
    half = targets * strips * rows
    if came is None:
        ahead = out_ref.shape[0] - sources * half
    else:
        ahead = out_ref.shape[0] - 2 * sources * half
    rider = refs.pop() if ahead else None
    if rider is not None:
        out_ref[pl.ds(0, ahead), :] = rider[...]
    place = ahead
    for source in range(sources):
        stay_ref[source] = first_ref[source, bit]
        out_ref[pl.ds(place, half), :] = first_ref[source, 1 - bit].reshape(half, lanes)
        place += half
    if came is not None:
        got_ref = refs[0]
        for source in range(sources):
            base = came + source * 2 * half
            mine = got_ref[pl.ds(pl.multiple_of(base + bit * half, rows), half), :]
            stay_ref[sources + source] = mine.reshape(targets, strips, rows, lanes)
            out_ref[pl.ds(place, half), :] = got_ref[
                pl.ds(pl.multiple_of(base + (1 - bit) * half, rows), half), :
            ]
            place += half


def switch_stage(first, got, came, rider, stage, cores, order):
    sources, targets, strips, rows, lanes = first.shape
    operands = (first.reshape(sources, 2, targets // 2, strips, rows, lanes),)
    total = sources * (1 if got is None else 2)
    count = total * targets // 2 * strips * rows
    if got is not None:
        operands += (got,)
    if rider is not None:
        operands += (rider.reshape(-1, lanes),)
        count += operands[-1].shape[0]
    return call(
        functools.partial(switch_kernel, stage, cores, None if got is None else came),
        (
            jax.ShapeDtypeStruct((total, targets // 2, strips, rows, lanes), BF16),
            jax.ShapeDtypeStruct((count, lanes), BF16),
        ),
        order=order,
        inputs=len(operands),
    )(*operands, *order)


def gather_kernel(early, mine_ref, got_ref, out_ref):
    rows = pl.ds(early, mine_ref.shape[0] - early)
    out_ref[pl.ds(0, early)] = mine_ref[pl.ds(0, early)]
    out_ref[pl.ds(early, early)] = got_ref[pl.ds(0, early)]
    total = mine_ref[rows].astype(F32) + got_ref[rows].astype(F32)
    out_ref[pl.ds(2 * early, total.shape[0])] = total.astype(BF16)


def gather_stage(mine, got, early, order=()):
    return call(
        functools.partial(gather_kernel, early),
        jax.ShapeDtypeStruct((mine.shape[0] + early,) + mine.shape[1:], BF16),
        order=order,
        inputs=2,
    )(mine, got, *order)


def join_kernel(now, cores, value_ref, got_ref, late_ref, out_ref):
    total = value_ref[:, side(*now, cores)].reshape(got_ref.shape) + got_ref[...].astype(F32)
    early = total.shape[0]
    out_ref[pl.ds(0, early)] = total.reshape((early,) + out_ref.shape[1:]).astype(BF16)
    out_ref[pl.ds(early, late_ref.shape[0])] = late_ref[...].reshape((-1,) + out_ref.shape[1:])


def join(value, got, late, now, cores, order):
    shape = (got.shape[0] + late.shape[0],) + got.shape[2:]
    return call(
        functools.partial(join_kernel, now, cores),
        jax.ShapeDtypeStruct(shape, BF16),
        order=order,
        inputs=3,
        flops=SPACER,
    )(value, got, late, *order)


def kernel_grad_out_kernel(space, cores, early_units, late_units, mine_ref, got_ref, out_ref):
    halves = out_ref.shape[-1] // 128
    half = space // 2
    share = -(-early_units // space)

    def put(index, value):
        tap, part = divmod(index, halves)
        out_ref[tap, :, part * 128 : (part + 1) * 128] = value

    for unit in range(late_units):
        row = half * share + unit
        put(unit, mine_ref[row].astype(F32) + got_ref[row].astype(F32))
    for group in range(space):
        place = relative_group(group, space, cores)
        far, row = place // half, (place % half) * share
        for unit in range(share):
            index = group * share + unit
            if index < early_units:
                value = jnp.where(far == 1, got_ref[row + unit], mine_ref[row + unit])
                put(late_units + index, value.astype(F32))


def kernel_grad_out(mine, got, early_units, late_units, space, cores, co, order):
    taps = (early_units + late_units) * 128 // co
    return call(
        functools.partial(kernel_grad_out_kernel, space, cores, early_units, late_units),
        jax.ShapeDtypeStruct((taps, mine.shape[1], co), F32),
        order=order,
        inputs=2,
    )(mine, got, *order)


def store_units(product, scale, core, cores, chips, put):
    chans = product.shape[0] // 3
    co = product.shape[1]
    block = chans // (cores * chips)
    halves = co // 128
    product = product * scale
    for kw in range(3):
        for half in range(halves):
            unit = product[kw * chans : (kw + 1) * chans, half * 128 : (half + 1) * 128]
            unit = unit.reshape(chips, cores, block, 128)
            for chip in range(chips):
                first = unit[chip, 0]
                last = unit[chip, cores - 1]
                keep = jnp.where(core == 0, first, last)
                send = jnp.where(core == 0, last, first)
                put(kw * halves + half, chip, keep, send)


def kernel_grad_kernel(kds, cores, chips, scale, parts, even_ref, odd_ref, grads_ref, *refs):
    above_ref = refs[0] if 0 in kds else None
    keep_ref, send_refs = refs[-1 - parts], refs[-parts:]
    size = send_refs[0].shape[0]
    outs = even_ref.shape[0] // 2
    cells = even_ref.shape[1] * even_ref.shape[2]
    core = lax.axis_index("dp") % cores
    per_row = 3 * (grads_ref.shape[1] // 128)
    for unit in range(len(kds) * 3 * per_row, keep_ref.shape[0]):
        keep_ref[unit] = jnp.zeros(keep_ref.shape[1:], F32)
        send_refs[unit // size][unit % size] = jnp.zeros(keep_ref.shape[1:], BF16)
    for place, kd in enumerate(kds):
        if kd == 0:
            planes = [2 * d - 1 for d in range(1, outs + 1)]
            rhs = [grads_ref[pl.ds(d * cells, cells), :] for d in range(1, outs)] + [above_ref[...]]
            rhs = jnp.concatenate(rhs, axis=0)
        else:
            planes = [2 * d - 1 + kd for d in range(outs)]
            rhs = grads_ref[...]
        for kh in range(3):
            lhs = [tap_rows(even_ref, odd_ref, plane, kh) for plane in planes]
            product = lax.dot_general(
                jnp.concatenate(lhs, axis=0), rhs, (((0,), (0,)), ((), ())), preferred_element_type=F32
            )

            def put(unit, chip, keep, send, base=(place * 3 + kh) * per_row):
                keep_ref[base + unit, chip] = keep
                send_refs[(base + unit) // size][(base + unit) % size, chip] = send.astype(BF16)

            store_units(product, scale, core, cores, chips, put)


def kernel_grad_part(even, odd, grads, above, kds, cores, chips, scale, multiple, parts=1, order=()):
    chans = even.shape[-1] // 3
    co = grads.shape[-1]
    units = len(kds) * 9 * (co // 128)
    units += -units % math.lcm(multiple, parts)
    shape = (units, chips, chans // (cores * chips), 128)
    operands = (even, odd, grads) + ((above,) if 0 in kds else ())
    return call(
        functools.partial(kernel_grad_kernel, kds, cores, chips, scale, parts),
        (jax.ShapeDtypeStruct(shape, F32),)
        + (jax.ShapeDtypeStruct((units // parts,) + shape[1:], BF16),) * parts,
        order=order,
        inputs=len(operands),
    )(*operands, *order)


def volume_grad_kernel(grads_ref, above_ref, kernel_ref, out_ref, done_ref, shifted, wide):
    done_ref[...] = jnp.zeros_like(done_ref)
    planes, h2, _, width, chans = out_ref.shape
    w2 = width // 2
    cells = h2 * w2
    outs = planes // 2
    co = grads_ref.shape[1]
    here, right = [], []
    for d in range(outs + 1):
        plane = grads_ref[pl.ds(d * cells, cells), :] if d < outs else above_ref[...]
        shifted[pl.ds(0, cells), :] = plane.astype(F32)
        moved = shifted[pl.ds(1, cells), :]
        column = lax.broadcasted_iota(jnp.int32, moved.shape, 0) % w2
        moved = jnp.where(column == w2 - 1, 0.0, moved).astype(BF16)
        here.append(plane)
        right.append(moved)

    def down(rows):
        return jnp.concatenate([rows[w2:], jnp.zeros((w2, co), BF16)], axis=0)

    contract = (((1,), (1,)), ((), ()))
    for plane in range(planes):
        d = plane // 2
        depth = [(1, d)] if plane % 2 == 0 else [(2, d), (0, d + 1)]
        for odd_row in range(2):
            taps = [(1, False)] if odd_row == 0 else [(2, False), (0, True)]
            both, right_only = None, None
            for kd, source in depth:
                for kh, lower in taps:
                    lhs = down(here[source]) if lower else here[source]
                    rhs = kernel_ref[kd, kh, pl.ds(1, 2)].reshape(2 * chans, co)
                    term = lax.dot_general(lhs, rhs, contract, preferred_element_type=F32)
                    both = term if both is None else both + term
                    lhs = down(right[source]) if lower else right[source]
                    term = lax.dot_general(lhs, kernel_ref[kd, kh, 0], contract, preferred_element_type=F32)
                    right_only = term if right_only is None else right_only + term
            wide[pl.ds(0, cells, stride=2), :] = both[:, :chans]
            wide[pl.ds(1, cells, stride=2), :] = both[:, chans:] + right_only
            out_ref[plane, :, odd_row] = wide[...].reshape(h2, width, chans).astype(BF16)


def volume_grad_of(grads, above, kernel, height, width, order=()):
    cells, co = grads.shape
    chans = kernel.shape[3]
    planes = 2 * cells * 4 // (height * width)
    shape = (planes, height // 2, 2, width, chans)
    return call(
        volume_grad_kernel,
        (jax.ShapeDtypeStruct(shape, BF16), jax.ShapeDtypeStruct(DONE, F32)),
        [
            pltpu.VMEM((height * width // 4 + 8, co), F32),
            pltpu.VMEM((height * width // 2, chans), F32),
        ],
        order=order,
        inputs=3,
    )(grads, above, kernel, *order)


def exchange(value, partner):
    dp, space = lax.axis_size("dp"), lax.axis_size("space")
    pairs = []
    for i in range(dp):
        for j in range(space):
            to_dp, to_space = partner(i, j)
            pairs.append((i * space + j, to_dp * space + to_space))
    return lax.ppermute(value, ("dp", "space"), pairs)


def exchange_space(value, stage, cores):
    bits = bits_of(lax.axis_size("space"))

    def partner(i, j):
        bit = bits - 1 - stage if cores == 2 and i % 2 == 1 else stage
        return i, j ^ (1 << bit)

    return exchange(value, partner)


def exchange_chips(value, bit, cores):
    return exchange(value, lambda i, j: (i ^ (cores << bit), j))


def neighbour(value, steps):
    count = lax.axis_size("space")
    first, last = (max(0, -steps), min(count, count - steps))
    return lax.ppermute(value, "space", [(source, source + steps) for source in range(first, last)])


def exchange_stage(value, axis, stage, cores):
    return exchange_space(value, stage, cores) if axis == "space" else exchange_chips(value, stage, cores)


def add_cores(keep, sends, then, cores, order=()):
    got = tuple(exchange(send, lambda i, j: (i ^ 1, j)) if cores == 2 else 0 * send for send in sends)
    return add_stage(keep, got, None, then, cores, order)


def body(volume, kernel, cotangent):
    samples, planes, height, width, ci = volume.shape
    co = kernel.shape[-1]
    assert samples == 1
    dp, space = lax.axis_size("dp"), lax.axis_size("space")
    cores = 2 if dp % 2 == 0 else 1
    chips = dp // cores
    outs = planes // 2
    cells = height * width // 4
    scale = 1.0 / math.sqrt(dp * space * samples * outs * cells)
    over_space = [("space", stage) for stage in range(bits_of(space))]
    over_chips = [("chips", stage) for stage in range(bits_of(chips))]

    share = neighbour(halo_share(volume, kernel), 1)
    preact, even, odd = partial_preact(volume, kernel)
    grads, flipped = activation(preact, share, cotangent.reshape(outs * cells, co), space, cores)
    above = neighbour(grads[:cells], -1)

    early = kernel_grad_part(even, odd, grads, None, (1, 2), cores, chips, scale, space)
    early_units, late_units = 18 * (co // 128), 9 * (co // 128)
    plan = over_space + over_chips
    value, sent = add_cores(early[0], early[1:], plan[0], cores)
    late_plan, late_now, late_half = list(over_chips), None, None
    switch_at = [len(over_space) - 1 + 2 * stage for stage in range(len(over_space))]
    stay, moved = flipped[None], None
    for place, now in enumerate(plan):
        got = exchange_stage(sent, *now, cores)
        tokens = [sent]
        if place == 0:
            late = kernel_grad_part(even, odd, grads, above, (0,), cores, chips, scale, 1, 1, (sent,))
            tokens.append(late[1])
        elif late_half is None:
            then = late_plan.pop(0) if late_plan else None
            if late_now is None:
                result = add_cores(late[0], late[1:], then, cores, (sent,))
            else:
                result = add_stage(late_value, late_got, late_now, then, cores, (sent,))
            late_now = then
            if then is None:
                late_half = result
            else:
                late_value, late_sent = result
                late_got = (exchange_stage(late_sent, *then, cores),)
                tokens.append(late_sent)
        if switch_at and place == switch_at[0]:
            stage = len(over_space) - len(switch_at)
            switch_at.pop(0)
            stay, out = switch_stage(stay, moved, 0, None, stage, cores, (tokens[-1],))
            moved = exchange_space(out, stage, cores)
            tokens.append(out)
        if place + 1 < len(plan):
            value, sent = add_stage(value, (got,), now, plan[place + 1], cores, tuple(tokens[1:]))
    for stage in range(len(over_space) - len(switch_at), len(over_space)):
        stay, out = switch_stage(stay, moved, 0, None, stage, cores, (sent,))
        moved = exchange_space(out, stage, cores)
    if late_half is None:
        late_half = add_stage(late_value, late_got, late_now, None, cores)

    mine = join(value, got, late_half, plan[-1], cores, tuple(tokens[1:]))
    early_rows = mine.shape[0] - late_half.shape[0]
    switched = None
    for step, (_, stage) in enumerate(reversed(over_space)):
        got = exchange_space(mine, stage, cores)
        order = ()
        if switched is None:
            switched, done = switched_of(stay, moved, 0, space, cores, (mine,))
            order = (done,)
        if step + 1 < len(over_space):
            mine = gather_stage(mine, got, early_rows << step, order)
    volume_grad, done = volume_grad_of(grads, above, kernel, height, width, (mine,))
    kernel_grad = kernel_grad_out(mine, got, early_units, late_units, space, cores, co, (done,))

    return (
        switched[None],
        volume_grad.reshape(volume.shape),
        kernel_grad.reshape(3, 3, 3, ci // dp, co),
    )


def solution(mesh):
    in_specs = (P("dp", "space", None, None, None), P(), P("dp", "space", None, None, None))
    out_specs = (
        P("dp", "space", None),
        P("dp", "space", None, None, None),
        P(None, None, None, "dp", None),
    )
    return jax.shard_map(body, mesh=mesh, in_specs=in_specs, out_specs=out_specs, check_vma=False)
```

```python
import functools
import math

import jax
import jax.numpy as jnp
from jax import lax
from jax.experimental import pallas as pl
from jax.experimental.pallas import tpu as pltpu
from jax.sharding import PartitionSpec as P

BF16 = jnp.bfloat16
F32 = jnp.float32
VMEM_LIMIT = 20 * 1024 * 1024
DONE = (8, 128)
PLANE_PARTS = 1
SPACER = 7 * 10**8
VMEM_WHOLE = 60 * 1024 * 1024


def call(kernel, out_shape, scratch=(), in_specs=None, limit=VMEM_LIMIT, order=(), inputs=0, flops=1000):
    extra = {} if in_specs is None else {"in_specs": in_specs}
    if order:
        whole = pl.BlockSpec(memory_space=pltpu.VMEM)
        extra["in_specs"] = [whole] * inputs + [pl.BlockSpec(memory_space=pl.ANY)] * len(order)
        inner, count = kernel, len(order)

        def kernel(*refs):
            inner(*refs[:inputs], *refs[inputs + count :])

    return pl.pallas_call(
        kernel,
        out_shape=out_shape,
        scratch_shapes=list(scratch),
        compiler_params=pltpu.CompilerParams(vmem_limit_bytes=limit),
        cost_estimate=pl.CostEstimate(flops=flops, bytes_accessed=1000, transcendentals=0),
        **extra,
    )


def spread_plane(plane, wide):
    height, width, chans = plane.shape
    cells = height * width
    half = width // 2
    wide[pl.ds(8, cells), :] = plane.reshape(cells, chans).astype(F32)
    left = wide[pl.ds(7, cells // 2, stride=2), :]
    even = wide[pl.ds(8, cells // 2, stride=2), :]
    odd = wide[pl.ds(9, cells // 2, stride=2), :]
    column = lax.broadcasted_iota(jnp.int32, left.shape, 0) % half
    left = jnp.where(column == 0, 0.0, left)
    joined = jnp.concatenate([left.astype(BF16), even.astype(BF16), odd.astype(BF16)], axis=1)
    joined = joined.reshape(height // 2, 2, half, 3 * chans)
    return joined[:, 0], joined[:, 1]


def tap_rows(even, odd, plane, kh):
    height = even.shape[1]
    picked = even[plane] if kh == 1 else odd[plane, pl.ds(0 if kh == 0 else 1, height)]
    return picked.reshape(height * even.shape[2], even.shape[3])


def bits_of(count):
    bits = count.bit_length() - 1
    assert 1 << bits == count
    return bits


def odd_core(cores):
    return lax.axis_index("dp") % cores == 1 if cores == 2 else False


def reverse_bits(value, bits):
    return sum(((value >> bit) & 1) << (bits - 1 - bit) for bit in range(bits))


def staged_place(target, space, cores):
    return jnp.where(odd_core(cores), target, reverse_bits(target, bits_of(space)))


def relative_place(source, space, cores):
    bits = bits_of(space)
    off = source ^ lax.axis_index("space")
    return jnp.where(odd_core(cores), reverse_bits(off, bits), off)


def relative_group(group, space, cores):
    bits = bits_of(space)
    index = lax.axis_index("space")
    mine = jnp.where(odd_core(cores), index, reverse_bits(index, bits))
    return group ^ mine


def halo_kernel(volume_ref, kernel_ref, share_ref, plane, weights, wide, sems):
    planes, height, width, chans = volume_ref.shape[1:]
    part = height // PLANE_PARTS
    rows = [pl.ds(index * part, part) for index in range(PLANE_PARTS)]
    copies = [
        pltpu.make_async_copy(volume_ref.at[0, planes - 1, row], plane.at[row], sems.at[index])
        for index, row in enumerate(rows)
    ]
    loads = [
        pltpu.make_async_copy(kernel_ref.at[0, kh], weights.at[kh], sems.at[PLANE_PARTS + kh])
        for kh in range(3)
    ]
    for copy in copies + loads:
        copy.start()
    for copy in copies:
        copy.wait()
    even, odd = spread_plane(plane[...], wide)
    above = jnp.concatenate([jnp.zeros_like(odd[:1]), odd[:-1]], axis=0)
    total = None
    for kh, rows in enumerate((above, even, odd)):
        loads[kh].wait()
        lhs = rows.reshape(height * width // 4, 3 * chans)
        rhs = weights[kh].reshape(3 * chans, weights.shape[-1])
        term = jnp.dot(lhs, rhs, preferred_element_type=F32)
        total = term if total is None else total + term
    share_ref[...] = total.astype(BF16)


def halo_share(volume, kernel):
    _, planes, height, width, chans = volume.shape
    co = kernel.shape[-1]
    return call(
        halo_kernel,
        jax.ShapeDtypeStruct((height * width // 4, co), BF16),
        [
            pltpu.VMEM((height, width, chans), BF16),
            pltpu.VMEM((3, 3, chans, co), BF16),
            pltpu.VMEM((height * width + 16, chans), F32),
            pltpu.SemaphoreType.DMA((PLANE_PARTS + 3,)),
        ],
        [pl.BlockSpec(memory_space=pltpu.HBM)] * 2,
        VMEM_WHOLE,
    )(volume, kernel)


def preact_kernel(volume_ref, kernel_ref, preact_ref, even_ref, odd_ref, wide):
    planes, height, width, chans = volume_ref.shape[1:]
    cells = height * width // 4
    outs = planes // 2
    for plane in range(planes):
        even, odd = spread_plane(volume_ref[0, plane], wide)
        even_ref[plane] = even
        odd_ref[plane, pl.ds(0, 1)] = jnp.zeros_like(odd[:1])
        odd_ref[plane, pl.ds(1, height // 2)] = odd
    co = kernel_ref.shape[-1]
    total = None
    for kd in (1, 2):
        for kh in range(3):
            lhs = [tap_rows(even_ref, odd_ref, 2 * d - 1 + kd, kh) for d in range(outs)]
            rhs = kernel_ref[kd, kh].reshape(3 * chans, co)
            term = jnp.dot(jnp.concatenate(lhs, axis=0), rhs, preferred_element_type=F32)
            total = term if total is None else total + term
    preact_ref[...] = total
    if outs > 1:
        total = preact_ref[pl.ds(cells, (outs - 1) * cells), :]
        for kh in range(3):
            lhs = [tap_rows(even_ref, odd_ref, 2 * d - 1, kh) for d in range(1, outs)]
            rhs = kernel_ref[0, kh].reshape(3 * chans, co)
            total += jnp.dot(jnp.concatenate(lhs, axis=0), rhs, preferred_element_type=F32)
        preact_ref[pl.ds(cells, (outs - 1) * cells), :] = total


def partial_preact(volume, kernel):
    _, planes, height, width, chans = volume.shape
    co = kernel.shape[-1]
    cells = height * width // 4
    h2, w2 = height // 2, width // 2
    return call(
        preact_kernel,
        (
            jax.ShapeDtypeStruct((planes // 2 * cells, co), F32),
            jax.ShapeDtypeStruct((planes, h2, w2, 3 * chans), BF16),
            jax.ShapeDtypeStruct((planes, h2 + 1, w2, 3 * chans), BF16),
        ),
        [pltpu.VMEM((height * width + 16, chans), F32)],
    )(volume, kernel)


def activation_kernel(space, cores, preact_ref, share_ref, cotangent_ref, grad_ref, flipped_ref):
    cells, co = share_ref.shape
    count = preact_ref.shape[0] // cells
    group = co // space
    strips = cells // 128
    for d in range(count):
        rows = pl.ds(d * cells, cells)
        value = preact_ref[rows, :]
        if d == 0:
            value = value + share_ref[...].astype(F32)
        sig = jax.nn.sigmoid(value)
        slope = sig * (1.0 + value * (1.0 - sig))
        grad_ref[rows, :] = (cotangent_ref[rows, :].astype(F32) * slope).astype(BF16)
        flipped = (value * sig).T.astype(BF16)
        for target in range(space):
            place = staged_place(target, space, cores)
            for strip in range(strips):
                flipped_ref[place, d * strips + strip] = flipped[
                    target * group : (target + 1) * group, strip * 128 : (strip + 1) * 128
                ]


def activation(preact, share, cotangent, space, cores):
    cells, co = preact.shape
    return call(
        functools.partial(activation_kernel, space, cores),
        (
            jax.ShapeDtypeStruct((cells, co), BF16),
            jax.ShapeDtypeStruct((space, cells // 128, co // space, 128), BF16),
        ),
    )(preact, share, cotangent)


def switched_kernel(space, cores, came, kept_ref, got_ref, out_ref, done_ref):
    done_ref[...] = jnp.zeros_like(done_ref)
    half = space // 2
    rows = kept_ref.shape[1]
    strips = kept_ref.shape[0] // half
    for source in range(space):
        place = relative_place(source, space, cores)
        far = place // half
        for strip in range(strips):
            column = (source * strips + strip) * 128
            row = (place % half) * strips + strip
            there = got_ref[pl.ds(pl.multiple_of(came + row * rows, rows), rows), :]
            out_ref[:, column : column + 128] = jnp.where(far == 1, there, kept_ref[row])


def switched_of(kept, got, came, space, cores, order):
    group = kept.shape[-2]
    kept = kept.reshape(-1, group, 128)
    return call(
        functools.partial(switched_kernel, space, cores, came),
        (
            jax.ShapeDtypeStruct((group, 2 * kept.shape[0] * 128), BF16),
            jax.ShapeDtypeStruct(DONE, F32),
        ),
        order=order,
        inputs=2,
    )(kept, got, *order)


def side(axis, stage, cores):
    if axis == "chips":
        return (lax.axis_index("dp") // cores >> stage) & 1
    bits = bits_of(lax.axis_size("space"))
    index = lax.axis_index("space")
    return jnp.where(odd_core(cores), (index >> (bits - 1 - stage)) & 1, (index >> stage) & 1)


def halves_of(shape, axis):
    units, chips = shape[:2]
    lead = (1, 2, units // 2 * chips) if axis == "space" else (units * chips // 2, 2, 1)
    return lead + tuple(shape[2:])


def half_shape(shape, axis):
    units, chips = shape[:2]
    return ((units // 2, chips) if axis == "space" else (units, chips // 2)) + tuple(shape[2:])


def add_kernel(now, then, cores, value_ref, *refs):
    outs = 1 if then is None else 2
    got = jnp.concatenate([ref[...] for ref in refs[:-outs]], axis=0).astype(F32)
    total = value_ref[...] if now is None else value_ref[:, side(*now, cores)]
    total = total.reshape(got.shape) + got
    if then is None:
        refs[-1][...] = total.astype(BF16)
        return
    keep_ref, sent_ref = refs[-2:]
    keep_ref[...] = total.reshape(keep_ref.shape)
    sent_ref[...] = keep_ref[:, 1 - side(*then, cores)].reshape(sent_ref.shape).astype(BF16)


def add_stage(value, got, now, then, cores, order=(), flops=1000):
    shape = (sum(piece.shape[0] for piece in got),) + got[0].shape[1:]
    if then is None:
        outs = jax.ShapeDtypeStruct(shape, BF16)
    else:
        outs = (
            jax.ShapeDtypeStruct(halves_of(shape, then[0]), F32),
            jax.ShapeDtypeStruct(half_shape(shape, then[0]), BF16),
        )
    return call(
        functools.partial(add_kernel, now, then, cores),
        outs,
        order=order,
        inputs=1 + len(got),
        flops=flops,
    )(value, *got, *order)


def switch_kernel(stage, cores, came, first_ref, *refs):
    stay_ref, out_ref = refs[-2:]
    refs = list(refs[:-2])
    bit = side("space", stage, cores)
    sources, _, targets, strips, rows, lanes = first_ref.shape
    half = targets * strips * rows
    if came is None:
        ahead = out_ref.shape[0] - sources * half
    else:
        ahead = out_ref.shape[0] - 2 * sources * half
    rider = refs.pop() if ahead else None
    if rider is not None:
        out_ref[pl.ds(0, ahead), :] = rider[...]
    place = ahead
    for source in range(sources):
        stay_ref[source] = first_ref[source, bit]
        out_ref[pl.ds(place, half), :] = first_ref[source, 1 - bit].reshape(half, lanes)
        place += half
    if came is not None:
        got_ref = refs[0]
        for source in range(sources):
            base = came + source * 2 * half
            mine = got_ref[pl.ds(pl.multiple_of(base + bit * half, rows), half), :]
            stay_ref[sources + source] = mine.reshape(targets, strips, rows, lanes)
            out_ref[pl.ds(place, half), :] = got_ref[
                pl.ds(pl.multiple_of(base + (1 - bit) * half, rows), half), :
            ]
            place += half


def switch_stage(first, got, came, rider, stage, cores, order):
    sources, targets, strips, rows, lanes = first.shape
    operands = (first.reshape(sources, 2, targets // 2, strips, rows, lanes),)
    total = sources * (1 if got is None else 2)
    count = total * targets // 2 * strips * rows
    if got is not None:
        operands += (got,)
    if rider is not None:
        operands += (rider.reshape(-1, lanes),)
        count += operands[-1].shape[0]
    return call(
        functools.partial(switch_kernel, stage, cores, None if got is None else came),
        (
            jax.ShapeDtypeStruct((total, targets // 2, strips, rows, lanes), BF16),
            jax.ShapeDtypeStruct((count, lanes), BF16),
        ),
        order=order,
        inputs=len(operands),
    )(*operands, *order)


def gather_kernel(early, mine_ref, got_ref, *outs):
    rows = pl.ds(early, mine_ref.shape[0] - early)
    outs[0][pl.ds(0, early)] = mine_ref[pl.ds(0, early)]
    outs[0][pl.ds(early, early)] = got_ref[pl.ds(0, early)]
    total = mine_ref[rows].astype(F32) + got_ref[rows].astype(F32)
    if len(outs) == 2:
        outs[1][...] = total
    else:
        outs[0][pl.ds(2 * early, total.shape[0])] = total.astype(BF16)


def gather_stage(mine, got, early, last, order=()):
    late, rest = mine.shape[0] - early, mine.shape[1:]
    if last:
        outs = (
            jax.ShapeDtypeStruct((2 * early,) + rest, BF16),
            jax.ShapeDtypeStruct((late,) + rest, F32),
        )
    else:
        outs = (jax.ShapeDtypeStruct((2 * early + late,) + rest, BF16),)
    return call(functools.partial(gather_kernel, early), outs, order=order, inputs=2)(mine, got, *order)


def join_kernel(early_ref, late_ref, got_ref, out_ref):
    early = early_ref.shape[0]
    total = late_ref[...].astype(F32) + got_ref[...].astype(F32)
    out_ref[pl.ds(0, early)] = early_ref[...].reshape((early,) + out_ref.shape[1:])
    out_ref[pl.ds(early, total.shape[0])] = total.reshape((-1,) + out_ref.shape[1:]).astype(BF16)


def join(early, late, got, order):
    return call(
        join_kernel,
        jax.ShapeDtypeStruct((early.shape[0] + late.shape[0],) + got.shape[2:], BF16),
        order=order,
        inputs=3,
    )(early, late, got, *order)


def kernel_grad_out_kernel(space, cores, early_units, mine_ref, got_ref, late_ref, out_ref):
    halves = out_ref.shape[-1] // 128
    half = space // 2
    share = -(-early_units // space)
    late_units = late_ref.shape[0]

    def put(index, value):
        tap, part = divmod(index, halves)
        out_ref[tap, :, part * 128 : (part + 1) * 128] = value.astype(F32)

    for unit in range(late_units):
        put(unit, late_ref[unit])
    for group in range(space):
        place = relative_group(group, space, cores)
        far, row = place // half, (place % half) * share
        for unit in range(share):
            index = group * share + unit
            if index < early_units:
                put(late_units + index, jnp.where(far == 1, got_ref[row + unit], mine_ref[row + unit]))


def kernel_grad_out(mine, got, late, early_units, space, cores, co):
    taps = (early_units + late.shape[0]) * 128 // co
    return call(
        functools.partial(kernel_grad_out_kernel, space, cores, early_units),
        jax.ShapeDtypeStruct((taps, mine.shape[1], co), F32),
    )(mine, got, late)


def store_units(product, scale, core, cores, chips, put):
    chans = product.shape[0] // 3
    co = product.shape[1]
    block = chans // (cores * chips)
    halves = co // 128
    product = product * scale
    for kw in range(3):
        for half in range(halves):
            unit = product[kw * chans : (kw + 1) * chans, half * 128 : (half + 1) * 128]
            unit = unit.reshape(chips, cores, block, 128)
            for chip in range(chips):
                first = unit[chip, 0]
                last = unit[chip, cores - 1]
                keep = jnp.where(core == 0, first, last)
                send = jnp.where(core == 0, last, first)
                put(kw * halves + half, chip, keep, send)


def kernel_grad_kernel(kds, cores, chips, scale, parts, even_ref, odd_ref, grads_ref, *refs):
    above_ref = refs[0] if 0 in kds else None
    keep_ref, send_refs = refs[-1 - parts], refs[-parts:]
    size = send_refs[0].shape[0]
    outs = even_ref.shape[0] // 2
    cells = even_ref.shape[1] * even_ref.shape[2]
    core = lax.axis_index("dp") % cores
    per_row = 3 * (grads_ref.shape[1] // 128)
    for unit in range(len(kds) * 3 * per_row, keep_ref.shape[0]):
        keep_ref[unit] = jnp.zeros(keep_ref.shape[1:], F32)
        send_refs[unit // size][unit % size] = jnp.zeros(keep_ref.shape[1:], BF16)
    for place, kd in enumerate(kds):
        if kd == 0:
            planes = [2 * d - 1 for d in range(1, outs + 1)]
            rhs = [grads_ref[pl.ds(d * cells, cells), :] for d in range(1, outs)] + [above_ref[...]]
            rhs = jnp.concatenate(rhs, axis=0)
        else:
            planes = [2 * d - 1 + kd for d in range(outs)]
            rhs = grads_ref[...]
        for kh in range(3):
            lhs = [tap_rows(even_ref, odd_ref, plane, kh) for plane in planes]
            product = lax.dot_general(
                jnp.concatenate(lhs, axis=0), rhs, (((0,), (0,)), ((), ())), preferred_element_type=F32
            )

            def put(unit, chip, keep, send, base=(place * 3 + kh) * per_row):
                keep_ref[base + unit, chip] = keep
                send_refs[(base + unit) // size][(base + unit) % size, chip] = send.astype(BF16)

            store_units(product, scale, core, cores, chips, put)


def kernel_grad_part(even, odd, grads, above, kds, cores, chips, scale, multiple, parts=1, order=()):
    chans = even.shape[-1] // 3
    co = grads.shape[-1]
    units = len(kds) * 9 * (co // 128)
    units += -units % math.lcm(multiple, parts)
    shape = (units, chips, chans // (cores * chips), 128)
    operands = (even, odd, grads) + ((above,) if 0 in kds else ())
    return call(
        functools.partial(kernel_grad_kernel, kds, cores, chips, scale, parts),
        (jax.ShapeDtypeStruct(shape, F32),)
        + (jax.ShapeDtypeStruct((units // parts,) + shape[1:], BF16),) * parts,
        order=order,
        inputs=len(operands),
    )(*operands, *order)


def volume_grad_kernel(grads_ref, above_ref, kernel_ref, out_ref, done_ref, shifted, wide):
    done_ref[...] = jnp.zeros_like(done_ref)
    planes, h2, _, width, chans = out_ref.shape
    w2 = width // 2
    cells = h2 * w2
    outs = planes // 2
    co = grads_ref.shape[1]
    here, right = [], []
    for d in range(outs + 1):
        plane = grads_ref[pl.ds(d * cells, cells), :] if d < outs else above_ref[...]
        shifted[pl.ds(0, cells), :] = plane.astype(F32)
        moved = shifted[pl.ds(1, cells), :]
        column = lax.broadcasted_iota(jnp.int32, moved.shape, 0) % w2
        moved = jnp.where(column == w2 - 1, 0.0, moved).astype(BF16)
        here.append(plane)
        right.append(moved)

    def down(rows):
        return jnp.concatenate([rows[w2:], jnp.zeros((w2, co), BF16)], axis=0)

    contract = (((1,), (1,)), ((), ()))
    for plane in range(planes):
        d = plane // 2
        depth = [(1, d)] if plane % 2 == 0 else [(2, d), (0, d + 1)]
        for odd_row in range(2):
            taps = [(1, False)] if odd_row == 0 else [(2, False), (0, True)]
            both, right_only = None, None
            for kd, source in depth:
                for kh, lower in taps:
                    lhs = down(here[source]) if lower else here[source]
                    rhs = kernel_ref[kd, kh, pl.ds(1, 2)].reshape(2 * chans, co)
                    term = lax.dot_general(lhs, rhs, contract, preferred_element_type=F32)
                    both = term if both is None else both + term
                    lhs = down(right[source]) if lower else right[source]
                    term = lax.dot_general(lhs, kernel_ref[kd, kh, 0], contract, preferred_element_type=F32)
                    right_only = term if right_only is None else right_only + term
            wide[pl.ds(0, cells, stride=2), :] = both[:, :chans]
            wide[pl.ds(1, cells, stride=2), :] = both[:, chans:] + right_only
            out_ref[plane, :, odd_row] = wide[...].reshape(h2, width, chans).astype(BF16)


def volume_grad_of(grads, above, kernel, height, width, order=()):
    cells, co = grads.shape
    chans = kernel.shape[3]
    planes = 2 * cells * 4 // (height * width)
    shape = (planes, height // 2, 2, width, chans)
    return call(
        volume_grad_kernel,
        (jax.ShapeDtypeStruct(shape, BF16), jax.ShapeDtypeStruct(DONE, F32)),
        [
            pltpu.VMEM((height * width // 4 + 8, co), F32),
            pltpu.VMEM((height * width // 2, chans), F32),
        ],
        order=order,
        inputs=3,
    )(grads, above, kernel, *order)


def exchange(value, partner):
    dp, space = lax.axis_size("dp"), lax.axis_size("space")
    pairs = []
    for i in range(dp):
        for j in range(space):
            to_dp, to_space = partner(i, j)
            pairs.append((i * space + j, to_dp * space + to_space))
    return lax.ppermute(value, ("dp", "space"), pairs)


def exchange_space(value, stage, cores):
    bits = bits_of(lax.axis_size("space"))

    def partner(i, j):
        bit = bits - 1 - stage if cores == 2 and i % 2 == 1 else stage
        return i, j ^ (1 << bit)

    return exchange(value, partner)


def exchange_chips(value, bit, cores):
    return exchange(value, lambda i, j: (i ^ (cores << bit), j))


def neighbour(value, steps):
    count = lax.axis_size("space")
    first, last = (max(0, -steps), min(count, count - steps))
    return lax.ppermute(value, "space", [(source, source + steps) for source in range(first, last)])


def exchange_stage(value, axis, stage, cores):
    return exchange_space(value, stage, cores) if axis == "space" else exchange_chips(value, stage, cores)


def add_cores(keep, sends, then, cores, order=()):
    got = tuple(exchange(send, lambda i, j: (i ^ 1, j)) if cores == 2 else 0 * send for send in sends)
    return add_stage(keep, got, None, then, cores, order)


def body(volume, kernel, cotangent):
    samples, planes, height, width, ci = volume.shape
    co = kernel.shape[-1]
    assert samples == 1
    dp, space = lax.axis_size("dp"), lax.axis_size("space")
    cores = 2 if dp % 2 == 0 else 1
    chips = dp // cores
    outs = planes // 2
    cells = height * width // 4
    scale = 1.0 / math.sqrt(dp * space * samples * outs * cells)
    over_space = [("space", stage) for stage in range(bits_of(space))]
    over_chips = [("chips", stage) for stage in range(bits_of(chips))]

    share = neighbour(halo_share(volume, kernel), 1)
    preact, even, odd = partial_preact(volume, kernel)
    grads, flipped = activation(preact, share, cotangent.reshape(outs * cells, co), space, cores)
    above = neighbour(grads[:cells], -1)

    early = kernel_grad_part(even, odd, grads, None, (1, 2), cores, chips, scale, space)
    early_units = 18 * (co // 128)
    plan = over_space + over_chips
    value, sent = add_cores(early[0], early[1:], plan[0], cores)
    late_plan, late_now, late_half = list(over_chips), None, None
    switch_at = [len(over_space) - 1 + stage for stage in range(len(over_space))]
    stay, moved = flipped[None], None
    for place, now in enumerate(plan):
        got = exchange_stage(sent, *now, cores)
        tokens = [sent]
        if place == 0:
            late = kernel_grad_part(even, odd, grads, above, (0,), cores, chips, scale, 1, 1, (sent,))
            tokens.append(late[1])
        elif late_half is None:
            then = late_plan.pop(0) if late_plan else None
            if late_now is None:
                result = add_cores(late[0], late[1:], then, cores, (sent,))
            else:
                result = add_stage(late_value, late_got, late_now, then, cores, (sent,))
            late_now = then
            if then is None:
                late_half = result
            else:
                late_value, late_sent = result
                late_got = (exchange_stage(late_sent, *then, cores),)
                tokens.append(late_sent)
        if switch_at and place == switch_at[0]:
            stage = len(over_space) - len(switch_at)
            switch_at.pop(0)
            stay, out = switch_stage(stay, moved, 0, None, stage, cores, (tokens[-1],))
            moved = exchange_space(out, stage, cores)
            tokens.append(out)
        if place + 1 < len(plan):
            value, sent = add_stage(value, (got,), now, plan[place + 1], cores, tuple(tokens[1:]))
    for stage in range(len(over_space) - len(switch_at), len(over_space)):
        stay, out = switch_stage(stay, moved, 0, None, stage, cores, (sent,))
        moved = exchange_space(out, stage, cores)
    if late_half is None:
        late_half = add_stage(late_value, late_got, late_now, None, cores)
    late_got = exchange_space(late_half, 0, cores)
    early_sum = add_stage(value, (got,), plan[-1], None, cores, (late_half,), SPACER)

    switched, done = switched_of(stay, moved, 0, space, cores, (late_half,))
    mine = join(early_sum, late_half, late_got, (done,))
    early_rows = early_sum.shape[0]
    volume_grad, done = volume_grad_of(grads, above, kernel, height, width, (mine,))
    for step, (_, stage) in enumerate(reversed(over_space)):
        got = exchange_space(mine, stage, cores)
        order = () if step else (done,)
        if stage:
            mine, *late_sum = gather_stage(mine, got, early_rows << step, stage == 1, order)
    kernel_grad = kernel_grad_out(mine, got, late_sum[0], early_units, space, cores, co)

    return (
        switched[None],
        volume_grad.reshape(volume.shape),
        kernel_grad.reshape(3, 3, 3, ci // dp, co),
    )


def solution(mesh):
    in_specs = (P("dp", "space", None, None, None), P(), P("dp", "space", None, None, None))
    out_specs = (
        P("dp", "space", None),
        P("dp", "space", None, None, None),
        P(None, None, None, "dp", None),
    )
    return jax.shard_map(body, mesh=mesh, in_specs=in_specs, out_specs=out_specs, check_vma=False)
```

```python
import functools
import math

import jax
import jax.numpy as jnp
from jax import lax
from jax.experimental import pallas as pl
from jax.experimental.pallas import tpu as pltpu
from jax.sharding import PartitionSpec as P

BF16 = jnp.bfloat16
F32 = jnp.float32
VMEM_LIMIT = 20 * 1024 * 1024
DONE = (8, 128)
PLANE_PARTS = 1
SPACER = 6 * 10**9
VMEM_WHOLE = 63 * 1024 * 1024


def call(kernel, out_shape, scratch=(), in_specs=None, limit=VMEM_LIMIT, order=(), inputs=0, flops=1000):
    extra = {} if in_specs is None else {"in_specs": in_specs}
    if order:
        whole = pl.BlockSpec(memory_space=pltpu.VMEM)
        extra["in_specs"] = [whole] * inputs + [pl.BlockSpec(memory_space=pl.ANY)] * len(order)
        inner, count = kernel, len(order)

        def kernel(*refs):
            inner(*refs[:inputs], *refs[inputs + count :])

    return pl.pallas_call(
        kernel,
        out_shape=out_shape,
        scratch_shapes=list(scratch),
        compiler_params=pltpu.CompilerParams(vmem_limit_bytes=limit),
        cost_estimate=pl.CostEstimate(flops=flops, bytes_accessed=1000, transcendentals=0),
        **extra,
    )


def spread_plane(plane, wide):
    height, width, chans = plane.shape
    cells = height * width
    half = width // 2
    wide[pl.ds(8, cells), :] = plane.reshape(cells, chans).astype(F32)
    left = wide[pl.ds(7, cells // 2, stride=2), :]
    even = wide[pl.ds(8, cells // 2, stride=2), :]
    odd = wide[pl.ds(9, cells // 2, stride=2), :]
    column = lax.broadcasted_iota(jnp.int32, left.shape, 0) % half
    left = jnp.where(column == 0, 0.0, left)
    joined = jnp.concatenate([left.astype(BF16), even.astype(BF16), odd.astype(BF16)], axis=1)
    joined = joined.reshape(height // 2, 2, half, 3 * chans)
    return joined[:, 0], joined[:, 1]


def tap_rows(even, odd, plane, kh):
    height = even.shape[1]
    picked = even[plane] if kh == 1 else odd[plane, pl.ds(0 if kh == 0 else 1, height)]
    return picked.reshape(height * even.shape[2], even.shape[3])


def bits_of(count):
    bits = count.bit_length() - 1
    assert 1 << bits == count
    return bits


def odd_core(cores):
    return lax.axis_index("dp") % cores == 1 if cores == 2 else False


def reverse_bits(value, bits):
    return sum(((value >> bit) & 1) << (bits - 1 - bit) for bit in range(bits))


def staged_place(target, space, cores):
    return jnp.where(odd_core(cores), target, reverse_bits(target, bits_of(space)))


def relative_place(source, space, cores):
    bits = bits_of(space)
    off = source ^ lax.axis_index("space")
    return jnp.where(odd_core(cores), reverse_bits(off, bits), off)


def relative_group(group, space, cores):
    bits = bits_of(space)
    index = lax.axis_index("space")
    mine = jnp.where(odd_core(cores), index, reverse_bits(index, bits))
    return group ^ mine


def halo_kernel(volume_ref, kernel_ref, share_ref, plane, weights, wide, sems):
    planes, height, width, chans = volume_ref.shape[1:]
    part = height // PLANE_PARTS
    rows = [pl.ds(index * part, part) for index in range(PLANE_PARTS)]
    copies = [
        pltpu.make_async_copy(volume_ref.at[0, planes - 1, row], plane.at[row], sems.at[index])
        for index, row in enumerate(rows)
    ]
    loads = [
        pltpu.make_async_copy(kernel_ref.at[0, kh], weights.at[kh], sems.at[PLANE_PARTS + kh])
        for kh in range(3)
    ]
    for copy in copies + loads:
        copy.start()
    for copy in copies:
        copy.wait()
    even, odd = spread_plane(plane[...], wide)
    above = jnp.concatenate([jnp.zeros_like(odd[:1]), odd[:-1]], axis=0)
    total = None
    for kh, rows in enumerate((above, even, odd)):
        loads[kh].wait()
        lhs = rows.reshape(height * width // 4, 3 * chans)
        rhs = weights[kh].reshape(3 * chans, weights.shape[-1])
        term = jnp.dot(lhs, rhs, preferred_element_type=F32)
        total = term if total is None else total + term
    share_ref[...] = total.astype(BF16)


def halo_share(volume, kernel):
    _, planes, height, width, chans = volume.shape
    co = kernel.shape[-1]
    return call(
        halo_kernel,
        jax.ShapeDtypeStruct((height * width // 4, co), BF16),
        [
            pltpu.VMEM((height, width, chans), BF16),
            pltpu.VMEM((3, 3, chans, co), BF16),
            pltpu.VMEM((height * width + 16, chans), F32),
            pltpu.SemaphoreType.DMA((PLANE_PARTS + 3,)),
        ],
        [pl.BlockSpec(memory_space=pltpu.HBM)] * 2,
        VMEM_WHOLE,
    )(volume, kernel)


def preact_kernel(volume_ref, kernel_ref, preact_ref, even_ref, odd_ref, wide):
    planes, height, width, chans = volume_ref.shape[1:]
    cells = height * width // 4
    outs = planes // 2
    for plane in range(planes):
        even, odd = spread_plane(volume_ref[0, plane], wide)
        even_ref[plane] = even
        odd_ref[plane, pl.ds(0, 1)] = jnp.zeros_like(odd[:1])
        odd_ref[plane, pl.ds(1, height // 2)] = odd
    co = kernel_ref.shape[-1]
    total = None
    for kd in (1, 2):
        for kh in range(3):
            lhs = [tap_rows(even_ref, odd_ref, 2 * d - 1 + kd, kh) for d in range(outs)]
            rhs = kernel_ref[kd, kh].reshape(3 * chans, co)
            term = jnp.dot(jnp.concatenate(lhs, axis=0), rhs, preferred_element_type=F32)
            total = term if total is None else total + term
    preact_ref[...] = total
    if outs > 1:
        total = preact_ref[pl.ds(cells, (outs - 1) * cells), :]
        for kh in range(3):
            lhs = [tap_rows(even_ref, odd_ref, 2 * d - 1, kh) for d in range(1, outs)]
            rhs = kernel_ref[0, kh].reshape(3 * chans, co)
            total += jnp.dot(jnp.concatenate(lhs, axis=0), rhs, preferred_element_type=F32)
        preact_ref[pl.ds(cells, (outs - 1) * cells), :] = total


def partial_preact(volume, kernel):
    _, planes, height, width, chans = volume.shape
    co = kernel.shape[-1]
    cells = height * width // 4
    h2, w2 = height // 2, width // 2
    return call(
        preact_kernel,
        (
            jax.ShapeDtypeStruct((planes // 2 * cells, co), F32),
            jax.ShapeDtypeStruct((planes, h2, w2, 3 * chans), BF16),
            jax.ShapeDtypeStruct((planes, h2 + 1, w2, 3 * chans), BF16),
        ),
        [pltpu.VMEM((height * width + 16, chans), F32)],
    )(volume, kernel)


def activation_kernel(space, cores, start, preact_ref, cotangent_ref, *refs):
    grad_ref, flipped_ref = refs[-2:]
    share_ref = refs[0] if len(refs) == 3 else None
    co = preact_ref.shape[1]
    count = grad_ref.shape[0]
    group, strips = co // space, flipped_ref.shape[1]
    rows = pl.ds(start, count)
    value = preact_ref[rows, :]
    if share_ref is not None:
        value = value + share_ref[...].astype(F32)
    sig = jax.nn.sigmoid(value)
    slope = sig * (1.0 + value * (1.0 - sig))
    grad_ref[...] = (cotangent_ref[rows, :].astype(F32) * slope).astype(BF16)
    flipped = (value * sig).T.astype(BF16)
    for target in range(space):
        place = staged_place(target, space, cores)
        for strip in range(strips):
            flipped_ref[place, strip] = flipped[
                target * group : (target + 1) * group, strip * 128 : (strip + 1) * 128
            ]


def activation(preact, cotangent, share, start, count, space, cores):
    co = preact.shape[1]
    return call(
        functools.partial(activation_kernel, space, cores, start),
        (
            jax.ShapeDtypeStruct((count, co), BF16),
            jax.ShapeDtypeStruct((space, count // 128, co // space, 128), BF16),
        ),
    )(preact, cotangent, *(() if share is None else (share,)))


def switched_kernel(space, cores, came, kept_ref, got_ref, out_ref, done_ref):
    done_ref[...] = jnp.zeros_like(done_ref)
    half = space // 2
    rows = kept_ref.shape[1]
    strips = kept_ref.shape[0] // half
    for source in range(space):
        place = relative_place(source, space, cores)
        far = place // half
        for strip in range(strips):
            column = (source * strips + strip) * 128
            row = (place % half) * strips + strip
            there = got_ref[pl.ds(pl.multiple_of(came + row * rows, rows), rows), :]
            out_ref[:, column : column + 128] = jnp.where(far == 1, there, kept_ref[row])


def switched_of(kept, got, came, space, cores, order):
    group = kept.shape[-2]
    kept = kept.reshape(-1, group, 128)
    return call(
        functools.partial(switched_kernel, space, cores, came),
        (
            jax.ShapeDtypeStruct((group, 2 * kept.shape[0] * 128), BF16),
            jax.ShapeDtypeStruct(DONE, F32),
        ),
        order=order,
        inputs=2,
    )(kept, got, *order)


def side(axis, stage, cores):
    if axis == "chips":
        return (lax.axis_index("dp") // cores >> stage) & 1
    bits = bits_of(lax.axis_size("space"))
    index = lax.axis_index("space")
    return jnp.where(odd_core(cores), (index >> (bits - 1 - stage)) & 1, (index >> stage) & 1)


def halves_of(shape, axis):
    units, chips = shape[:2]
    lead = (1, 2, units // 2 * chips) if axis == "space" else (units * chips // 2, 2, 1)
    return lead + tuple(shape[2:])


def half_shape(shape, axis):
    units, chips = shape[:2]
    return ((units // 2, chips) if axis == "space" else (units, chips // 2)) + tuple(shape[2:])


def add_kernel(now, then, cores, value_ref, *refs):
    outs = 1 if then is None else 2
    got = jnp.concatenate([ref[...] for ref in refs[:-outs]], axis=0).astype(F32)
    total = value_ref[...] if now is None else value_ref[:, side(*now, cores)]
    total = total.reshape(got.shape) + got
    if then is None:
        refs[-1][...] = total.astype(BF16)
        return
    keep_ref, sent_ref = refs[-2:]
    keep_ref[...] = total.reshape(keep_ref.shape)
    sent_ref[...] = keep_ref[:, 1 - side(*then, cores)].reshape(sent_ref.shape).astype(BF16)


def add_stage(value, got, now, then, cores, order=(), flops=1000):
    shape = (sum(piece.shape[0] for piece in got),) + got[0].shape[1:]
    if then is None:
        outs = jax.ShapeDtypeStruct(shape, BF16)
    else:
        outs = (
            jax.ShapeDtypeStruct(halves_of(shape, then[0]), F32),
            jax.ShapeDtypeStruct(half_shape(shape, then[0]), BF16),
        )
    return call(
        functools.partial(add_kernel, now, then, cores),
        outs,
        order=order,
        inputs=1 + len(got),
        flops=flops,
    )(value, *got, *order)


def switch_kernel(stage, cores, came, first_ref, *refs):
    stay_ref, out_ref = refs[-2:]
    refs = list(refs[:-2])
    bit = side("space", stage, cores)
    sources, _, targets, strips, rows, lanes = first_ref.shape
    half = targets * strips * rows
    if came is None:
        ahead = out_ref.shape[0] - sources * half
    else:
        ahead = out_ref.shape[0] - 2 * sources * half
    rider = refs.pop() if ahead else None
    if rider is not None:
        out_ref[pl.ds(0, ahead), :] = rider[...]
    place = ahead
    for source in range(sources):
        stay_ref[source] = first_ref[source, bit]
        out_ref[pl.ds(place, half), :] = first_ref[source, 1 - bit].reshape(half, lanes)
        place += half
    if came is not None:
        got_ref = refs[0]
        for source in range(sources):
            base = came + source * 2 * half
            mine = got_ref[pl.ds(pl.multiple_of(base + bit * half, rows), half), :]
            stay_ref[sources + source] = mine.reshape(targets, strips, rows, lanes)
            out_ref[pl.ds(place, half), :] = got_ref[
                pl.ds(pl.multiple_of(base + (1 - bit) * half, rows), half), :
            ]
            place += half


def switch_stage(first, got, came, rider, stage, cores, order):
    sources, targets, strips, rows, lanes = first.shape
    operands = (first.reshape(sources, 2, targets // 2, strips, rows, lanes),)
    total = sources * (1 if got is None else 2)
    count = total * targets // 2 * strips * rows
    if got is not None:
        operands += (got,)
    if rider is not None:
        operands += (rider.reshape(-1, lanes),)
        count += operands[-1].shape[0]
    return call(
        functools.partial(switch_kernel, stage, cores, None if got is None else came),
        (
            jax.ShapeDtypeStruct((total, targets // 2, strips, rows, lanes), BF16),
            jax.ShapeDtypeStruct((count, lanes), BF16),
        ),
        order=order,
        inputs=len(operands),
    )(*operands, *order)


def gather_kernel(early, mine_ref, got_ref, out_ref):
    rows = pl.ds(early, mine_ref.shape[0] - early)
    out_ref[pl.ds(0, early)] = mine_ref[pl.ds(0, early)]
    out_ref[pl.ds(early, early)] = got_ref[pl.ds(0, early)]
    total = mine_ref[rows].astype(F32) + got_ref[rows].astype(F32)
    out_ref[pl.ds(2 * early, total.shape[0])] = total.astype(BF16)


def gather_stage(mine, got, early, order=()):
    return call(
        functools.partial(gather_kernel, early),
        jax.ShapeDtypeStruct((mine.shape[0] + early,) + mine.shape[1:], BF16),
        order=order,
        inputs=2,
    )(mine, got, *order)


def join_kernel(now, cores, value_ref, got_ref, late_ref, out_ref):
    total = value_ref[:, side(*now, cores)].reshape(got_ref.shape) + got_ref[...].astype(F32)
    early = total.shape[0]
    out_ref[pl.ds(0, early)] = total.reshape((early,) + out_ref.shape[1:]).astype(BF16)
    out_ref[pl.ds(early, late_ref.shape[0])] = late_ref[...].reshape((-1,) + out_ref.shape[1:])


def join(value, got, late, now, cores, order):
    shape = (got.shape[0] + late.shape[0],) + got.shape[2:]
    return call(
        functools.partial(join_kernel, now, cores),
        jax.ShapeDtypeStruct(shape, BF16),
        order=order,
        inputs=3,
        flops=SPACER,
    )(value, got, late, *order)


def kernel_grad_out_kernel(space, cores, early_units, late_units, mine_ref, got_ref, out_ref):
    halves = out_ref.shape[-1] // 128
    half = space // 2
    share = -(-early_units // space)

    def put(index, value):
        tap, part = divmod(index, halves)
        out_ref[tap, :, part * 128 : (part + 1) * 128] = value

    for unit in range(late_units):
        row = half * share + unit
        put(unit, mine_ref[row].astype(F32) + got_ref[row].astype(F32))
    for group in range(space):
        place = relative_group(group, space, cores)
        far, row = place // half, (place % half) * share
        for unit in range(share):
            index = group * share + unit
            if index < early_units:
                value = jnp.where(far == 1, got_ref[row + unit], mine_ref[row + unit])
                put(late_units + index, value.astype(F32))


def kernel_grad_out(mine, got, early_units, late_units, space, cores, co, order):
    taps = (early_units + late_units) * 128 // co
    return call(
        functools.partial(kernel_grad_out_kernel, space, cores, early_units, late_units),
        jax.ShapeDtypeStruct((taps, mine.shape[1], co), F32),
        order=order,
        inputs=2,
    )(mine, got, *order)


def store_units(product, scale, core, cores, chips, put):
    chans = product.shape[0] // 3
    co = product.shape[1]
    block = chans // (cores * chips)
    halves = co // 128
    product = product * scale
    for kw in range(3):
        for half in range(halves):
            unit = product[kw * chans : (kw + 1) * chans, half * 128 : (half + 1) * 128]
            unit = unit.reshape(chips, cores, block, 128)
            for chip in range(chips):
                first = unit[chip, 0]
                last = unit[chip, cores - 1]
                keep = jnp.where(core == 0, first, last)
                send = jnp.where(core == 0, last, first)
                put(kw * halves + half, chip, keep, send)


def tap_products(even_ref, odd_ref, planes, rhs, put):
    for kh in range(3):
        lhs = [tap_rows(even_ref, odd_ref, plane, kh) for plane in planes]
        put(
            kh,
            lax.dot_general(
                jnp.concatenate(lhs, axis=0), rhs, (((0,), (0,)), ((), ())), preferred_element_type=F32
            ),
        )


def ahead_kernel(even_ref, odd_ref, rest_ref, out_ref):
    outs = even_ref.shape[0] // 2
    for place, kd in enumerate((1, 2)):
        planes = [2 * d - 1 + kd for d in range(1, outs)]

        def put(kh, product, base=3 * place):
            out_ref[base + kh] = product

        tap_products(even_ref, odd_ref, planes, rest_ref[...], put)


def early_ahead(even, odd, rest):
    return call(
        ahead_kernel, jax.ShapeDtypeStruct((6, even.shape[-1], rest.shape[-1]), F32)
    )(even, odd, rest)


def kernel_grad_kernel(early, cores, chips, scale, even_ref, odd_ref, grads_ref, other_ref, keep_ref, send_ref):
    outs = even_ref.shape[0] // 2
    core = lax.axis_index("dp") % cores
    per_row = 3 * (grads_ref.shape[1] // 128)
    kds = (1, 2) if early else (0,)
    for unit in range(len(kds) * 3 * per_row, keep_ref.shape[0]):
        keep_ref[unit] = jnp.zeros(keep_ref.shape[1:], F32)
        send_ref[unit] = jnp.zeros(keep_ref.shape[1:], BF16)
    for place, kd in enumerate(kds):
        if early:
            planes, rhs = [kd - 1], grads_ref[...]
        else:
            planes = [2 * d - 1 for d in range(1, outs + 1)]
            rhs = jnp.concatenate([grads_ref[...], other_ref[...]], axis=0)

        def take(kh, product, base=3 * place):
            if early:
                product = product + other_ref[base + kh]

            def put(unit, chip, keep, send):
                keep_ref[(base + kh) * per_row + unit, chip] = keep
                send_ref[(base + kh) * per_row + unit, chip] = send.astype(BF16)

            store_units(product, scale, core, cores, chips, put)

        tap_products(even_ref, odd_ref, planes, rhs, take)


def kernel_grad_part(even, odd, grads, other, early, cores, chips, scale, multiple, order=()):
    chans = even.shape[-1] // 3
    units = (18 if early else 9) * (grads.shape[-1] // 128)
    units += -units % multiple
    shape = (units, chips, chans // (cores * chips), 128)
    return call(
        functools.partial(kernel_grad_kernel, early, cores, chips, scale),
        (jax.ShapeDtypeStruct(shape, F32), jax.ShapeDtypeStruct(shape, BF16)),
        order=order,
        inputs=4,
    )(even, odd, grads, other, *order)


def volume_grad_kernel(first_ref, rest_ref, above_ref, kernel_ref, out_ref, done_ref, shifted, wide):
    done_ref[...] = jnp.zeros_like(done_ref)
    planes, h2, _, width, chans = out_ref.shape
    w2 = width // 2
    cells = h2 * w2
    outs = planes // 2
    co = first_ref.shape[1]
    here, right = [], []
    for d in range(outs + 1):
        if 0 < d < outs:
            plane = rest_ref[pl.ds((d - 1) * cells, cells), :]
        else:
            plane = (first_ref if d == 0 else above_ref)[...]
        shifted[pl.ds(0, cells), :] = plane.astype(F32)
        moved = shifted[pl.ds(1, cells), :]
        column = lax.broadcasted_iota(jnp.int32, moved.shape, 0) % w2
        moved = jnp.where(column == w2 - 1, 0.0, moved).astype(BF16)
        here.append(plane)
        right.append(moved)

    def down(rows):
        return jnp.concatenate([rows[w2:], jnp.zeros((w2, co), BF16)], axis=0)

    contract = (((1,), (1,)), ((), ()))
    for plane in range(planes):
        d = plane // 2
        depth = [(1, d)] if plane % 2 == 0 else [(2, d), (0, d + 1)]
        for odd_row in range(2):
            taps = [(1, False)] if odd_row == 0 else [(2, False), (0, True)]
            both, right_only = None, None
            for kd, source in depth:
                for kh, lower in taps:
                    lhs = down(here[source]) if lower else here[source]
                    rhs = kernel_ref[kd, kh, pl.ds(1, 2)].reshape(2 * chans, co)
                    term = lax.dot_general(lhs, rhs, contract, preferred_element_type=F32)
                    both = term if both is None else both + term
                    lhs = down(right[source]) if lower else right[source]
                    term = lax.dot_general(lhs, kernel_ref[kd, kh, 0], contract, preferred_element_type=F32)
                    right_only = term if right_only is None else right_only + term
            wide[pl.ds(0, cells, stride=2), :] = both[:, :chans]
            wide[pl.ds(1, cells, stride=2), :] = both[:, chans:] + right_only
            out_ref[plane, :, odd_row] = wide[...].reshape(h2, width, chans).astype(BF16)


def volume_grad_of(first, rest, above, kernel, height, width, order=()):
    cells, co = first.shape[0] + rest.shape[0], first.shape[1]
    chans = kernel.shape[3]
    planes = 2 * cells * 4 // (height * width)
    shape = (planes, height // 2, 2, width, chans)
    return call(
        volume_grad_kernel,
        (jax.ShapeDtypeStruct(shape, BF16), jax.ShapeDtypeStruct(DONE, F32)),
        [
            pltpu.VMEM((height * width // 4 + 8, co), F32),
            pltpu.VMEM((height * width // 2, chans), F32),
        ],
        order=order,
        inputs=4,
    )(first, rest, above, kernel, *order)


def exchange(value, partner):
    dp, space = lax.axis_size("dp"), lax.axis_size("space")
    pairs = []
    for i in range(dp):
        for j in range(space):
            to_dp, to_space = partner(i, j)
            pairs.append((i * space + j, to_dp * space + to_space))
    return lax.ppermute(value, ("dp", "space"), pairs)


def exchange_space(value, stage, cores):
    bits = bits_of(lax.axis_size("space"))

    def partner(i, j):
        bit = bits - 1 - stage if cores == 2 and i % 2 == 1 else stage
        return i, j ^ (1 << bit)

    return exchange(value, partner)


def exchange_chips(value, bit, cores):
    return exchange(value, lambda i, j: (i ^ (cores << bit), j))


def neighbour(value, steps):
    count = lax.axis_size("space")
    first, last = (max(0, -steps), min(count, count - steps))
    return lax.ppermute(value, "space", [(source, source + steps) for source in range(first, last)])


def exchange_stage(value, axis, stage, cores):
    return exchange_space(value, stage, cores) if axis == "space" else exchange_chips(value, stage, cores)


def add_cores(keep, sends, then, cores, order=()):
    got = tuple(exchange(send, lambda i, j: (i ^ 1, j)) if cores == 2 else 0 * send for send in sends)
    return add_stage(keep, got, None, then, cores, order)


def body(volume, kernel, cotangent):
    samples, planes, height, width, ci = volume.shape
    co = kernel.shape[-1]
    assert samples == 1
    dp, space = lax.axis_size("dp"), lax.axis_size("space")
    cores = 2 if dp % 2 == 0 else 1
    chips = dp // cores
    outs = planes // 2
    cells = height * width // 4
    scale = 1.0 / math.sqrt(dp * space * samples * outs * cells)
    over_space = [("space", stage) for stage in range(bits_of(space))]
    over_chips = [("chips", stage) for stage in range(bits_of(chips))]

    share = neighbour(halo_share(volume, kernel), 1)
    preact, even, odd = partial_preact(volume, kernel)
    cotangent = cotangent.reshape(outs * cells, co)
    rest, flipped_rest = activation(preact, cotangent, None, cells, (outs - 1) * cells, space, cores)
    products = early_ahead(even, odd, rest)
    first, flipped = activation(preact, cotangent, share, 0, cells, space, cores)
    flipped = jnp.concatenate([flipped, flipped_rest], axis=1)
    above = neighbour(first, -1)

    early = kernel_grad_part(even, odd, first, products, True, cores, chips, scale, space)
    early_units, late_units = 18 * (co // 128), 9 * (co // 128)
    plan = over_space + over_chips
    value, sent = add_cores(early[0], early[1:], plan[0], cores)
    late_plan, late_now, late_half = list(over_chips), None, None
    switch_at = [len(over_space) - 1 + 2 * stage for stage in range(len(over_space))]
    stay, moved = flipped[None], None
    for place, now in enumerate(plan):
        got = exchange_stage(sent, *now, cores)
        tokens = [sent]
        if place == 0:
            late = kernel_grad_part(even, odd, rest, above, False, cores, chips, scale, 1, (sent,))
            tokens.append(late[1])
        elif late_half is None:
            then = late_plan.pop(0) if late_plan else None
            if late_now is None:
                result = add_cores(late[0], late[1:], then, cores, (sent,))
            else:
                result = add_stage(late_value, late_got, late_now, then, cores, (sent,))
            late_now = then
            if then is None:
                late_half = result
            else:
                late_value, late_sent = result
                late_got = (exchange_stage(late_sent, *then, cores),)
                tokens.append(late_sent)
        if switch_at and place == switch_at[0]:
            stage = len(over_space) - len(switch_at)
            switch_at.pop(0)
            stay, out = switch_stage(stay, moved, 0, None, stage, cores, (tokens[-1],))
            moved = exchange_space(out, stage, cores)
            tokens.append(out)
        if place + 1 < len(plan):
            weight = SPACER if place >= len(over_space) else 1000
            value, sent = add_stage(
                value, (got,), now, plan[place + 1], cores, tuple(tokens[1:]), weight
            )
    for stage in range(len(over_space) - len(switch_at), len(over_space)):
        stay, out = switch_stage(stay, moved, 0, None, stage, cores, (sent,))
        moved = exchange_space(out, stage, cores)
    if late_half is None:
        late_half = add_stage(late_value, late_got, late_now, None, cores)

    mine = join(value, got, late_half, plan[-1], cores, tuple(tokens[1:]))
    early_rows = mine.shape[0] - late_half.shape[0]
    switched = None
    for step, (_, stage) in enumerate(reversed(over_space)):
        got = exchange_space(mine, stage, cores)
        order = ()
        if switched is None:
            switched, done = switched_of(stay, moved, 0, space, cores, (mine,))
            order = (done,)
        if step + 1 < len(over_space):
            mine = gather_stage(mine, got, early_rows << step, order)
    volume_grad, done = volume_grad_of(first, rest, above, kernel, height, width, (mine,))
    kernel_grad = kernel_grad_out(mine, got, early_units, late_units, space, cores, co, (done,))

    return (
        switched[None],
        volume_grad.reshape(volume.shape),
        kernel_grad.reshape(3, 3, 3, ci // dp, co),
    )


def solution(mesh):
    in_specs = (P("dp", "space", None, None, None), P(), P("dp", "space", None, None, None))
    out_specs = (
        P("dp", "space", None),
        P("dp", "space", None, None, None),
        P(None, None, None, "dp", None),
    )
    return jax.shard_map(body, mesh=mesh, in_specs=in_specs, out_specs=out_specs, check_vma=False)
```

```python
import functools
import math

import jax
import jax.numpy as jnp
from jax import lax
from jax.experimental import pallas as pl
from jax.experimental.pallas import tpu as pltpu
from jax.sharding import PartitionSpec as P

BF16 = jnp.bfloat16
F32 = jnp.float32
VMEM_LIMIT = 20 * 1024 * 1024
DONE = (8, 128)
PLANE_PARTS = 1
SPACER = 6 * 10**9
VMEM_WHOLE = 60 * 1024 * 1024


def call(kernel, out_shape, scratch=(), in_specs=None, limit=VMEM_LIMIT, order=(), inputs=0, flops=1000):
    extra = {} if in_specs is None else {"in_specs": in_specs}
    if order:
        whole = pl.BlockSpec(memory_space=pltpu.VMEM)
        extra["in_specs"] = [whole] * inputs + [pl.BlockSpec(memory_space=pl.ANY)] * len(order)
        inner, count = kernel, len(order)

        def kernel(*refs):
            inner(*refs[:inputs], *refs[inputs + count :])

    return pl.pallas_call(
        kernel,
        out_shape=out_shape,
        scratch_shapes=list(scratch),
        compiler_params=pltpu.CompilerParams(vmem_limit_bytes=limit),
        cost_estimate=pl.CostEstimate(flops=flops, bytes_accessed=1000, transcendentals=0),
        **extra,
    )


def spread_plane(plane, wide):
    height, width, chans = plane.shape
    cells = height * width
    half = width // 2
    wide[pl.ds(8, cells), :] = plane.reshape(cells, chans).astype(F32)
    left = wide[pl.ds(7, cells // 2, stride=2), :]
    even = wide[pl.ds(8, cells // 2, stride=2), :]
    odd = wide[pl.ds(9, cells // 2, stride=2), :]
    column = lax.broadcasted_iota(jnp.int32, left.shape, 0) % half
    left = jnp.where(column == 0, 0.0, left)
    joined = jnp.concatenate([left.astype(BF16), even.astype(BF16), odd.astype(BF16)], axis=1)
    joined = joined.reshape(height // 2, 2, half, 3 * chans)
    return joined[:, 0], joined[:, 1]


def tap_rows(even, odd, plane, kh):
    height = even.shape[1]
    picked = even[plane] if kh == 1 else odd[plane, pl.ds(0 if kh == 0 else 1, height)]
    return picked.reshape(height * even.shape[2], even.shape[3])


def bits_of(count):
    bits = count.bit_length() - 1
    assert 1 << bits == count
    return bits


def odd_core(cores):
    return lax.axis_index("dp") % cores == 1 if cores == 2 else False


def reverse_bits(value, bits):
    return sum(((value >> bit) & 1) << (bits - 1 - bit) for bit in range(bits))


def staged_place(target, space, cores):
    return jnp.where(odd_core(cores), target, reverse_bits(target, bits_of(space)))


def relative_place(source, space, cores):
    bits = bits_of(space)
    off = source ^ lax.axis_index("space")
    return jnp.where(odd_core(cores), reverse_bits(off, bits), off)


def relative_group(group, space, cores):
    bits = bits_of(space)
    index = lax.axis_index("space")
    mine = jnp.where(odd_core(cores), index, reverse_bits(index, bits))
    return group ^ mine


def halo_kernel(volume_ref, kernel_ref, share_ref, plane, weights, wide, sems):
    planes, height, width, chans = volume_ref.shape[1:]
    part = height // PLANE_PARTS
    rows = [pl.ds(index * part, part) for index in range(PLANE_PARTS)]
    copies = [
        pltpu.make_async_copy(volume_ref.at[0, planes - 1, row], plane.at[row], sems.at[index])
        for index, row in enumerate(rows)
    ]
    loads = [
        pltpu.make_async_copy(kernel_ref.at[0, kh], weights.at[kh], sems.at[PLANE_PARTS + kh])
        for kh in range(3)
    ]
    for copy in copies + loads:
        copy.start()
    for copy in copies:
        copy.wait()
    even, odd = spread_plane(plane[...], wide)
    above = jnp.concatenate([jnp.zeros_like(odd[:1]), odd[:-1]], axis=0)
    total = None
    for kh, rows in enumerate((above, even, odd)):
        loads[kh].wait()
        lhs = rows.reshape(height * width // 4, 3 * chans)
        rhs = weights[kh].reshape(3 * chans, weights.shape[-1])
        term = jnp.dot(lhs, rhs, preferred_element_type=F32)
        total = term if total is None else total + term
    share_ref[...] = total.astype(BF16)


def halo_share(volume, kernel):
    _, planes, height, width, chans = volume.shape
    co = kernel.shape[-1]
    return call(
        halo_kernel,
        jax.ShapeDtypeStruct((height * width // 4, co), BF16),
        [
            pltpu.VMEM((height, width, chans), BF16),
            pltpu.VMEM((3, 3, chans, co), BF16),
            pltpu.VMEM((height * width + 16, chans), F32),
            pltpu.SemaphoreType.DMA((PLANE_PARTS + 3,)),
        ],
        [pl.BlockSpec(memory_space=pltpu.HBM)] * 2,
        VMEM_WHOLE,
    )(volume, kernel)


def preact_kernel(volume_ref, kernel_ref, preact_ref, even_ref, odd_ref, wide):
    planes, height, width, chans = volume_ref.shape[1:]
    cells = height * width // 4
    outs = planes // 2
    for plane in range(planes):
        even, odd = spread_plane(volume_ref[0, plane], wide)
        even_ref[plane] = even
        odd_ref[plane, pl.ds(0, 1)] = jnp.zeros_like(odd[:1])
        odd_ref[plane, pl.ds(1, height // 2)] = odd
    co = kernel_ref.shape[-1]
    total = None
    for kd in (1, 2):
        for kh in range(3):
            lhs = [tap_rows(even_ref, odd_ref, 2 * d - 1 + kd, kh) for d in range(outs)]
            rhs = kernel_ref[kd, kh].reshape(3 * chans, co)
            term = jnp.dot(jnp.concatenate(lhs, axis=0), rhs, preferred_element_type=F32)
            total = term if total is None else total + term
    preact_ref[...] = total
    if outs > 1:
        total = preact_ref[pl.ds(cells, (outs - 1) * cells), :]
        for kh in range(3):
            lhs = [tap_rows(even_ref, odd_ref, 2 * d - 1, kh) for d in range(1, outs)]
            rhs = kernel_ref[0, kh].reshape(3 * chans, co)
            total += jnp.dot(jnp.concatenate(lhs, axis=0), rhs, preferred_element_type=F32)
        preact_ref[pl.ds(cells, (outs - 1) * cells), :] = total


def partial_preact(volume, kernel):
    _, planes, height, width, chans = volume.shape
    co = kernel.shape[-1]
    cells = height * width // 4
    h2, w2 = height // 2, width // 2
    return call(
        preact_kernel,
        (
            jax.ShapeDtypeStruct((planes // 2 * cells, co), F32),
            jax.ShapeDtypeStruct((planes, h2, w2, 3 * chans), BF16),
            jax.ShapeDtypeStruct((planes, h2 + 1, w2, 3 * chans), BF16),
        ),
        [pltpu.VMEM((height * width + 16, chans), F32)],
    )(volume, kernel)


def activation_kernel(space, cores, start, preact_ref, cotangent_ref, *refs):
    grad_ref, flipped_ref = refs[-2:]
    share_ref = refs[0] if len(refs) == 3 else None
    co = preact_ref.shape[1]
    count = grad_ref.shape[0]
    group, strips = co // space, flipped_ref.shape[1]
    rows = pl.ds(start, count)
    value = preact_ref[rows, :]
    if share_ref is not None:
        value = value + share_ref[...].astype(F32)
    sig = jax.nn.sigmoid(value)
    slope = sig * (1.0 + value * (1.0 - sig))
    grad_ref[...] = (cotangent_ref[rows, :].astype(F32) * slope).astype(BF16)
    flipped = (value * sig).T.astype(BF16)
    for target in range(space):
        place = staged_place(target, space, cores)
        for strip in range(strips):
            flipped_ref[place, strip] = flipped[
                target * group : (target + 1) * group, strip * 128 : (strip + 1) * 128
            ]


def activation(preact, cotangent, share, start, count, space, cores):
    co = preact.shape[1]
    return call(
        functools.partial(activation_kernel, space, cores, start),
        (
            jax.ShapeDtypeStruct((count, co), BF16),
            jax.ShapeDtypeStruct((space, count // 128, co // space, 128), BF16),
        ),
    )(preact, cotangent, *(() if share is None else (share,)))


def switched_kernel(space, cores, came, kept_ref, got_ref, out_ref, done_ref):
    done_ref[...] = jnp.zeros_like(done_ref)
    half = space // 2
    rows = kept_ref.shape[1]
    strips = kept_ref.shape[0] // half
    for source in range(space):
        place = relative_place(source, space, cores)
        far = place // half
        for strip in range(strips):
            column = (source * strips + strip) * 128
            row = (place % half) * strips + strip
            there = got_ref[pl.ds(pl.multiple_of(came + row * rows, rows), rows), :]
            out_ref[:, column : column + 128] = jnp.where(far == 1, there, kept_ref[row])


def switched_of(kept, got, came, space, cores, order):
    group = kept.shape[-2]
    kept = kept.reshape(-1, group, 128)
    return call(
        functools.partial(switched_kernel, space, cores, came),
        (
            jax.ShapeDtypeStruct((group, 2 * kept.shape[0] * 128), BF16),
            jax.ShapeDtypeStruct(DONE, F32),
        ),
        order=order,
        inputs=2,
    )(kept, got, *order)


def side(axis, stage, cores):
    if axis == "chips":
        return (lax.axis_index("dp") // cores >> stage) & 1
    bits = bits_of(lax.axis_size("space"))
    index = lax.axis_index("space")
    return jnp.where(odd_core(cores), (index >> (bits - 1 - stage)) & 1, (index >> stage) & 1)


def halves_of(shape, axis):
    units, chips = shape[:2]
    lead = (1, 2, units // 2 * chips) if axis == "space" else (units * chips // 2, 2, 1)
    return lead + tuple(shape[2:])


def half_shape(shape, axis):
    units, chips = shape[:2]
    return ((units // 2, chips) if axis == "space" else (units, chips // 2)) + tuple(shape[2:])


def add_kernel(now, then, cores, value_ref, *refs):
    outs = 1 if then is None else 2
    got = jnp.concatenate([ref[...] for ref in refs[:-outs]], axis=0).astype(F32)
    total = value_ref[...] if now is None else value_ref[:, side(*now, cores)]
    total = total.reshape(got.shape) + got
    if then is None:
        refs[-1][...] = total.astype(BF16)
        return
    keep_ref, sent_ref = refs[-2:]
    keep_ref[...] = total.reshape(keep_ref.shape)
    sent_ref[...] = keep_ref[:, 1 - side(*then, cores)].reshape(sent_ref.shape).astype(BF16)


def add_stage(value, got, now, then, cores, order=(), flops=1000):
    shape = (sum(piece.shape[0] for piece in got),) + got[0].shape[1:]
    if then is None:
        outs = jax.ShapeDtypeStruct(shape, BF16)
    else:
        outs = (
            jax.ShapeDtypeStruct(halves_of(shape, then[0]), F32),
            jax.ShapeDtypeStruct(half_shape(shape, then[0]), BF16),
        )
    return call(
        functools.partial(add_kernel, now, then, cores),
        outs,
        order=order,
        inputs=1 + len(got),
        flops=flops,
    )(value, *got, *order)


def switch_kernel(stage, cores, came, first_ref, *refs):
    stay_ref, out_ref = refs[-2:]
    refs = list(refs[:-2])
    bit = side("space", stage, cores)
    sources, _, targets, strips, rows, lanes = first_ref.shape
    half = targets * strips * rows
    if came is None:
        ahead = out_ref.shape[0] - sources * half
    else:
        ahead = out_ref.shape[0] - 2 * sources * half
    rider = refs.pop() if ahead else None
    if rider is not None:
        out_ref[pl.ds(0, ahead), :] = rider[...]
    place = ahead
    for source in range(sources):
        stay_ref[source] = first_ref[source, bit]
        out_ref[pl.ds(place, half), :] = first_ref[source, 1 - bit].reshape(half, lanes)
        place += half
    if came is not None:
        got_ref = refs[0]
        for source in range(sources):
            base = came + source * 2 * half
            mine = got_ref[pl.ds(pl.multiple_of(base + bit * half, rows), half), :]
            stay_ref[sources + source] = mine.reshape(targets, strips, rows, lanes)
            out_ref[pl.ds(place, half), :] = got_ref[
                pl.ds(pl.multiple_of(base + (1 - bit) * half, rows), half), :
            ]
            place += half


def switch_stage(first, got, came, rider, stage, cores, order):
    sources, targets, strips, rows, lanes = first.shape
    operands = (first.reshape(sources, 2, targets // 2, strips, rows, lanes),)
    total = sources * (1 if got is None else 2)
    count = total * targets // 2 * strips * rows
    if got is not None:
        operands += (got,)
    if rider is not None:
        operands += (rider.reshape(-1, lanes),)
        count += operands[-1].shape[0]
    return call(
        functools.partial(switch_kernel, stage, cores, None if got is None else came),
        (
            jax.ShapeDtypeStruct((total, targets // 2, strips, rows, lanes), BF16),
            jax.ShapeDtypeStruct((count, lanes), BF16),
        ),
        order=order,
        inputs=len(operands),
    )(*operands, *order)


def gather_kernel(early, mine_ref, got_ref, out_ref):
    rows = pl.ds(early, mine_ref.shape[0] - early)
    out_ref[pl.ds(0, early)] = mine_ref[pl.ds(0, early)]
    out_ref[pl.ds(early, early)] = got_ref[pl.ds(0, early)]
    total = mine_ref[rows].astype(F32) + got_ref[rows].astype(F32)
    out_ref[pl.ds(2 * early, total.shape[0])] = total.astype(BF16)


def gather_stage(mine, got, early, order=()):
    return call(
        functools.partial(gather_kernel, early),
        jax.ShapeDtypeStruct((mine.shape[0] + early,) + mine.shape[1:], BF16),
        order=order,
        inputs=2,
    )(mine, got, *order)


def join_kernel(now, cores, value_ref, got_ref, late_ref, out_ref):
    total = value_ref[:, side(*now, cores)].reshape(got_ref.shape) + got_ref[...].astype(F32)
    early = total.shape[0]
    out_ref[pl.ds(0, early)] = total.reshape((early,) + out_ref.shape[1:]).astype(BF16)
    out_ref[pl.ds(early, late_ref.shape[0])] = late_ref[...].reshape((-1,) + out_ref.shape[1:])


def join(value, got, late, now, cores, order):
    shape = (got.shape[0] + late.shape[0],) + got.shape[2:]
    return call(
        functools.partial(join_kernel, now, cores),
        jax.ShapeDtypeStruct(shape, BF16),
        order=order,
        inputs=3,
        flops=SPACER,
    )(value, got, late, *order)


def kernel_grad_out_kernel(space, cores, early_units, late_units, mine_ref, got_ref, out_ref):
    halves = out_ref.shape[-1] // 128
    half = space // 2
    share = -(-early_units // space)

    def put(index, value):
        tap, part = divmod(index, halves)
        out_ref[tap, :, part * 128 : (part + 1) * 128] = value

    for unit in range(late_units):
        row = half * share + unit
        put(unit, mine_ref[row].astype(F32) + got_ref[row].astype(F32))
    for group in range(space):
        place = relative_group(group, space, cores)
        far, row = place // half, (place % half) * share
        for unit in range(share):
            index = group * share + unit
            if index < early_units:
                value = jnp.where(far == 1, got_ref[row + unit], mine_ref[row + unit])
                put(late_units + index, value.astype(F32))


def kernel_grad_out(mine, got, early_units, late_units, space, cores, co, order):
    taps = (early_units + late_units) * 128 // co
    return call(
        functools.partial(kernel_grad_out_kernel, space, cores, early_units, late_units),
        jax.ShapeDtypeStruct((taps, mine.shape[1], co), F32),
        order=order,
        inputs=2,
    )(mine, got, *order)


def store_units(product, scale, core, cores, chips, put):
    chans = product.shape[0] // 3
    co = product.shape[1]
    block = chans // (cores * chips)
    halves = co // 128
    product = product * scale
    for kw in range(3):
        for half in range(halves):
            unit = product[kw * chans : (kw + 1) * chans, half * 128 : (half + 1) * 128]
            unit = unit.reshape(chips, cores, block, 128)
            for chip in range(chips):
                first = unit[chip, 0]
                last = unit[chip, cores - 1]
                keep = jnp.where(core == 0, first, last)
                send = jnp.where(core == 0, last, first)
                put(kw * halves + half, chip, keep, send)


def tap_products(even_ref, odd_ref, planes, rhs, put):
    for kh in range(3):
        lhs = [tap_rows(even_ref, odd_ref, plane, kh) for plane in planes]
        put(
            kh,
            lax.dot_general(
                jnp.concatenate(lhs, axis=0), rhs, (((0,), (0,)), ((), ())), preferred_element_type=F32
            ),
        )


def ahead_kernel(even_ref, odd_ref, rest_ref, out_ref):
    outs = even_ref.shape[0] // 2
    for place, kd in enumerate((1, 2)):
        planes = [2 * d - 1 + kd for d in range(1, outs)]

        def put(kh, product, base=3 * place):
            out_ref[base + kh] = product

        tap_products(even_ref, odd_ref, planes, rest_ref[...], put)


def early_ahead(even, odd, rest):
    return call(
        ahead_kernel, jax.ShapeDtypeStruct((6, even.shape[-1], rest.shape[-1]), F32)
    )(even, odd, rest)


def kernel_grad_kernel(early, cores, chips, scale, even_ref, odd_ref, grads_ref, other_ref, keep_ref, send_ref):
    outs = even_ref.shape[0] // 2
    core = lax.axis_index("dp") % cores
    per_row = 3 * (grads_ref.shape[1] // 128)
    kds = (1, 2) if early else (0,)
    for unit in range(len(kds) * 3 * per_row, keep_ref.shape[0]):
        keep_ref[unit] = jnp.zeros(keep_ref.shape[1:], F32)
        send_ref[unit] = jnp.zeros(keep_ref.shape[1:], BF16)
    for place, kd in enumerate(kds):
        if early:
            planes, rhs = [kd - 1], grads_ref[...]
        else:
            planes = [2 * d - 1 for d in range(1, outs + 1)]
            rhs = jnp.concatenate([grads_ref[...], other_ref[...]], axis=0)

        def take(kh, product, base=3 * place):
            if early:
                product = product + other_ref[base + kh]

            def put(unit, chip, keep, send):
                keep_ref[(base + kh) * per_row + unit, chip] = keep
                send_ref[(base + kh) * per_row + unit, chip] = send.astype(BF16)

            store_units(product, scale, core, cores, chips, put)

        tap_products(even_ref, odd_ref, planes, rhs, take)


def kernel_grad_part(even, odd, grads, other, early, cores, chips, scale, multiple, order=()):
    chans = even.shape[-1] // 3
    units = (18 if early else 9) * (grads.shape[-1] // 128)
    units += -units % multiple
    shape = (units, chips, chans // (cores * chips), 128)
    return call(
        functools.partial(kernel_grad_kernel, early, cores, chips, scale),
        (jax.ShapeDtypeStruct(shape, F32), jax.ShapeDtypeStruct(shape, BF16)),
        order=order,
        inputs=4,
    )(even, odd, grads, other, *order)


def volume_grad_kernel(first_ref, rest_ref, above_ref, kernel_ref, out_ref, done_ref, shifted, wide):
    done_ref[...] = jnp.zeros_like(done_ref)
    planes, h2, _, width, chans = out_ref.shape
    w2 = width // 2
    cells = h2 * w2
    outs = planes // 2
    co = first_ref.shape[1]
    here, right = [], []
    for d in range(outs + 1):
        if 0 < d < outs:
            plane = rest_ref[pl.ds((d - 1) * cells, cells), :]
        else:
            plane = (first_ref if d == 0 else above_ref)[...]
        shifted[pl.ds(0, cells), :] = plane.astype(F32)
        moved = shifted[pl.ds(1, cells), :]
        column = lax.broadcasted_iota(jnp.int32, moved.shape, 0) % w2
        moved = jnp.where(column == w2 - 1, 0.0, moved).astype(BF16)
        here.append(plane)
        right.append(moved)

    def down(rows):
        return jnp.concatenate([rows[w2:], jnp.zeros((w2, co), BF16)], axis=0)

    contract = (((1,), (1,)), ((), ()))
    for plane in range(planes):
        d = plane // 2
        depth = [(1, d)] if plane % 2 == 0 else [(2, d), (0, d + 1)]
        for odd_row in range(2):
            taps = [(1, False)] if odd_row == 0 else [(2, False), (0, True)]
            both, right_only = None, None
            for kd, source in depth:
                for kh, lower in taps:
                    lhs = down(here[source]) if lower else here[source]
                    rhs = kernel_ref[kd, kh, pl.ds(1, 2)].reshape(2 * chans, co)
                    term = lax.dot_general(lhs, rhs, contract, preferred_element_type=F32)
                    both = term if both is None else both + term
                    lhs = down(right[source]) if lower else right[source]
                    term = lax.dot_general(lhs, kernel_ref[kd, kh, 0], contract, preferred_element_type=F32)
                    right_only = term if right_only is None else right_only + term
            wide[pl.ds(0, cells, stride=2), :] = both[:, :chans]
            wide[pl.ds(1, cells, stride=2), :] = both[:, chans:] + right_only
            out_ref[plane, :, odd_row] = wide[...].reshape(h2, width, chans).astype(BF16)


def volume_grad_of(first, rest, above, kernel, height, width, order=()):
    cells, co = first.shape[0] + rest.shape[0], first.shape[1]
    chans = kernel.shape[3]
    planes = 2 * cells * 4 // (height * width)
    shape = (planes, height // 2, 2, width, chans)
    return call(
        volume_grad_kernel,
        (jax.ShapeDtypeStruct(shape, BF16), jax.ShapeDtypeStruct(DONE, F32)),
        [
            pltpu.VMEM((height * width // 4 + 8, co), F32),
            pltpu.VMEM((height * width // 2, chans), F32),
        ],
        order=order,
        inputs=4,
    )(first, rest, above, kernel, *order)


def exchange(value, partner):
    dp, space = lax.axis_size("dp"), lax.axis_size("space")
    pairs = []
    for i in range(dp):
        for j in range(space):
            to_dp, to_space = partner(i, j)
            pairs.append((i * space + j, to_dp * space + to_space))
    return lax.ppermute(value, ("dp", "space"), pairs)


def exchange_space(value, stage, cores):
    bits = bits_of(lax.axis_size("space"))

    def partner(i, j):
        bit = bits - 1 - stage if cores == 2 and i % 2 == 1 else stage
        return i, j ^ (1 << bit)

    return exchange(value, partner)


def exchange_chips(value, bit, cores):
    return exchange(value, lambda i, j: (i ^ (cores << bit), j))


def neighbour(value, steps):
    count = lax.axis_size("space")
    first, last = (max(0, -steps), min(count, count - steps))
    return lax.ppermute(value, "space", [(source, source + steps) for source in range(first, last)])


def exchange_stage(value, axis, stage, cores):
    return exchange_space(value, stage, cores) if axis == "space" else exchange_chips(value, stage, cores)


def add_cores(keep, sends, then, cores, order=()):
    got = tuple(exchange(send, lambda i, j: (i ^ 1, j)) if cores == 2 else 0 * send for send in sends)
    return add_stage(keep, got, None, then, cores, order)


def body(volume, kernel, cotangent):
    samples, planes, height, width, ci = volume.shape
    co = kernel.shape[-1]
    assert samples == 1
    dp, space = lax.axis_size("dp"), lax.axis_size("space")
    cores = 2 if dp % 2 == 0 else 1
    chips = dp // cores
    outs = planes // 2
    cells = height * width // 4
    scale = 1.0 / math.sqrt(dp * space * samples * outs * cells)
    over_space = [("space", stage) for stage in range(bits_of(space))]
    over_chips = [("chips", stage) for stage in range(bits_of(chips))]

    share = neighbour(halo_share(volume, kernel), 1)
    preact, even, odd = partial_preact(volume, kernel)
    cotangent = cotangent.reshape(outs * cells, co)
    rest, flipped_rest = activation(preact, cotangent, None, cells, (outs - 1) * cells, space, cores)
    products = early_ahead(even, odd, rest)
    first, flipped = activation(preact, cotangent, share, 0, cells, space, cores)
    flipped = jnp.concatenate([flipped, flipped_rest], axis=1)
    above = neighbour(first, -1)

    early = kernel_grad_part(even, odd, first, products, True, cores, chips, scale, space)
    early_units, late_units = 18 * (co // 128), 9 * (co // 128)
    plan = over_space + over_chips
    value, sent = add_cores(early[0], early[1:], plan[0], cores)
    late_plan, late_now, late_half = list(over_chips), None, None
    switch_at = [len(over_space) - 1 + 2 * stage for stage in range(len(over_space))]
    stay, moved = flipped[None], None
    for place, now in enumerate(plan):
        got = exchange_stage(sent, *now, cores)
        tokens = [sent]
        if place == 0:
            late = kernel_grad_part(even, odd, rest, above, False, cores, chips, scale, 1, (sent,))
            tokens.append(late[1])
        elif late_half is None:
            then = late_plan.pop(0) if late_plan else None
            if late_now is None:
                result = add_cores(late[0], late[1:], then, cores, (sent,))
            else:
                result = add_stage(late_value, late_got, late_now, then, cores, (sent,))
            late_now = then
            if then is None:
                late_half = result
            else:
                late_value, late_sent = result
                late_got = (exchange_stage(late_sent, *then, cores),)
                tokens.append(late_sent)
        if switch_at and place == switch_at[0]:
            stage = len(over_space) - len(switch_at)
            switch_at.pop(0)
            stay, out = switch_stage(stay, moved, 0, None, stage, cores, (tokens[-1],))
            moved = exchange_space(out, stage, cores)
            tokens.append(out)
        if place + 1 < len(plan):
            weight = SPACER if place >= len(over_space) else 1000
            value, sent = add_stage(
                value, (got,), now, plan[place + 1], cores, tuple(tokens[1:]), weight
            )
    for stage in range(len(over_space) - len(switch_at), len(over_space)):
        stay, out = switch_stage(stay, moved, 0, None, stage, cores, (sent,))
        moved = exchange_space(out, stage, cores)
    if late_half is None:
        late_half = add_stage(late_value, late_got, late_now, None, cores)

    mine = join(value, got, late_half, plan[-1], cores, tuple(tokens[1:]))
    early_rows = mine.shape[0] - late_half.shape[0]
    switched = None
    for step, (_, stage) in enumerate(reversed(over_space)):
        got = exchange_space(mine, stage, cores)
        order = ()
        if switched is None:
            switched, done = switched_of(stay, moved, 0, space, cores, (mine,))
            order = (done,)
        if step + 1 < len(over_space):
            mine = gather_stage(mine, got, early_rows << step, order)
    volume_grad, done = volume_grad_of(first, rest, above, kernel, height, width, (mine,))
    kernel_grad = kernel_grad_out(mine, got, early_units, late_units, space, cores, co, (done,))

    return (
        switched[None],
        volume_grad.reshape(volume.shape),
        kernel_grad.reshape(3, 3, 3, ci // dp, co),
    )


def solution(mesh):
    in_specs = (P("dp", "space", None, None, None), P(), P("dp", "space", None, None, None))
    out_specs = (
        P("dp", "space", None),
        P("dp", "space", None, None, None),
        P(None, None, None, "dp", None),
    )
    return jax.shard_map(body, mesh=mesh, in_specs=in_specs, out_specs=out_specs, check_vma=False)
```

```python
import functools
import math

import jax
import jax.numpy as jnp
from jax import lax
from jax.experimental import pallas as pl
from jax.experimental.pallas import tpu as pltpu
from jax.sharding import PartitionSpec as P

BF16 = jnp.bfloat16
F32 = jnp.float32
VMEM_LIMIT = 20 * 1024 * 1024
DONE = (8, 128)
PLANE_PARTS = 1
SPACER = 6 * 10**9
VMEM_WHOLE = 60 * 1024 * 1024


def call(kernel, out_shape, scratch=(), in_specs=None, limit=VMEM_LIMIT, order=(), inputs=0, flops=1000):
    extra = {} if in_specs is None else {"in_specs": in_specs}
    if order:
        whole = pl.BlockSpec(memory_space=pltpu.VMEM)
        extra["in_specs"] = [whole] * inputs + [pl.BlockSpec(memory_space=pl.ANY)] * len(order)
        inner, count = kernel, len(order)

        def kernel(*refs):
            inner(*refs[:inputs], *refs[inputs + count :])

    return pl.pallas_call(
        kernel,
        out_shape=out_shape,
        scratch_shapes=list(scratch),
        compiler_params=pltpu.CompilerParams(vmem_limit_bytes=limit),
        cost_estimate=pl.CostEstimate(flops=flops, bytes_accessed=1000, transcendentals=0),
        **extra,
    )


def spread_plane(plane, wide):
    height, width, chans = plane.shape
    cells = height * width
    half = width // 2
    wide[pl.ds(8, cells), :] = plane.reshape(cells, chans).astype(F32)
    left = wide[pl.ds(7, cells // 2, stride=2), :]
    even = wide[pl.ds(8, cells // 2, stride=2), :]
    odd = wide[pl.ds(9, cells // 2, stride=2), :]
    column = lax.broadcasted_iota(jnp.int32, left.shape, 0) % half
    left = jnp.where(column == 0, 0.0, left)
    joined = jnp.concatenate([left.astype(BF16), even.astype(BF16), odd.astype(BF16)], axis=1)
    joined = joined.reshape(height // 2, 2, half, 3 * chans)
    return joined[:, 0], joined[:, 1]


def tap_rows(even, odd, plane, kh):
    height = even.shape[1]
    picked = even[plane] if kh == 1 else odd[plane, pl.ds(0 if kh == 0 else 1, height)]
    return picked.reshape(height * even.shape[2], even.shape[3])


def bits_of(count):
    bits = count.bit_length() - 1
    assert 1 << bits == count
    return bits


def far_first(cores):
    return lax.axis_index("dp") % cores == 0 if cores == 2 else False


def reverse_bits(value, bits):
    return sum(((value >> bit) & 1) << (bits - 1 - bit) for bit in range(bits))


def staged_place(target, space, cores):
    return jnp.where(far_first(cores), target, reverse_bits(target, bits_of(space)))


def relative_place(source, space, cores):
    bits = bits_of(space)
    off = source ^ lax.axis_index("space")
    return jnp.where(far_first(cores), reverse_bits(off, bits), off)


def relative_group(group, space, cores):
    bits = bits_of(space)
    index = lax.axis_index("space")
    mine = jnp.where(far_first(cores), index, reverse_bits(index, bits))
    return group ^ mine


def halo_kernel(volume_ref, kernel_ref, share_ref, plane, weights, wide, sems):
    planes, height, width, chans = volume_ref.shape[1:]
    part = height // PLANE_PARTS
    rows = [pl.ds(index * part, part) for index in range(PLANE_PARTS)]
    copies = [
        pltpu.make_async_copy(volume_ref.at[0, planes - 1, row], plane.at[row], sems.at[index])
        for index, row in enumerate(rows)
    ]
    loads = [
        pltpu.make_async_copy(kernel_ref.at[0, kh], weights.at[kh], sems.at[PLANE_PARTS + kh])
        for kh in range(3)
    ]
    for copy in copies + loads:
        copy.start()
    for copy in copies:
        copy.wait()
    even, odd = spread_plane(plane[...], wide)
    above = jnp.concatenate([jnp.zeros_like(odd[:1]), odd[:-1]], axis=0)
    total = None
    for kh, rows in enumerate((above, even, odd)):
        loads[kh].wait()
        lhs = rows.reshape(height * width // 4, 3 * chans)
        rhs = weights[kh].reshape(3 * chans, weights.shape[-1])
        term = jnp.dot(lhs, rhs, preferred_element_type=F32)
        total = term if total is None else total + term
    share_ref[...] = total.astype(BF16)


def halo_share(volume, kernel):
    _, planes, height, width, chans = volume.shape
    co = kernel.shape[-1]
    return call(
        halo_kernel,
        jax.ShapeDtypeStruct((height * width // 4, co), BF16),
        [
            pltpu.VMEM((height, width, chans), BF16),
            pltpu.VMEM((3, 3, chans, co), BF16),
            pltpu.VMEM((height * width + 16, chans), F32),
            pltpu.SemaphoreType.DMA((PLANE_PARTS + 3,)),
        ],
        [pl.BlockSpec(memory_space=pltpu.HBM)] * 2,
        VMEM_WHOLE,
    )(volume, kernel)


def preact_kernel(volume_ref, kernel_ref, preact_ref, even_ref, odd_ref, wide):
    planes, height, width, chans = volume_ref.shape[1:]
    cells = height * width // 4
    outs = planes // 2
    for plane in range(planes):
        even, odd = spread_plane(volume_ref[0, plane], wide)
        even_ref[plane] = even
        odd_ref[plane, pl.ds(0, 1)] = jnp.zeros_like(odd[:1])
        odd_ref[plane, pl.ds(1, height // 2)] = odd
    co = kernel_ref.shape[-1]
    total = None
    for kd in (1, 2):
        for kh in range(3):
            lhs = [tap_rows(even_ref, odd_ref, 2 * d - 1 + kd, kh) for d in range(outs)]
            rhs = kernel_ref[kd, kh].reshape(3 * chans, co)
            term = jnp.dot(jnp.concatenate(lhs, axis=0), rhs, preferred_element_type=F32)
            total = term if total is None else total + term
    preact_ref[...] = total
    if outs > 1:
        total = preact_ref[pl.ds(cells, (outs - 1) * cells), :]
        for kh in range(3):
            lhs = [tap_rows(even_ref, odd_ref, 2 * d - 1, kh) for d in range(1, outs)]
            rhs = kernel_ref[0, kh].reshape(3 * chans, co)
            total += jnp.dot(jnp.concatenate(lhs, axis=0), rhs, preferred_element_type=F32)
        preact_ref[pl.ds(cells, (outs - 1) * cells), :] = total


def partial_preact(volume, kernel):
    _, planes, height, width, chans = volume.shape
    co = kernel.shape[-1]
    cells = height * width // 4
    h2, w2 = height // 2, width // 2
    return call(
        preact_kernel,
        (
            jax.ShapeDtypeStruct((planes // 2 * cells, co), F32),
            jax.ShapeDtypeStruct((planes, h2, w2, 3 * chans), BF16),
            jax.ShapeDtypeStruct((planes, h2 + 1, w2, 3 * chans), BF16),
        ),
        [pltpu.VMEM((height * width + 16, chans), F32)],
    )(volume, kernel)


def activation_kernel(space, cores, start, preact_ref, cotangent_ref, *refs):
    grad_ref, flipped_ref = refs[-2:]
    share_ref = refs[0] if len(refs) == 3 else None
    co = preact_ref.shape[1]
    count = grad_ref.shape[0]
    group, strips = co // space, flipped_ref.shape[1]
    rows = pl.ds(start, count)
    value = preact_ref[rows, :]
    if share_ref is not None:
        value = value + share_ref[...].astype(F32)
    sig = jax.nn.sigmoid(value)
    slope = sig * (1.0 + value * (1.0 - sig))
    grad_ref[...] = (cotangent_ref[rows, :].astype(F32) * slope).astype(BF16)
    flipped = (value * sig).T.astype(BF16)
    for target in range(space):
        place = staged_place(target, space, cores)
        for strip in range(strips):
            flipped_ref[place, strip] = flipped[
                target * group : (target + 1) * group, strip * 128 : (strip + 1) * 128
            ]


def activation(preact, cotangent, share, start, count, space, cores):
    co = preact.shape[1]
    return call(
        functools.partial(activation_kernel, space, cores, start),
        (
            jax.ShapeDtypeStruct((count, co), BF16),
            jax.ShapeDtypeStruct((space, count // 128, co // space, 128), BF16),
        ),
    )(preact, cotangent, *(() if share is None else (share,)))


def switched_kernel(space, cores, came, kept_ref, got_ref, out_ref, done_ref):
    done_ref[...] = jnp.zeros_like(done_ref)
    half = space // 2
    rows = kept_ref.shape[1]
    strips = kept_ref.shape[0] // half
    for source in range(space):
        place = relative_place(source, space, cores)
        far = place // half
        for strip in range(strips):
            column = (source * strips + strip) * 128
            row = (place % half) * strips + strip
            there = got_ref[pl.ds(pl.multiple_of(came + row * rows, rows), rows), :]
            out_ref[:, column : column + 128] = jnp.where(far == 1, there, kept_ref[row])


def switched_of(kept, got, came, space, cores, order):
    group = kept.shape[-2]
    kept = kept.reshape(-1, group, 128)
    return call(
        functools.partial(switched_kernel, space, cores, came),
        (
            jax.ShapeDtypeStruct((group, 2 * kept.shape[0] * 128), BF16),
            jax.ShapeDtypeStruct(DONE, F32),
        ),
        order=order,
        inputs=2,
    )(kept, got, *order)


def side(axis, stage, cores):
    if axis == "chips":
        return (lax.axis_index("dp") // cores >> stage) & 1
    bits = bits_of(lax.axis_size("space"))
    index = lax.axis_index("space")
    return jnp.where(far_first(cores), (index >> (bits - 1 - stage)) & 1, (index >> stage) & 1)


def halves_of(shape, axis):
    units, chips = shape[:2]
    lead = (1, 2, units // 2 * chips) if axis == "space" else (units * chips // 2, 2, 1)
    return lead + tuple(shape[2:])


def half_shape(shape, axis):
    units, chips = shape[:2]
    return ((units // 2, chips) if axis == "space" else (units, chips // 2)) + tuple(shape[2:])


def add_kernel(now, then, cores, value_ref, *refs):
    outs = 1 if then is None else 2
    got = jnp.concatenate([ref[...] for ref in refs[:-outs]], axis=0).astype(F32)
    total = value_ref[...] if now is None else value_ref[:, side(*now, cores)]
    total = total.reshape(got.shape) + got
    if then is None:
        refs[-1][...] = total.astype(BF16)
        return
    keep_ref, sent_ref = refs[-2:]
    keep_ref[...] = total.reshape(keep_ref.shape)
    sent_ref[...] = keep_ref[:, 1 - side(*then, cores)].reshape(sent_ref.shape).astype(BF16)


def add_stage(value, got, now, then, cores, order=(), flops=1000):
    shape = (sum(piece.shape[0] for piece in got),) + got[0].shape[1:]
    if then is None:
        outs = jax.ShapeDtypeStruct(shape, BF16)
    else:
        outs = (
            jax.ShapeDtypeStruct(halves_of(shape, then[0]), F32),
            jax.ShapeDtypeStruct(half_shape(shape, then[0]), BF16),
        )
    return call(
        functools.partial(add_kernel, now, then, cores),
        outs,
        order=order,
        inputs=1 + len(got),
        flops=flops,
    )(value, *got, *order)


def switch_kernel(stage, cores, came, first_ref, *refs):
    stay_ref, out_ref = refs[-2:]
    refs = list(refs[:-2])
    bit = side("space", stage, cores)
    sources, _, targets, strips, rows, lanes = first_ref.shape
    half = targets * strips * rows
    if came is None:
        ahead = out_ref.shape[0] - sources * half
    else:
        ahead = out_ref.shape[0] - 2 * sources * half
    rider = refs.pop() if ahead else None
    if rider is not None:
        out_ref[pl.ds(0, ahead), :] = rider[...]
    place = ahead
    for source in range(sources):
        stay_ref[source] = first_ref[source, bit]
        out_ref[pl.ds(place, half), :] = first_ref[source, 1 - bit].reshape(half, lanes)
        place += half
    if came is not None:
        got_ref = refs[0]
        for source in range(sources):
            base = came + source * 2 * half
            mine = got_ref[pl.ds(pl.multiple_of(base + bit * half, rows), half), :]
            stay_ref[sources + source] = mine.reshape(targets, strips, rows, lanes)
            out_ref[pl.ds(place, half), :] = got_ref[
                pl.ds(pl.multiple_of(base + (1 - bit) * half, rows), half), :
            ]
            place += half


def switch_stage(first, got, came, rider, stage, cores, order):
    sources, targets, strips, rows, lanes = first.shape
    operands = (first.reshape(sources, 2, targets // 2, strips, rows, lanes),)
    total = sources * (1 if got is None else 2)
    count = total * targets // 2 * strips * rows
    if got is not None:
        operands += (got,)
    if rider is not None:
        operands += (rider.reshape(-1, lanes),)
        count += operands[-1].shape[0]
    return call(
        functools.partial(switch_kernel, stage, cores, None if got is None else came),
        (
            jax.ShapeDtypeStruct((total, targets // 2, strips, rows, lanes), BF16),
            jax.ShapeDtypeStruct((count, lanes), BF16),
        ),
        order=order,
        inputs=len(operands),
    )(*operands, *order)


def gather_kernel(early, mine_ref, got_ref, out_ref):
    rows = pl.ds(early, mine_ref.shape[0] - early)
    out_ref[pl.ds(0, early)] = mine_ref[pl.ds(0, early)]
    out_ref[pl.ds(early, early)] = got_ref[pl.ds(0, early)]
    total = mine_ref[rows].astype(F32) + got_ref[rows].astype(F32)
    out_ref[pl.ds(2 * early, total.shape[0])] = total.astype(BF16)


def gather_stage(mine, got, early, order=()):
    return call(
        functools.partial(gather_kernel, early),
        jax.ShapeDtypeStruct((mine.shape[0] + early,) + mine.shape[1:], BF16),
        order=order,
        inputs=2,
    )(mine, got, *order)


def join_kernel(now, cores, value_ref, got_ref, late_ref, out_ref):
    total = value_ref[:, side(*now, cores)].reshape(got_ref.shape) + got_ref[...].astype(F32)
    early = total.shape[0]
    out_ref[pl.ds(0, early)] = total.reshape((early,) + out_ref.shape[1:]).astype(BF16)
    out_ref[pl.ds(early, late_ref.shape[0])] = late_ref[...].reshape((-1,) + out_ref.shape[1:])


def join(value, got, late, now, cores, order):
    shape = (got.shape[0] + late.shape[0],) + got.shape[2:]
    return call(
        functools.partial(join_kernel, now, cores),
        jax.ShapeDtypeStruct(shape, BF16),
        order=order,
        inputs=3,
        flops=SPACER,
    )(value, got, late, *order)


def kernel_grad_out_kernel(space, cores, early_units, late_units, mine_ref, got_ref, out_ref):
    halves = out_ref.shape[-1] // 128
    half = space // 2
    share = -(-early_units // space)

    def put(index, value):
        tap, part = divmod(index, halves)
        out_ref[tap, :, part * 128 : (part + 1) * 128] = value

    for unit in range(late_units):
        row = half * share + unit
        put(unit, mine_ref[row].astype(F32) + got_ref[row].astype(F32))
    for group in range(space):
        place = relative_group(group, space, cores)
        far, row = place // half, (place % half) * share
        for unit in range(share):
            index = group * share + unit
            if index < early_units:
                value = jnp.where(far == 1, got_ref[row + unit], mine_ref[row + unit])
                put(late_units + index, value.astype(F32))


def kernel_grad_out(mine, got, early_units, late_units, space, cores, co, order):
    taps = (early_units + late_units) * 128 // co
    return call(
        functools.partial(kernel_grad_out_kernel, space, cores, early_units, late_units),
        jax.ShapeDtypeStruct((taps, mine.shape[1], co), F32),
        order=order,
        inputs=2,
    )(mine, got, *order)


def store_units(product, scale, core, cores, chips, put):
    chans = product.shape[0] // 3
    co = product.shape[1]
    block = chans // (cores * chips)
    halves = co // 128
    product = product * scale
    for kw in range(3):
        for half in range(halves):
            unit = product[kw * chans : (kw + 1) * chans, half * 128 : (half + 1) * 128]
            unit = unit.reshape(chips, cores, block, 128)
            for chip in range(chips):
                first = unit[chip, 0]
                last = unit[chip, cores - 1]
                keep = jnp.where(core == 0, first, last)
                send = jnp.where(core == 0, last, first)
                put(kw * halves + half, chip, keep, send)


def tap_products(even_ref, odd_ref, planes, rhs, put):
    for kh in range(3):
        lhs = [tap_rows(even_ref, odd_ref, plane, kh) for plane in planes]
        put(
            kh,
            lax.dot_general(
                jnp.concatenate(lhs, axis=0), rhs, (((0,), (0,)), ((), ())), preferred_element_type=F32
            ),
        )


def ahead_kernel(even_ref, odd_ref, rest_ref, out_ref):
    outs = even_ref.shape[0] // 2
    for place, kd in enumerate((1, 2)):
        planes = [2 * d - 1 + kd for d in range(1, outs)]

        def put(kh, product, base=3 * place):
            out_ref[base + kh] = product

        tap_products(even_ref, odd_ref, planes, rest_ref[...], put)


def early_ahead(even, odd, rest):
    return call(
        ahead_kernel, jax.ShapeDtypeStruct((6, even.shape[-1], rest.shape[-1]), F32)
    )(even, odd, rest)


def kernel_grad_kernel(early, cores, chips, scale, even_ref, odd_ref, grads_ref, other_ref, keep_ref, send_ref):
    outs = even_ref.shape[0] // 2
    core = lax.axis_index("dp") % cores
    per_row = 3 * (grads_ref.shape[1] // 128)
    kds = (1, 2) if early else (0,)
    for unit in range(len(kds) * 3 * per_row, keep_ref.shape[0]):
        keep_ref[unit] = jnp.zeros(keep_ref.shape[1:], F32)
        send_ref[unit] = jnp.zeros(keep_ref.shape[1:], BF16)
    for place, kd in enumerate(kds):
        if early:
            planes, rhs = [kd - 1], grads_ref[...]
        else:
            planes = [2 * d - 1 for d in range(1, outs + 1)]
            rhs = jnp.concatenate([grads_ref[...], other_ref[...]], axis=0)

        def take(kh, product, base=3 * place):
            if early:
                product = product + other_ref[base + kh]

            def put(unit, chip, keep, send):
                keep_ref[(base + kh) * per_row + unit, chip] = keep
                send_ref[(base + kh) * per_row + unit, chip] = send.astype(BF16)

            store_units(product, scale, core, cores, chips, put)

        tap_products(even_ref, odd_ref, planes, rhs, take)


def kernel_grad_part(even, odd, grads, other, early, cores, chips, scale, multiple, order=()):
    chans = even.shape[-1] // 3
    units = (18 if early else 9) * (grads.shape[-1] // 128)
    units += -units % multiple
    shape = (units, chips, chans // (cores * chips), 128)
    return call(
        functools.partial(kernel_grad_kernel, early, cores, chips, scale),
        (jax.ShapeDtypeStruct(shape, F32), jax.ShapeDtypeStruct(shape, BF16)),
        order=order,
        inputs=4,
    )(even, odd, grads, other, *order)


def volume_grad_kernel(first_ref, rest_ref, above_ref, kernel_ref, out_ref, done_ref, shifted, wide):
    done_ref[...] = jnp.zeros_like(done_ref)
    planes, h2, _, width, chans = out_ref.shape
    w2 = width // 2
    cells = h2 * w2
    outs = planes // 2
    co = first_ref.shape[1]
    here, right = [], []
    for d in range(outs + 1):
        if 0 < d < outs:
            plane = rest_ref[pl.ds((d - 1) * cells, cells), :]
        else:
            plane = (first_ref if d == 0 else above_ref)[...]
        shifted[pl.ds(0, cells), :] = plane.astype(F32)
        moved = shifted[pl.ds(1, cells), :]
        column = lax.broadcasted_iota(jnp.int32, moved.shape, 0) % w2
        moved = jnp.where(column == w2 - 1, 0.0, moved).astype(BF16)
        here.append(plane)
        right.append(moved)

    def down(rows):
        return jnp.concatenate([rows[w2:], jnp.zeros((w2, co), BF16)], axis=0)

    contract = (((1,), (1,)), ((), ()))
    for plane in range(planes):
        d = plane // 2
        depth = [(1, d)] if plane % 2 == 0 else [(2, d), (0, d + 1)]
        for odd_row in range(2):
            taps = [(1, False)] if odd_row == 0 else [(2, False), (0, True)]
            both, right_only = None, None
            for kd, source in depth:
                for kh, lower in taps:
                    lhs = down(here[source]) if lower else here[source]
                    rhs = kernel_ref[kd, kh, pl.ds(1, 2)].reshape(2 * chans, co)
                    term = lax.dot_general(lhs, rhs, contract, preferred_element_type=F32)
                    both = term if both is None else both + term
                    lhs = down(right[source]) if lower else right[source]
                    term = lax.dot_general(lhs, kernel_ref[kd, kh, 0], contract, preferred_element_type=F32)
                    right_only = term if right_only is None else right_only + term
            wide[pl.ds(0, cells, stride=2), :] = both[:, :chans]
            wide[pl.ds(1, cells, stride=2), :] = both[:, chans:] + right_only
            out_ref[plane, :, odd_row] = wide[...].reshape(h2, width, chans).astype(BF16)


def volume_grad_of(first, rest, above, kernel, height, width, order=()):
    cells, co = first.shape[0] + rest.shape[0], first.shape[1]
    chans = kernel.shape[3]
    planes = 2 * cells * 4 // (height * width)
    shape = (planes, height // 2, 2, width, chans)
    return call(
        volume_grad_kernel,
        (jax.ShapeDtypeStruct(shape, BF16), jax.ShapeDtypeStruct(DONE, F32)),
        [
            pltpu.VMEM((height * width // 4 + 8, co), F32),
            pltpu.VMEM((height * width // 2, chans), F32),
        ],
        order=order,
        inputs=4,
    )(first, rest, above, kernel, *order)


def exchange(value, partner):
    dp, space = lax.axis_size("dp"), lax.axis_size("space")
    pairs = []
    for i in range(dp):
        for j in range(space):
            to_dp, to_space = partner(i, j)
            pairs.append((i * space + j, to_dp * space + to_space))
    return lax.ppermute(value, ("dp", "space"), pairs)


def exchange_space(value, stage, cores):
    bits = bits_of(lax.axis_size("space"))

    def partner(i, j):
        bit = bits - 1 - stage if cores == 2 and i % 2 == 0 else stage
        return i, j ^ (1 << bit)

    return exchange(value, partner)


def exchange_chips(value, bit, cores):
    return exchange(value, lambda i, j: (i ^ (cores << bit), j))


def neighbour(value, steps):
    count = lax.axis_size("space")
    first, last = (max(0, -steps), min(count, count - steps))
    return lax.ppermute(value, "space", [(source, source + steps) for source in range(first, last)])


def exchange_stage(value, axis, stage, cores):
    return exchange_space(value, stage, cores) if axis == "space" else exchange_chips(value, stage, cores)


def add_cores(keep, sends, then, cores, order=()):
    got = tuple(exchange(send, lambda i, j: (i ^ 1, j)) if cores == 2 else 0 * send for send in sends)
    return add_stage(keep, got, None, then, cores, order)


def body(volume, kernel, cotangent):
    samples, planes, height, width, ci = volume.shape
    co = kernel.shape[-1]
    assert samples == 1
    dp, space = lax.axis_size("dp"), lax.axis_size("space")
    cores = 2 if dp % 2 == 0 else 1
    chips = dp // cores
    outs = planes // 2
    cells = height * width // 4
    scale = 1.0 / math.sqrt(dp * space * samples * outs * cells)
    over_space = [("space", stage) for stage in range(bits_of(space))]
    over_chips = [("chips", stage) for stage in range(bits_of(chips))]

    share = neighbour(halo_share(volume, kernel), 1)
    preact, even, odd = partial_preact(volume, kernel)
    cotangent = cotangent.reshape(outs * cells, co)
    rest, flipped_rest = activation(preact, cotangent, None, cells, (outs - 1) * cells, space, cores)
    products = early_ahead(even, odd, rest)
    first, flipped = activation(preact, cotangent, share, 0, cells, space, cores)
    flipped = jnp.concatenate([flipped, flipped_rest], axis=1)
    above = neighbour(first, -1)

    early = kernel_grad_part(even, odd, first, products, True, cores, chips, scale, space)
    early_units, late_units = 18 * (co // 128), 9 * (co // 128)
    plan = over_space + over_chips
    value, sent = add_cores(early[0], early[1:], plan[0], cores)
    late_plan, late_now, late_half = list(over_chips), None, None
    switch_at = [len(over_space) - 1 + 2 * stage for stage in range(len(over_space))]
    stay, moved = flipped[None], None
    for place, now in enumerate(plan):
        got = exchange_stage(sent, *now, cores)
        tokens = [sent]
        if place == 0:
            late = kernel_grad_part(even, odd, rest, above, False, cores, chips, scale, 1, (sent,))
            tokens.append(late[1])
        elif late_half is None:
            then = late_plan.pop(0) if late_plan else None
            if late_now is None:
                result = add_cores(late[0], late[1:], then, cores, (sent,))
            else:
                result = add_stage(late_value, late_got, late_now, then, cores, (sent,))
            late_now = then
            if then is None:
                late_half = result
            else:
                late_value, late_sent = result
                late_got = (exchange_stage(late_sent, *then, cores),)
                tokens.append(late_sent)
        if switch_at and place == switch_at[0]:
            stage = len(over_space) - len(switch_at)
            switch_at.pop(0)
            stay, out = switch_stage(stay, moved, 0, None, stage, cores, (tokens[-1],))
            moved = exchange_space(out, stage, cores)
            tokens.append(out)
        if place + 1 < len(plan):
            weight = SPACER if place >= len(over_space) else 1000
            value, sent = add_stage(
                value, (got,), now, plan[place + 1], cores, tuple(tokens[1:]), weight
            )
    for stage in range(len(over_space) - len(switch_at), len(over_space)):
        stay, out = switch_stage(stay, moved, 0, None, stage, cores, (sent,))
        moved = exchange_space(out, stage, cores)
    if late_half is None:
        late_half = add_stage(late_value, late_got, late_now, None, cores)

    mine = join(value, got, late_half, plan[-1], cores, tuple(tokens[1:]))
    early_rows = mine.shape[0] - late_half.shape[0]
    switched = None
    for step, (_, stage) in enumerate(reversed(over_space)):
        got = exchange_space(mine, stage, cores)
        order = ()
        if switched is None:
            switched, done = switched_of(stay, moved, 0, space, cores, (mine,))
            order = (done,)
        if step + 1 < len(over_space):
            mine = gather_stage(mine, got, early_rows << step, order)
    volume_grad, done = volume_grad_of(first, rest, above, kernel, height, width, (mine,))
    kernel_grad = kernel_grad_out(mine, got, early_units, late_units, space, cores, co, (done,))

    return (
        switched[None],
        volume_grad.reshape(volume.shape),
        kernel_grad.reshape(3, 3, 3, ci // dp, co),
    )


def solution(mesh):
    in_specs = (P("dp", "space", None, None, None), P(), P("dp", "space", None, None, None))
    out_specs = (
        P("dp", "space", None),
        P("dp", "space", None, None, None),
        P(None, None, None, "dp", None),
    )
    return jax.shard_map(body, mesh=mesh, in_specs=in_specs, out_specs=out_specs, check_vma=False)
```

```python
import functools
import math

import jax
import jax.numpy as jnp
from jax import lax
from jax.experimental import pallas as pl
from jax.experimental.pallas import tpu as pltpu
from jax.sharding import PartitionSpec as P

BF16 = jnp.bfloat16
F32 = jnp.float32
VMEM_LIMIT = 20 * 1024 * 1024
DONE = (8, 128)
PLANE_PARTS = 1
SPACER = 6 * 10**9
VMEM_WHOLE = 60 * 1024 * 1024


def call(kernel, out_shape, scratch=(), in_specs=None, limit=VMEM_LIMIT, order=(), inputs=0, flops=1000):
    extra = {} if in_specs is None else {"in_specs": in_specs}
    if order:
        whole = pl.BlockSpec(memory_space=pltpu.VMEM)
        extra["in_specs"] = [whole] * inputs + [pl.BlockSpec(memory_space=pl.ANY)] * len(order)
        inner, count = kernel, len(order)

        def kernel(*refs):
            inner(*refs[:inputs], *refs[inputs + count :])

    return pl.pallas_call(
        kernel,
        out_shape=out_shape,
        scratch_shapes=list(scratch),
        compiler_params=pltpu.CompilerParams(vmem_limit_bytes=limit),
        cost_estimate=pl.CostEstimate(flops=flops, bytes_accessed=1000, transcendentals=0),
        **extra,
    )


def spread_plane(plane, wide):
    height, width, chans = plane.shape
    cells = height * width
    half = width // 2
    wide[pl.ds(8, cells), :] = plane.reshape(cells, chans).astype(F32)
    left = wide[pl.ds(7, cells // 2, stride=2), :]
    even = wide[pl.ds(8, cells // 2, stride=2), :]
    odd = wide[pl.ds(9, cells // 2, stride=2), :]
    column = lax.broadcasted_iota(jnp.int32, left.shape, 0) % half
    left = jnp.where(column == 0, 0.0, left)
    joined = jnp.concatenate([left.astype(BF16), even.astype(BF16), odd.astype(BF16)], axis=1)
    joined = joined.reshape(height // 2, 2, half, 3 * chans)
    return joined[:, 0], joined[:, 1]


def tap_rows(even, odd, plane, kh):
    height = even.shape[1]
    picked = even[plane] if kh == 1 else odd[plane, pl.ds(0 if kh == 0 else 1, height)]
    return picked.reshape(height * even.shape[2], even.shape[3])


def bits_of(count):
    bits = count.bit_length() - 1
    assert 1 << bits == count
    return bits


def far_first(cores):
    return lax.axis_index("dp") % cores == 0 if cores == 2 else False


def reverse_bits(value, bits):
    return sum(((value >> bit) & 1) << (bits - 1 - bit) for bit in range(bits))


def staged_place(target, space, cores):
    return jnp.where(far_first(cores), target, reverse_bits(target, bits_of(space)))


def relative_place(source, space, cores):
    bits = bits_of(space)
    off = source ^ lax.axis_index("space")
    return jnp.where(far_first(cores), reverse_bits(off, bits), off)


def relative_group(group, space, cores):
    bits = bits_of(space)
    index = lax.axis_index("space")
    mine = jnp.where(far_first(cores), index, reverse_bits(index, bits))
    return group ^ mine


def halo_kernel(volume_ref, kernel_ref, share_ref, plane, weights, wide, sems):
    planes, height, width, chans = volume_ref.shape[1:]
    part = height // PLANE_PARTS
    rows = [pl.ds(index * part, part) for index in range(PLANE_PARTS)]
    copies = [
        pltpu.make_async_copy(volume_ref.at[0, planes - 1, row], plane.at[row], sems.at[index])
        for index, row in enumerate(rows)
    ]
    loads = [
        pltpu.make_async_copy(kernel_ref.at[0, kh], weights.at[kh], sems.at[PLANE_PARTS + kh])
        for kh in range(3)
    ]
    for copy in copies + loads:
        copy.start()
    for copy in copies:
        copy.wait()
    even, odd = spread_plane(plane[...], wide)
    above = jnp.concatenate([jnp.zeros_like(odd[:1]), odd[:-1]], axis=0)
    total = None
    for kh, rows in enumerate((above, even, odd)):
        loads[kh].wait()
        lhs = rows.reshape(height * width // 4, 3 * chans)
        rhs = weights[kh].reshape(3 * chans, weights.shape[-1])
        term = jnp.dot(lhs, rhs, preferred_element_type=F32)
        total = term if total is None else total + term
    share_ref[...] = total.astype(BF16)


def halo_share(volume, kernel):
    _, planes, height, width, chans = volume.shape
    co = kernel.shape[-1]
    return call(
        halo_kernel,
        jax.ShapeDtypeStruct((height * width // 4, co), BF16),
        [
            pltpu.VMEM((height, width, chans), BF16),
            pltpu.VMEM((3, 3, chans, co), BF16),
            pltpu.VMEM((height * width + 16, chans), F32),
            pltpu.SemaphoreType.DMA((PLANE_PARTS + 3,)),
        ],
        [pl.BlockSpec(memory_space=pltpu.HBM)] * 2,
        VMEM_WHOLE,
    )(volume, kernel)


def preact_kernel(volume_ref, kernel_ref, preact_ref, even_ref, odd_ref, wide):
    planes, height, width, chans = volume_ref.shape[1:]
    cells = height * width // 4
    outs = planes // 2
    for plane in range(planes):
        even, odd = spread_plane(volume_ref[0, plane], wide)
        even_ref[plane] = even
        odd_ref[plane, pl.ds(0, 1)] = jnp.zeros_like(odd[:1])
        odd_ref[plane, pl.ds(1, height // 2)] = odd
    co = kernel_ref.shape[-1]
    total = None
    for kd in (1, 2):
        for kh in range(3):
            lhs = [tap_rows(even_ref, odd_ref, 2 * d - 1 + kd, kh) for d in range(outs)]
            rhs = kernel_ref[kd, kh].reshape(3 * chans, co)
            term = jnp.dot(jnp.concatenate(lhs, axis=0), rhs, preferred_element_type=F32)
            total = term if total is None else total + term
    preact_ref[...] = total
    if outs > 1:
        total = preact_ref[pl.ds(cells, (outs - 1) * cells), :]
        for kh in range(3):
            lhs = [tap_rows(even_ref, odd_ref, 2 * d - 1, kh) for d in range(1, outs)]
            rhs = kernel_ref[0, kh].reshape(3 * chans, co)
            total += jnp.dot(jnp.concatenate(lhs, axis=0), rhs, preferred_element_type=F32)
        preact_ref[pl.ds(cells, (outs - 1) * cells), :] = total


def partial_preact(volume, kernel):
    _, planes, height, width, chans = volume.shape
    co = kernel.shape[-1]
    cells = height * width // 4
    h2, w2 = height // 2, width // 2
    return call(
        preact_kernel,
        (
            jax.ShapeDtypeStruct((planes // 2 * cells, co), F32),
            jax.ShapeDtypeStruct((planes, h2, w2, 3 * chans), BF16),
            jax.ShapeDtypeStruct((planes, h2 + 1, w2, 3 * chans), BF16),
        ),
        [pltpu.VMEM((height * width + 16, chans), F32)],
    )(volume, kernel)


def activation_kernel(space, cores, start, preact_ref, cotangent_ref, *refs):
    grad_ref, flipped_ref = refs[-2:]
    share_ref = refs[0] if len(refs) == 3 else None
    co = preact_ref.shape[1]
    count = grad_ref.shape[0]
    group, strips = co // space, flipped_ref.shape[1]
    rows = pl.ds(start, count)
    value = preact_ref[rows, :]
    if share_ref is not None:
        value = value + share_ref[...].astype(F32)
    sig = jax.nn.sigmoid(value)
    slope = sig * (1.0 + value * (1.0 - sig))
    grad_ref[...] = (cotangent_ref[rows, :].astype(F32) * slope).astype(BF16)
    flipped = (value * sig).T.astype(BF16)
    for target in range(space):
        place = staged_place(target, space, cores)
        for strip in range(strips):
            flipped_ref[place, strip] = flipped[
                target * group : (target + 1) * group, strip * 128 : (strip + 1) * 128
            ]


def activation(preact, cotangent, share, start, count, space, cores):
    co = preact.shape[1]
    return call(
        functools.partial(activation_kernel, space, cores, start),
        (
            jax.ShapeDtypeStruct((count, co), BF16),
            jax.ShapeDtypeStruct((space, count // 128, co // space, 128), BF16),
        ),
    )(preact, cotangent, *(() if share is None else (share,)))


def switched_kernel(space, cores, came, kept_ref, got_ref, out_ref, done_ref):
    done_ref[...] = jnp.zeros_like(done_ref)
    half = space // 2
    rows = kept_ref.shape[1]
    strips = kept_ref.shape[0] // half
    for source in range(space):
        place = relative_place(source, space, cores)
        far = place // half
        for strip in range(strips):
            column = (source * strips + strip) * 128
            row = (place % half) * strips + strip
            there = got_ref[pl.ds(pl.multiple_of(came + row * rows, rows), rows), :]
            out_ref[:, column : column + 128] = jnp.where(far == 1, there, kept_ref[row])


def switched_of(kept, got, came, space, cores, order):
    group = kept.shape[-2]
    kept = kept.reshape(-1, group, 128)
    return call(
        functools.partial(switched_kernel, space, cores, came),
        (
            jax.ShapeDtypeStruct((group, 2 * kept.shape[0] * 128), BF16),
            jax.ShapeDtypeStruct(DONE, F32),
        ),
        order=order,
        inputs=2,
    )(kept, got, *order)


def side(axis, stage, cores):
    if axis == "chips":
        bits = bits_of(lax.axis_size("dp") // cores)
        index = lax.axis_index("dp") // cores
    else:
        bits = bits_of(lax.axis_size("space"))
        index = lax.axis_index("space")
    return jnp.where(far_first(cores), (index >> (bits - 1 - stage)) & 1, (index >> stage) & 1)


def halves_of(shape, axis):
    units, chips = shape[:2]
    lead = (1, 2, units // 2 * chips) if axis == "space" else (units * chips // 2, 2, 1)
    return lead + tuple(shape[2:])


def half_shape(shape, axis):
    units, chips = shape[:2]
    return ((units // 2, chips) if axis == "space" else (units, chips // 2)) + tuple(shape[2:])


def add_kernel(now, then, cores, value_ref, *refs):
    outs = 1 if then is None else 2
    got = jnp.concatenate([ref[...] for ref in refs[:-outs]], axis=0).astype(F32)
    total = value_ref[...] if now is None else value_ref[:, side(*now, cores)]
    total = total.reshape(got.shape) + got
    if then is None:
        refs[-1][...] = total.astype(BF16)
        return
    keep_ref, sent_ref = refs[-2:]
    keep_ref[...] = total.reshape(keep_ref.shape)
    sent_ref[...] = keep_ref[:, 1 - side(*then, cores)].reshape(sent_ref.shape).astype(BF16)


def add_stage(value, got, now, then, cores, order=(), flops=1000):
    shape = (sum(piece.shape[0] for piece in got),) + got[0].shape[1:]
    if then is None:
        outs = jax.ShapeDtypeStruct(shape, BF16)
    else:
        outs = (
            jax.ShapeDtypeStruct(halves_of(shape, then[0]), F32),
            jax.ShapeDtypeStruct(half_shape(shape, then[0]), BF16),
        )
    return call(
        functools.partial(add_kernel, now, then, cores),
        outs,
        order=order,
        inputs=1 + len(got),
        flops=flops,
    )(value, *got, *order)


def switch_kernel(stage, cores, came, first_ref, *refs):
    stay_ref, out_ref = refs[-2:]
    refs = list(refs[:-2])
    bit = side("space", stage, cores)
    sources, _, targets, strips, rows, lanes = first_ref.shape
    half = targets * strips * rows
    if came is None:
        ahead = out_ref.shape[0] - sources * half
    else:
        ahead = out_ref.shape[0] - 2 * sources * half
    rider = refs.pop() if ahead else None
    if rider is not None:
        out_ref[pl.ds(0, ahead), :] = rider[...]
    place = ahead
    for source in range(sources):
        stay_ref[source] = first_ref[source, bit]
        out_ref[pl.ds(place, half), :] = first_ref[source, 1 - bit].reshape(half, lanes)
        place += half
    if came is not None:
        got_ref = refs[0]
        for source in range(sources):
            base = came + source * 2 * half
            mine = got_ref[pl.ds(pl.multiple_of(base + bit * half, rows), half), :]
            stay_ref[sources + source] = mine.reshape(targets, strips, rows, lanes)
            out_ref[pl.ds(place, half), :] = got_ref[
                pl.ds(pl.multiple_of(base + (1 - bit) * half, rows), half), :
            ]
            place += half


def switch_stage(first, got, came, rider, stage, cores, order):
    sources, targets, strips, rows, lanes = first.shape
    operands = (first.reshape(sources, 2, targets // 2, strips, rows, lanes),)
    total = sources * (1 if got is None else 2)
    count = total * targets // 2 * strips * rows
    if got is not None:
        operands += (got,)
    if rider is not None:
        operands += (rider.reshape(-1, lanes),)
        count += operands[-1].shape[0]
    return call(
        functools.partial(switch_kernel, stage, cores, None if got is None else came),
        (
            jax.ShapeDtypeStruct((total, targets // 2, strips, rows, lanes), BF16),
            jax.ShapeDtypeStruct((count, lanes), BF16),
        ),
        order=order,
        inputs=len(operands),
    )(*operands, *order)


def gather_kernel(early, mine_ref, got_ref, out_ref):
    rows = pl.ds(early, mine_ref.shape[0] - early)
    out_ref[pl.ds(0, early)] = mine_ref[pl.ds(0, early)]
    out_ref[pl.ds(early, early)] = got_ref[pl.ds(0, early)]
    total = mine_ref[rows].astype(F32) + got_ref[rows].astype(F32)
    out_ref[pl.ds(2 * early, total.shape[0])] = total.astype(BF16)


def gather_stage(mine, got, early, order=()):
    return call(
        functools.partial(gather_kernel, early),
        jax.ShapeDtypeStruct((mine.shape[0] + early,) + mine.shape[1:], BF16),
        order=order,
        inputs=2,
    )(mine, got, *order)


def join_kernel(now, cores, value_ref, got_ref, late_ref, out_ref):
    total = value_ref[:, side(*now, cores)].reshape(got_ref.shape) + got_ref[...].astype(F32)
    early = total.shape[0]
    out_ref[pl.ds(0, early)] = total.reshape((early,) + out_ref.shape[1:]).astype(BF16)
    out_ref[pl.ds(early, late_ref.shape[0])] = late_ref[...].reshape((-1,) + out_ref.shape[1:])


def join(value, got, late, now, cores, order):
    shape = (got.shape[0] + late.shape[0],) + got.shape[2:]
    return call(
        functools.partial(join_kernel, now, cores),
        jax.ShapeDtypeStruct(shape, BF16),
        order=order,
        inputs=3,
        flops=SPACER,
    )(value, got, late, *order)


def kernel_grad_out_kernel(space, cores, early_units, late_units, mine_ref, got_ref, out_ref):
    halves = out_ref.shape[-1] // 128
    half = space // 2
    share = -(-early_units // space)

    def put(index, value):
        tap, part = divmod(index, halves)
        out_ref[tap, :, part * 128 : (part + 1) * 128] = value

    for unit in range(late_units):
        row = half * share + unit
        put(unit, mine_ref[row].astype(F32) + got_ref[row].astype(F32))
    for group in range(space):
        place = relative_group(group, space, cores)
        far, row = place // half, (place % half) * share
        for unit in range(share):
            index = group * share + unit
            if index < early_units:
                value = jnp.where(far == 1, got_ref[row + unit], mine_ref[row + unit])
                put(late_units + index, value.astype(F32))


def kernel_grad_out(mine, got, early_units, late_units, space, cores, co, order):
    taps = (early_units + late_units) * 128 // co
    return call(
        functools.partial(kernel_grad_out_kernel, space, cores, early_units, late_units),
        jax.ShapeDtypeStruct((taps, mine.shape[1], co), F32),
        order=order,
        inputs=2,
    )(mine, got, *order)


def store_units(product, scale, core, cores, chips, put):
    chans = product.shape[0] // 3
    co = product.shape[1]
    block = chans // (cores * chips)
    halves = co // 128
    product = product * scale
    for kw in range(3):
        for half in range(halves):
            unit = product[kw * chans : (kw + 1) * chans, half * 128 : (half + 1) * 128]
            unit = unit.reshape(chips, cores, block, 128)
            for chip in range(chips):
                first = unit[chip, 0]
                last = unit[chip, cores - 1]
                keep = jnp.where(core == 0, first, last)
                send = jnp.where(core == 0, last, first)
                put(kw * halves + half, chip, keep, send)


def tap_products(even_ref, odd_ref, planes, rhs, put):
    for kh in range(3):
        lhs = [tap_rows(even_ref, odd_ref, plane, kh) for plane in planes]
        put(
            kh,
            lax.dot_general(
                jnp.concatenate(lhs, axis=0), rhs, (((0,), (0,)), ((), ())), preferred_element_type=F32
            ),
        )


def ahead_kernel(even_ref, odd_ref, rest_ref, out_ref):
    outs = even_ref.shape[0] // 2
    for place, kd in enumerate((1, 2)):
        planes = [2 * d - 1 + kd for d in range(1, outs)]

        def put(kh, product, base=3 * place):
            out_ref[base + kh] = product

        tap_products(even_ref, odd_ref, planes, rest_ref[...], put)


def early_ahead(even, odd, rest):
    return call(
        ahead_kernel, jax.ShapeDtypeStruct((6, even.shape[-1], rest.shape[-1]), F32)
    )(even, odd, rest)


def kernel_grad_kernel(early, cores, chips, scale, even_ref, odd_ref, grads_ref, other_ref, keep_ref, send_ref):
    outs = even_ref.shape[0] // 2
    core = lax.axis_index("dp") % cores
    mine = far_first(cores)
    bits = bits_of(chips)
    places = [jnp.where(mine, reverse_bits(chip, bits), chip) for chip in range(chips)]
    others = [jnp.where(mine, chip, reverse_bits(chip, bits)) for chip in range(chips)]
    per_row = 3 * (grads_ref.shape[1] // 128)
    kds = (1, 2) if early else (0,)
    for unit in range(len(kds) * 3 * per_row, keep_ref.shape[0]):
        keep_ref[unit] = jnp.zeros(keep_ref.shape[1:], F32)
        send_ref[unit] = jnp.zeros(keep_ref.shape[1:], BF16)
    for place, kd in enumerate(kds):
        if early:
            planes, rhs = [kd - 1], grads_ref[...]
        else:
            planes = [2 * d - 1 for d in range(1, outs + 1)]
            rhs = jnp.concatenate([grads_ref[...], other_ref[...]], axis=0)

        def take(kh, product, base=3 * place):
            if early:
                product = product + other_ref[base + kh]

            def put(unit, chip, keep, send):
                keep_ref[(base + kh) * per_row + unit, places[chip]] = keep
                send_ref[(base + kh) * per_row + unit, others[chip]] = send.astype(BF16)

            store_units(product, scale, core, cores, chips, put)

        tap_products(even_ref, odd_ref, planes, rhs, take)


def kernel_grad_part(even, odd, grads, other, early, cores, chips, scale, multiple, order=()):
    chans = even.shape[-1] // 3
    units = (18 if early else 9) * (grads.shape[-1] // 128)
    units += -units % multiple
    shape = (units, chips, chans // (cores * chips), 128)
    return call(
        functools.partial(kernel_grad_kernel, early, cores, chips, scale),
        (jax.ShapeDtypeStruct(shape, F32), jax.ShapeDtypeStruct(shape, BF16)),
        order=order,
        inputs=4,
    )(even, odd, grads, other, *order)


def volume_grad_kernel(first_ref, rest_ref, above_ref, kernel_ref, out_ref, done_ref, shifted, wide):
    done_ref[...] = jnp.zeros_like(done_ref)
    planes, h2, _, width, chans = out_ref.shape
    w2 = width // 2
    cells = h2 * w2
    outs = planes // 2
    co = first_ref.shape[1]
    here, right = [], []
    for d in range(outs + 1):
        if 0 < d < outs:
            plane = rest_ref[pl.ds((d - 1) * cells, cells), :]
        else:
            plane = (first_ref if d == 0 else above_ref)[...]
        shifted[pl.ds(0, cells), :] = plane.astype(F32)
        moved = shifted[pl.ds(1, cells), :]
        column = lax.broadcasted_iota(jnp.int32, moved.shape, 0) % w2
        moved = jnp.where(column == w2 - 1, 0.0, moved).astype(BF16)
        here.append(plane)
        right.append(moved)

    def down(rows):
        return jnp.concatenate([rows[w2:], jnp.zeros((w2, co), BF16)], axis=0)

    contract = (((1,), (1,)), ((), ()))
    for plane in range(planes):
        d = plane // 2
        depth = [(1, d)] if plane % 2 == 0 else [(2, d), (0, d + 1)]
        for odd_row in range(2):
            taps = [(1, False)] if odd_row == 0 else [(2, False), (0, True)]
            both, right_only = None, None
            for kd, source in depth:
                for kh, lower in taps:
                    lhs = down(here[source]) if lower else here[source]
                    rhs = kernel_ref[kd, kh, pl.ds(1, 2)].reshape(2 * chans, co)
                    term = lax.dot_general(lhs, rhs, contract, preferred_element_type=F32)
                    both = term if both is None else both + term
                    lhs = down(right[source]) if lower else right[source]
                    term = lax.dot_general(lhs, kernel_ref[kd, kh, 0], contract, preferred_element_type=F32)
                    right_only = term if right_only is None else right_only + term
            wide[pl.ds(0, cells, stride=2), :] = both[:, :chans]
            wide[pl.ds(1, cells, stride=2), :] = both[:, chans:] + right_only
            out_ref[plane, :, odd_row] = wide[...].reshape(h2, width, chans).astype(BF16)


def volume_grad_of(first, rest, above, kernel, height, width, order=()):
    cells, co = first.shape[0] + rest.shape[0], first.shape[1]
    chans = kernel.shape[3]
    planes = 2 * cells * 4 // (height * width)
    shape = (planes, height // 2, 2, width, chans)
    return call(
        volume_grad_kernel,
        (jax.ShapeDtypeStruct(shape, BF16), jax.ShapeDtypeStruct(DONE, F32)),
        [
            pltpu.VMEM((height * width // 4 + 8, co), F32),
            pltpu.VMEM((height * width // 2, chans), F32),
        ],
        order=order,
        inputs=4,
    )(first, rest, above, kernel, *order)


def exchange(value, partner):
    dp, space = lax.axis_size("dp"), lax.axis_size("space")
    pairs = []
    for i in range(dp):
        for j in range(space):
            to_dp, to_space = partner(i, j)
            pairs.append((i * space + j, to_dp * space + to_space))
    return lax.ppermute(value, ("dp", "space"), pairs)


def exchange_space(value, stage, cores):
    bits = bits_of(lax.axis_size("space"))

    def partner(i, j):
        bit = bits - 1 - stage if cores == 2 and i % 2 == 0 else stage
        return i, j ^ (1 << bit)

    return exchange(value, partner)


def exchange_chips(value, stage, cores):
    bits = bits_of(lax.axis_size("dp") // cores)

    def partner(i, j):
        bit = bits - 1 - stage if cores == 2 and i % 2 == 0 else stage
        return i ^ (cores << bit), j

    return exchange(value, partner)


def neighbour(value, steps):
    count = lax.axis_size("space")
    first, last = (max(0, -steps), min(count, count - steps))
    return lax.ppermute(value, "space", [(source, source + steps) for source in range(first, last)])


def exchange_stage(value, axis, stage, cores):
    return exchange_space(value, stage, cores) if axis == "space" else exchange_chips(value, stage, cores)


def add_cores(keep, sends, then, cores, order=()):
    got = tuple(exchange(send, lambda i, j: (i ^ 1, j)) if cores == 2 else 0 * send for send in sends)
    return add_stage(keep, got, None, then, cores, order)


def body(volume, kernel, cotangent):
    samples, planes, height, width, ci = volume.shape
    co = kernel.shape[-1]
    assert samples == 1
    dp, space = lax.axis_size("dp"), lax.axis_size("space")
    cores = 2 if dp % 2 == 0 else 1
    chips = dp // cores
    outs = planes // 2
    cells = height * width // 4
    scale = 1.0 / math.sqrt(dp * space * samples * outs * cells)
    over_space = [("space", stage) for stage in range(bits_of(space))]
    over_chips = [("chips", stage) for stage in range(bits_of(chips))]

    share = neighbour(halo_share(volume, kernel), 1)
    preact, even, odd = partial_preact(volume, kernel)
    cotangent = cotangent.reshape(outs * cells, co)
    rest, flipped_rest = activation(preact, cotangent, None, cells, (outs - 1) * cells, space, cores)
    products = early_ahead(even, odd, rest)
    first, flipped = activation(preact, cotangent, share, 0, cells, space, cores)
    flipped = jnp.concatenate([flipped, flipped_rest], axis=1)
    above = neighbour(first, -1)

    early = kernel_grad_part(even, odd, first, products, True, cores, chips, scale, space)
    early_units, late_units = 18 * (co // 128), 9 * (co // 128)
    plan = over_space + over_chips
    value, sent = add_cores(early[0], early[1:], plan[0], cores)
    late_plan, late_now, late_half = list(over_chips), None, None
    switch_at = [len(over_space) - 1 + 2 * stage for stage in range(len(over_space))]
    stay, moved = flipped[None], None
    for place, now in enumerate(plan):
        got = exchange_stage(sent, *now, cores)
        tokens = [sent]
        if place == 0:
            late = kernel_grad_part(even, odd, rest, above, False, cores, chips, scale, 1, (sent,))
            tokens.append(late[1])
        elif late_half is None:
            then = late_plan.pop(0) if late_plan else None
            if late_now is None:
                result = add_cores(late[0], late[1:], then, cores, (sent,))
            else:
                result = add_stage(late_value, late_got, late_now, then, cores, (sent,))
            late_now = then
            if then is None:
                late_half = result
            else:
                late_value, late_sent = result
                late_got = (exchange_stage(late_sent, *then, cores),)
                tokens.append(late_sent)
        if switch_at and place == switch_at[0]:
            stage = len(over_space) - len(switch_at)
            switch_at.pop(0)
            stay, out = switch_stage(stay, moved, 0, None, stage, cores, (tokens[-1],))
            moved = exchange_space(out, stage, cores)
            tokens.append(out)
        if place + 1 < len(plan):
            weight = SPACER if place >= len(over_space) else 1000
            value, sent = add_stage(
                value, (got,), now, plan[place + 1], cores, tuple(tokens[1:]), weight
            )
    for stage in range(len(over_space) - len(switch_at), len(over_space)):
        stay, out = switch_stage(stay, moved, 0, None, stage, cores, (sent,))
        moved = exchange_space(out, stage, cores)
    if late_half is None:
        late_half = add_stage(late_value, late_got, late_now, None, cores)

    mine = join(value, got, late_half, plan[-1], cores, tuple(tokens[1:]))
    early_rows = mine.shape[0] - late_half.shape[0]
    switched = None
    for step, (_, stage) in enumerate(reversed(over_space)):
        got = exchange_space(mine, stage, cores)
        order = ()
        if switched is None:
            switched, done = switched_of(stay, moved, 0, space, cores, (mine,))
            order = (done,)
        if step + 1 < len(over_space):
            mine = gather_stage(mine, got, early_rows << step, order)
    volume_grad, done = volume_grad_of(first, rest, above, kernel, height, width, (mine,))
    kernel_grad = kernel_grad_out(mine, got, early_units, late_units, space, cores, co, (done,))

    return (
        switched[None],
        volume_grad.reshape(volume.shape),
        kernel_grad.reshape(3, 3, 3, ci // dp, co),
    )


def solution(mesh):
    in_specs = (P("dp", "space", None, None, None), P(), P("dp", "space", None, None, None))
    out_specs = (
        P("dp", "space", None),
        P("dp", "space", None, None, None),
        P(None, None, None, "dp", None),
    )
    return jax.shard_map(body, mesh=mesh, in_specs=in_specs, out_specs=out_specs, check_vma=False)
```

```python
import functools
import math

import jax
import jax.numpy as jnp
from jax import lax
from jax.experimental import pallas as pl
from jax.experimental.pallas import tpu as pltpu
from jax.sharding import PartitionSpec as P

BF16 = jnp.bfloat16
F32 = jnp.float32
VMEM_LIMIT = 20 * 1024 * 1024
DONE = (8, 128)
PLANE_PARTS = 1
SPACER = 6 * 10**9
VMEM_WHOLE = 60 * 1024 * 1024


def call(kernel, out_shape, scratch=(), in_specs=None, limit=VMEM_LIMIT, order=(), inputs=0, flops=1000):
    extra = {} if in_specs is None else {"in_specs": in_specs}
    if order:
        whole = pl.BlockSpec(memory_space=pltpu.VMEM)
        extra["in_specs"] = [whole] * inputs + [pl.BlockSpec(memory_space=pl.ANY)] * len(order)
        inner, count = kernel, len(order)

        def kernel(*refs):
            inner(*refs[:inputs], *refs[inputs + count :])

    return pl.pallas_call(
        kernel,
        out_shape=out_shape,
        scratch_shapes=list(scratch),
        compiler_params=pltpu.CompilerParams(vmem_limit_bytes=limit),
        cost_estimate=pl.CostEstimate(flops=flops, bytes_accessed=1000, transcendentals=0),
        **extra,
    )


def spread_plane(plane, wide):
    height, width, chans = plane.shape
    cells = height * width
    half = width // 2
    wide[pl.ds(8, cells), :] = plane.reshape(cells, chans).astype(F32)
    left = wide[pl.ds(7, cells // 2, stride=2), :]
    even = wide[pl.ds(8, cells // 2, stride=2), :]
    odd = wide[pl.ds(9, cells // 2, stride=2), :]
    column = lax.broadcasted_iota(jnp.int32, left.shape, 0) % half
    left = jnp.where(column == 0, 0.0, left)
    joined = jnp.concatenate([left.astype(BF16), even.astype(BF16), odd.astype(BF16)], axis=1)
    joined = joined.reshape(height // 2, 2, half, 3 * chans)
    return joined[:, 0], joined[:, 1]


def tap_rows(even, odd, plane, kh):
    height = even.shape[1]
    picked = even[plane] if kh == 1 else odd[plane, pl.ds(0 if kh == 0 else 1, height)]
    return picked.reshape(height * even.shape[2], even.shape[3])


def bits_of(count):
    bits = count.bit_length() - 1
    assert 1 << bits == count
    return bits


def far_first(cores):
    return lax.axis_index("dp") % cores == 0 if cores == 2 else False


def side_first(cores):
    return lax.axis_index("dp") % cores == 1 if cores == 2 else False


def reverse_bits(value, bits):
    return sum(((value >> bit) & 1) << (bits - 1 - bit) for bit in range(bits))


def staged_place(target, space, cores):
    return jnp.where(far_first(cores), target, reverse_bits(target, bits_of(space)))


def relative_place(source, space, cores):
    bits = bits_of(space)
    off = source ^ lax.axis_index("space")
    return jnp.where(far_first(cores), reverse_bits(off, bits), off)


def relative_group(group, space, cores):
    bits = bits_of(space)
    index = lax.axis_index("space")
    mine = jnp.where(far_first(cores), index, reverse_bits(index, bits))
    return group ^ mine


def halo_kernel(volume_ref, kernel_ref, share_ref, plane, weights, wide, sems):
    planes, height, width, chans = volume_ref.shape[1:]
    part = height // PLANE_PARTS
    rows = [pl.ds(index * part, part) for index in range(PLANE_PARTS)]
    copies = [
        pltpu.make_async_copy(volume_ref.at[0, planes - 1, row], plane.at[row], sems.at[index])
        for index, row in enumerate(rows)
    ]
    loads = [
        pltpu.make_async_copy(kernel_ref.at[0, kh], weights.at[kh], sems.at[PLANE_PARTS + kh])
        for kh in range(3)
    ]
    for copy in copies + loads:
        copy.start()
    for copy in copies:
        copy.wait()
    even, odd = spread_plane(plane[...], wide)
    above = jnp.concatenate([jnp.zeros_like(odd[:1]), odd[:-1]], axis=0)
    total = None
    for kh, rows in enumerate((above, even, odd)):
        loads[kh].wait()
        lhs = rows.reshape(height * width // 4, 3 * chans)
        rhs = weights[kh].reshape(3 * chans, weights.shape[-1])
        term = jnp.dot(lhs, rhs, preferred_element_type=F32)
        total = term if total is None else total + term
    share_ref[...] = total.astype(BF16)


def halo_share(volume, kernel):
    _, planes, height, width, chans = volume.shape
    co = kernel.shape[-1]
    return call(
        halo_kernel,
        jax.ShapeDtypeStruct((height * width // 4, co), BF16),
        [
            pltpu.VMEM((height, width, chans), BF16),
            pltpu.VMEM((3, 3, chans, co), BF16),
            pltpu.VMEM((height * width + 16, chans), F32),
            pltpu.SemaphoreType.DMA((PLANE_PARTS + 3,)),
        ],
        [pl.BlockSpec(memory_space=pltpu.HBM)] * 2,
        VMEM_WHOLE,
    )(volume, kernel)


def preact_kernel(volume_ref, kernel_ref, preact_ref, even_ref, odd_ref, wide):
    planes, height, width, chans = volume_ref.shape[1:]
    cells = height * width // 4
    outs = planes // 2
    for plane in range(planes):
        even, odd = spread_plane(volume_ref[0, plane], wide)
        even_ref[plane] = even
        odd_ref[plane, pl.ds(0, 1)] = jnp.zeros_like(odd[:1])
        odd_ref[plane, pl.ds(1, height // 2)] = odd
    co = kernel_ref.shape[-1]
    total = None
    for kd in (1, 2):
        for kh in range(3):
            lhs = [tap_rows(even_ref, odd_ref, 2 * d - 1 + kd, kh) for d in range(outs)]
            rhs = kernel_ref[kd, kh].reshape(3 * chans, co)
            term = jnp.dot(jnp.concatenate(lhs, axis=0), rhs, preferred_element_type=F32)
            total = term if total is None else total + term
    preact_ref[...] = total
    if outs > 1:
        total = preact_ref[pl.ds(cells, (outs - 1) * cells), :]
        for kh in range(3):
            lhs = [tap_rows(even_ref, odd_ref, 2 * d - 1, kh) for d in range(1, outs)]
            rhs = kernel_ref[0, kh].reshape(3 * chans, co)
            total += jnp.dot(jnp.concatenate(lhs, axis=0), rhs, preferred_element_type=F32)
        preact_ref[pl.ds(cells, (outs - 1) * cells), :] = total


def partial_preact(volume, kernel):
    _, planes, height, width, chans = volume.shape
    co = kernel.shape[-1]
    cells = height * width // 4
    h2, w2 = height // 2, width // 2
    return call(
        preact_kernel,
        (
            jax.ShapeDtypeStruct((planes // 2 * cells, co), F32),
            jax.ShapeDtypeStruct((planes, h2, w2, 3 * chans), BF16),
            jax.ShapeDtypeStruct((planes, h2 + 1, w2, 3 * chans), BF16),
        ),
        [pltpu.VMEM((height * width + 16, chans), F32)],
    )(volume, kernel)


def activation_kernel(space, cores, start, preact_ref, cotangent_ref, *refs):
    grad_ref, flipped_ref = refs[-2:]
    share_ref = refs[0] if len(refs) == 3 else None
    co = preact_ref.shape[1]
    count = grad_ref.shape[0]
    group, strips = co // space, flipped_ref.shape[1]
    rows = pl.ds(start, count)
    value = preact_ref[rows, :]
    if share_ref is not None:
        value = value + share_ref[...].astype(F32)
    sig = jax.nn.sigmoid(value)
    slope = sig * (1.0 + value * (1.0 - sig))
    grad_ref[...] = (cotangent_ref[rows, :].astype(F32) * slope).astype(BF16)
    flipped = (value * sig).T.astype(BF16)
    for target in range(space):
        place = staged_place(target, space, cores)
        for strip in range(strips):
            flipped_ref[place, strip] = flipped[
                target * group : (target + 1) * group, strip * 128 : (strip + 1) * 128
            ]


def activation(preact, cotangent, share, start, count, space, cores):
    co = preact.shape[1]
    return call(
        functools.partial(activation_kernel, space, cores, start),
        (
            jax.ShapeDtypeStruct((count, co), BF16),
            jax.ShapeDtypeStruct((space, count // 128, co // space, 128), BF16),
        ),
    )(preact, cotangent, *(() if share is None else (share,)))


def switched_kernel(space, cores, came, kept_ref, got_ref, out_ref, done_ref):
    done_ref[...] = jnp.zeros_like(done_ref)
    half = space // 2
    rows = kept_ref.shape[1]
    strips = kept_ref.shape[0] // half
    for source in range(space):
        place = relative_place(source, space, cores)
        far = place // half
        for strip in range(strips):
            column = (source * strips + strip) * 128
            row = (place % half) * strips + strip
            there = got_ref[pl.ds(pl.multiple_of(came + row * rows, rows), rows), :]
            out_ref[:, column : column + 128] = jnp.where(far == 1, there, kept_ref[row])


def switched_of(kept, got, came, space, cores, order):
    group = kept.shape[-2]
    kept = kept.reshape(-1, group, 128)
    return call(
        functools.partial(switched_kernel, space, cores, came),
        (
            jax.ShapeDtypeStruct((group, 2 * kept.shape[0] * 128), BF16),
            jax.ShapeDtypeStruct(DONE, F32),
        ),
        order=order,
        inputs=2,
    )(kept, got, *order)


def side(axis, stage, cores):
    if axis == "chips":
        bits = bits_of(lax.axis_size("dp") // cores)
        index = lax.axis_index("dp") // cores
        top_first = side_first(cores)
    else:
        bits = bits_of(lax.axis_size("space"))
        index = lax.axis_index("space")
        top_first = far_first(cores)
    return jnp.where(top_first, (index >> (bits - 1 - stage)) & 1, (index >> stage) & 1)


def halves_of(shape, axis):
    units, chips = shape[:2]
    lead = (1, 2, units // 2 * chips) if axis == "space" else (units * chips // 2, 2, 1)
    return lead + tuple(shape[2:])


def half_shape(shape, axis):
    units, chips = shape[:2]
    return ((units // 2, chips) if axis == "space" else (units, chips // 2)) + tuple(shape[2:])


def add_kernel(now, then, cores, value_ref, *refs):
    outs = 1 if then is None else 2
    got = jnp.concatenate([ref[...] for ref in refs[:-outs]], axis=0).astype(F32)
    total = value_ref[...] if now is None else value_ref[:, side(*now, cores)]
    total = total.reshape(got.shape) + got
    if then is None:
        refs[-1][...] = total.astype(BF16)
        return
    keep_ref, sent_ref = refs[-2:]
    keep_ref[...] = total.reshape(keep_ref.shape)
    sent_ref[...] = keep_ref[:, 1 - side(*then, cores)].reshape(sent_ref.shape).astype(BF16)


def add_stage(value, got, now, then, cores, order=(), flops=1000):
    shape = (sum(piece.shape[0] for piece in got),) + got[0].shape[1:]
    if then is None:
        outs = jax.ShapeDtypeStruct(shape, BF16)
    else:
        outs = (
            jax.ShapeDtypeStruct(halves_of(shape, then[0]), F32),
            jax.ShapeDtypeStruct(half_shape(shape, then[0]), BF16),
        )
    return call(
        functools.partial(add_kernel, now, then, cores),
        outs,
        order=order,
        inputs=1 + len(got),
        flops=flops,
    )(value, *got, *order)


def switch_kernel(stage, cores, came, first_ref, *refs):
    stay_ref, out_ref = refs[-2:]
    refs = list(refs[:-2])
    bit = side("space", stage, cores)
    sources, _, targets, strips, rows, lanes = first_ref.shape
    half = targets * strips * rows
    if came is None:
        ahead = out_ref.shape[0] - sources * half
    else:
        ahead = out_ref.shape[0] - 2 * sources * half
    rider = refs.pop() if ahead else None
    if rider is not None:
        out_ref[pl.ds(0, ahead), :] = rider[...]
    place = ahead
    for source in range(sources):
        stay_ref[source] = first_ref[source, bit]
        out_ref[pl.ds(place, half), :] = first_ref[source, 1 - bit].reshape(half, lanes)
        place += half
    if came is not None:
        got_ref = refs[0]
        for source in range(sources):
            base = came + source * 2 * half
            mine = got_ref[pl.ds(pl.multiple_of(base + bit * half, rows), half), :]
            stay_ref[sources + source] = mine.reshape(targets, strips, rows, lanes)
            out_ref[pl.ds(place, half), :] = got_ref[
                pl.ds(pl.multiple_of(base + (1 - bit) * half, rows), half), :
            ]
            place += half


def switch_stage(first, got, came, rider, stage, cores, order):
    sources, targets, strips, rows, lanes = first.shape
    operands = (first.reshape(sources, 2, targets // 2, strips, rows, lanes),)
    total = sources * (1 if got is None else 2)
    count = total * targets // 2 * strips * rows
    if got is not None:
        operands += (got,)
    if rider is not None:
        operands += (rider.reshape(-1, lanes),)
        count += operands[-1].shape[0]
    return call(
        functools.partial(switch_kernel, stage, cores, None if got is None else came),
        (
            jax.ShapeDtypeStruct((total, targets // 2, strips, rows, lanes), BF16),
            jax.ShapeDtypeStruct((count, lanes), BF16),
        ),
        order=order,
        inputs=len(operands),
    )(*operands, *order)


def gather_kernel(early, mine_ref, got_ref, out_ref):
    rows = pl.ds(early, mine_ref.shape[0] - early)
    out_ref[pl.ds(0, early)] = mine_ref[pl.ds(0, early)]
    out_ref[pl.ds(early, early)] = got_ref[pl.ds(0, early)]
    total = mine_ref[rows].astype(F32) + got_ref[rows].astype(F32)
    out_ref[pl.ds(2 * early, total.shape[0])] = total.astype(BF16)


def gather_stage(mine, got, early, order=()):
    return call(
        functools.partial(gather_kernel, early),
        jax.ShapeDtypeStruct((mine.shape[0] + early,) + mine.shape[1:], BF16),
        order=order,
        inputs=2,
    )(mine, got, *order)


def join_kernel(now, cores, value_ref, got_ref, late_ref, out_ref):
    total = value_ref[:, side(*now, cores)].reshape(got_ref.shape) + got_ref[...].astype(F32)
    early = total.shape[0]
    out_ref[pl.ds(0, early)] = total.reshape((early,) + out_ref.shape[1:]).astype(BF16)
    out_ref[pl.ds(early, late_ref.shape[0])] = late_ref[...].reshape((-1,) + out_ref.shape[1:])


def join(value, got, late, now, cores, order):
    shape = (got.shape[0] + late.shape[0],) + got.shape[2:]
    return call(
        functools.partial(join_kernel, now, cores),
        jax.ShapeDtypeStruct(shape, BF16),
        order=order,
        inputs=3,
        flops=SPACER,
    )(value, got, late, *order)


def kernel_grad_out_kernel(space, cores, early_units, late_units, mine_ref, got_ref, out_ref):
    halves = out_ref.shape[-1] // 128
    half = space // 2
    share = -(-early_units // space)

    def put(index, value):
        tap, part = divmod(index, halves)
        out_ref[tap, :, part * 128 : (part + 1) * 128] = value

    for unit in range(late_units):
        row = half * share + unit
        put(unit, mine_ref[row].astype(F32) + got_ref[row].astype(F32))
    for group in range(space):
        place = relative_group(group, space, cores)
        far, row = place // half, (place % half) * share
        for unit in range(share):
            index = group * share + unit
            if index < early_units:
                value = jnp.where(far == 1, got_ref[row + unit], mine_ref[row + unit])
                put(late_units + index, value.astype(F32))


def kernel_grad_out(mine, got, early_units, late_units, space, cores, co, order):
    taps = (early_units + late_units) * 128 // co
    return call(
        functools.partial(kernel_grad_out_kernel, space, cores, early_units, late_units),
        jax.ShapeDtypeStruct((taps, mine.shape[1], co), F32),
        order=order,
        inputs=2,
    )(mine, got, *order)


def store_units(product, scale, core, cores, chips, put):
    chans = product.shape[0] // 3
    co = product.shape[1]
    block = chans // (cores * chips)
    halves = co // 128
    product = product * scale
    for kw in range(3):
        for half in range(halves):
            unit = product[kw * chans : (kw + 1) * chans, half * 128 : (half + 1) * 128]
            unit = unit.reshape(chips, cores, block, 128)
            for chip in range(chips):
                first = unit[chip, 0]
                last = unit[chip, cores - 1]
                keep = jnp.where(core == 0, first, last)
                send = jnp.where(core == 0, last, first)
                put(kw * halves + half, chip, keep, send)


def tap_products(even_ref, odd_ref, planes, rhs, put):
    for kh in range(3):
        lhs = [tap_rows(even_ref, odd_ref, plane, kh) for plane in planes]
        put(
            kh,
            lax.dot_general(
                jnp.concatenate(lhs, axis=0), rhs, (((0,), (0,)), ((), ())), preferred_element_type=F32
            ),
        )


def ahead_kernel(even_ref, odd_ref, rest_ref, out_ref):
    outs = even_ref.shape[0] // 2
    for place, kd in enumerate((1, 2)):
        planes = [2 * d - 1 + kd for d in range(1, outs)]

        def put(kh, product, base=3 * place):
            out_ref[base + kh] = product

        tap_products(even_ref, odd_ref, planes, rest_ref[...], put)


def early_ahead(even, odd, rest):
    return call(
        ahead_kernel, jax.ShapeDtypeStruct((6, even.shape[-1], rest.shape[-1]), F32)
    )(even, odd, rest)


def kernel_grad_kernel(early, cores, chips, scale, even_ref, odd_ref, grads_ref, other_ref, keep_ref, send_ref):
    outs = even_ref.shape[0] // 2
    core = lax.axis_index("dp") % cores
    mine = side_first(cores)
    bits = bits_of(chips)
    places = [jnp.where(mine, reverse_bits(chip, bits), chip) for chip in range(chips)]
    others = [jnp.where(mine, chip, reverse_bits(chip, bits)) for chip in range(chips)]
    per_row = 3 * (grads_ref.shape[1] // 128)
    kds = (1, 2) if early else (0,)
    for unit in range(len(kds) * 3 * per_row, keep_ref.shape[0]):
        keep_ref[unit] = jnp.zeros(keep_ref.shape[1:], F32)
        send_ref[unit] = jnp.zeros(keep_ref.shape[1:], BF16)
    for place, kd in enumerate(kds):
        if early:
            planes, rhs = [kd - 1], grads_ref[...]
        else:
            planes = [2 * d - 1 for d in range(1, outs + 1)]
            rhs = jnp.concatenate([grads_ref[...], other_ref[...]], axis=0)

        def take(kh, product, base=3 * place):
            if early:
                product = product + other_ref[base + kh]

            def put(unit, chip, keep, send):
                keep_ref[(base + kh) * per_row + unit, places[chip]] = keep
                send_ref[(base + kh) * per_row + unit, others[chip]] = send.astype(BF16)

            store_units(product, scale, core, cores, chips, put)

        tap_products(even_ref, odd_ref, planes, rhs, take)


def kernel_grad_part(even, odd, grads, other, early, cores, chips, scale, multiple, order=()):
    chans = even.shape[-1] // 3
    units = (18 if early else 9) * (grads.shape[-1] // 128)
    units += -units % multiple
    shape = (units, chips, chans // (cores * chips), 128)
    return call(
        functools.partial(kernel_grad_kernel, early, cores, chips, scale),
        (jax.ShapeDtypeStruct(shape, F32), jax.ShapeDtypeStruct(shape, BF16)),
        order=order,
        inputs=4,
    )(even, odd, grads, other, *order)


def volume_grad_kernel(first_ref, rest_ref, above_ref, kernel_ref, out_ref, done_ref, shifted, wide):
    done_ref[...] = jnp.zeros_like(done_ref)
    planes, h2, _, width, chans = out_ref.shape
    w2 = width // 2
    cells = h2 * w2
    outs = planes // 2
    co = first_ref.shape[1]
    here, right = [], []
    for d in range(outs + 1):
        if 0 < d < outs:
            plane = rest_ref[pl.ds((d - 1) * cells, cells), :]
        else:
            plane = (first_ref if d == 0 else above_ref)[...]
        shifted[pl.ds(0, cells), :] = plane.astype(F32)
        moved = shifted[pl.ds(1, cells), :]
        column = lax.broadcasted_iota(jnp.int32, moved.shape, 0) % w2
        moved = jnp.where(column == w2 - 1, 0.0, moved).astype(BF16)
        here.append(plane)
        right.append(moved)

    def down(rows):
        return jnp.concatenate([rows[w2:], jnp.zeros((w2, co), BF16)], axis=0)

    contract = (((1,), (1,)), ((), ()))
    for plane in range(planes):
        d = plane // 2
        depth = [(1, d)] if plane % 2 == 0 else [(2, d), (0, d + 1)]
        for odd_row in range(2):
            taps = [(1, False)] if odd_row == 0 else [(2, False), (0, True)]
            both, right_only = None, None
            for kd, source in depth:
                for kh, lower in taps:
                    lhs = down(here[source]) if lower else here[source]
                    rhs = kernel_ref[kd, kh, pl.ds(1, 2)].reshape(2 * chans, co)
                    term = lax.dot_general(lhs, rhs, contract, preferred_element_type=F32)
                    both = term if both is None else both + term
                    lhs = down(right[source]) if lower else right[source]
                    term = lax.dot_general(lhs, kernel_ref[kd, kh, 0], contract, preferred_element_type=F32)
                    right_only = term if right_only is None else right_only + term
            wide[pl.ds(0, cells, stride=2), :] = both[:, :chans]
            wide[pl.ds(1, cells, stride=2), :] = both[:, chans:] + right_only
            out_ref[plane, :, odd_row] = wide[...].reshape(h2, width, chans).astype(BF16)


def volume_grad_of(first, rest, above, kernel, height, width, order=()):
    cells, co = first.shape[0] + rest.shape[0], first.shape[1]
    chans = kernel.shape[3]
    planes = 2 * cells * 4 // (height * width)
    shape = (planes, height // 2, 2, width, chans)
    return call(
        volume_grad_kernel,
        (jax.ShapeDtypeStruct(shape, BF16), jax.ShapeDtypeStruct(DONE, F32)),
        [
            pltpu.VMEM((height * width // 4 + 8, co), F32),
            pltpu.VMEM((height * width // 2, chans), F32),
        ],
        order=order,
        inputs=4,
    )(first, rest, above, kernel, *order)


def exchange(value, partner):
    dp, space = lax.axis_size("dp"), lax.axis_size("space")
    pairs = []
    for i in range(dp):
        for j in range(space):
            to_dp, to_space = partner(i, j)
            pairs.append((i * space + j, to_dp * space + to_space))
    return lax.ppermute(value, ("dp", "space"), pairs)


def exchange_space(value, stage, cores):
    bits = bits_of(lax.axis_size("space"))

    def partner(i, j):
        bit = bits - 1 - stage if cores == 2 and i % 2 == 0 else stage
        return i, j ^ (1 << bit)

    return exchange(value, partner)


def exchange_chips(value, stage, cores):
    bits = bits_of(lax.axis_size("dp") // cores)

    def partner(i, j):
        bit = bits - 1 - stage if cores == 2 and i % 2 == 1 else stage
        return i ^ (cores << bit), j

    return exchange(value, partner)


def neighbour(value, steps):
    count = lax.axis_size("space")
    first, last = (max(0, -steps), min(count, count - steps))
    return lax.ppermute(value, "space", [(source, source + steps) for source in range(first, last)])


def exchange_stage(value, axis, stage, cores):
    return exchange_space(value, stage, cores) if axis == "space" else exchange_chips(value, stage, cores)


def add_cores(keep, sends, then, cores, order=()):
    got = tuple(exchange(send, lambda i, j: (i ^ 1, j)) if cores == 2 else 0 * send for send in sends)
    return add_stage(keep, got, None, then, cores, order)


def body(volume, kernel, cotangent):
    samples, planes, height, width, ci = volume.shape
    co = kernel.shape[-1]
    assert samples == 1
    dp, space = lax.axis_size("dp"), lax.axis_size("space")
    cores = 2 if dp % 2 == 0 else 1
    chips = dp // cores
    outs = planes // 2
    cells = height * width // 4
    scale = 1.0 / math.sqrt(dp * space * samples * outs * cells)
    over_space = [("space", stage) for stage in range(bits_of(space))]
    over_chips = [("chips", stage) for stage in range(bits_of(chips))]

    share = neighbour(halo_share(volume, kernel), 1)
    preact, even, odd = partial_preact(volume, kernel)
    cotangent = cotangent.reshape(outs * cells, co)
    rest, flipped_rest = activation(preact, cotangent, None, cells, (outs - 1) * cells, space, cores)
    products = early_ahead(even, odd, rest)
    first, flipped = activation(preact, cotangent, share, 0, cells, space, cores)
    flipped = jnp.concatenate([flipped, flipped_rest], axis=1)
    above = neighbour(first, -1)

    early = kernel_grad_part(even, odd, first, products, True, cores, chips, scale, space)
    early_units, late_units = 18 * (co // 128), 9 * (co // 128)
    plan = over_space + over_chips
    value, sent = add_cores(early[0], early[1:], plan[0], cores)
    late_plan, late_now, late_half = list(over_chips), None, None
    switch_at = [len(over_space) - 1 + 2 * stage for stage in range(len(over_space))]
    stay, moved = flipped[None], None
    for place, now in enumerate(plan):
        got = exchange_stage(sent, *now, cores)
        tokens = [sent]
        if place == 0:
            late = kernel_grad_part(even, odd, rest, above, False, cores, chips, scale, 1, (sent,))
            tokens.append(late[1])
        elif late_half is None:
            then = late_plan.pop(0) if late_plan else None
            if late_now is None:
                result = add_cores(late[0], late[1:], then, cores, (sent,))
            else:
                result = add_stage(late_value, late_got, late_now, then, cores, (sent,))
            late_now = then
            if then is None:
                late_half = result
            else:
                late_value, late_sent = result
                late_got = (exchange_stage(late_sent, *then, cores),)
                tokens.append(late_sent)
        if switch_at and place == switch_at[0]:
            stage = len(over_space) - len(switch_at)
            switch_at.pop(0)
            stay, out = switch_stage(stay, moved, 0, None, stage, cores, (tokens[-1],))
            moved = exchange_space(out, stage, cores)
            tokens.append(out)
        if place + 1 < len(plan):
            weight = SPACER if place >= len(over_space) else 1000
            value, sent = add_stage(
                value, (got,), now, plan[place + 1], cores, tuple(tokens[1:]), weight
            )
    for stage in range(len(over_space) - len(switch_at), len(over_space)):
        stay, out = switch_stage(stay, moved, 0, None, stage, cores, (sent,))
        moved = exchange_space(out, stage, cores)
    if late_half is None:
        late_half = add_stage(late_value, late_got, late_now, None, cores)

    mine = join(value, got, late_half, plan[-1], cores, tuple(tokens[1:]))
    early_rows = mine.shape[0] - late_half.shape[0]
    switched = None
    for step, (_, stage) in enumerate(reversed(over_space)):
        got = exchange_space(mine, stage, cores)
        order = ()
        if switched is None:
            switched, done = switched_of(stay, moved, 0, space, cores, (mine,))
            order = (done,)
        if step + 1 < len(over_space):
            mine = gather_stage(mine, got, early_rows << step, order)
    volume_grad, done = volume_grad_of(first, rest, above, kernel, height, width, (mine,))
    kernel_grad = kernel_grad_out(mine, got, early_units, late_units, space, cores, co, (done,))

    return (
        switched[None],
        volume_grad.reshape(volume.shape),
        kernel_grad.reshape(3, 3, 3, ci // dp, co),
    )


def solution(mesh):
    in_specs = (P("dp", "space", None, None, None), P(), P("dp", "space", None, None, None))
    out_specs = (
        P("dp", "space", None),
        P("dp", "space", None, None, None),
        P(None, None, None, "dp", None),
    )
    return jax.shard_map(body, mesh=mesh, in_specs=in_specs, out_specs=out_specs, check_vma=False)
```
